32 devices in a mesh: blk: 4 (over y, x), tile: 8 (over z, core).
Axes of the slice: x: 2, y: 2, z: 4, core: 2. Of those that a mesh axis runs over, the one named last changes fastest.
Arguments:
- grid_feat: bfloat16 [8192, 512], P(('blk', 'tile')), may hold values from -18 to 18
- queries: bfloat16 [8192, 512], P(('blk', 'tile')), may hold values from -90 to 90
- obs_keys: bfloat16 [256, 512], P(('blk', 'tile')), may hold values from -4 to 4
- obs_values: bfloat16 [256, 512], P(('blk', 'tile')), may hold values from -6 to 6
- block_mask: int32 [64, 2], P(('blk', 'tile')), may hold values from 0 to 1, as said below
- obs_valid: int32 [2], replicated, may hold values from 2 to 128, as said below
- out_weight: bfloat16 [512, 512], replicated, may hold values from -0.25 to 0.25
- conv_weight: bfloat16 [3, 3, 512, 512], replicated, may hold values from -0.09375 to 0.09375
Outputs:
- layer_out: bfloat16 [8192, 512], P(('blk', 'tile'))
The draws below stay inside these ranges and needn't reach their ends.
Inputs may be any that keep to these rules, and one draw needn't show every extreme that they name: `block_mask`: row t has a 1 in column t mod 2. `obs_valid`: at least one entry equals 128.
All inputs are finite; a program needn't handle non-finite values.
Results may differ from the reference program's by a relative error of at most 0.007.
Values may be sent and summed in bfloat16 or wider, within the bound.
No kernel may reach another device: no remote copies, remote signals or barrier semaphores. Data moves between devices by JAX's collectives and lax.ppermute only.
A program may use at most 64 MiB of HBM per device.

```python
import jax
import jax.numpy as jnp
from jax import lax

D = 512
HEADS = 8
HEAD = 64
LON = 128
OBS_BLOCK = 128
TILES_DEV = 2
NTILES = 64
NQ = 8192
OBS = 256
NOBLK = 2


def draw_obs_keys(key, part):
    own = jax.random.fold_in(key, 31)
    keys = jnp.clip(jax.random.normal(own, (OBS, D), jnp.float32), -4.0, 4.0)
    return keys.astype(jnp.bfloat16)


def draw_queries(key, part):
    own = jax.random.fold_in(key, 32)
    values = jnp.clip(jax.random.normal(own, (NQ, D), jnp.float32), -4.0, 4.0)
    return values.astype(jnp.bfloat16)


def draw_grid_feat(key, part):
    own = jax.random.fold_in(key, 33)
    values = jnp.clip(jax.random.normal(own, (NQ, D), jnp.float32), -5.0, 5.0)
    return values.astype(jnp.bfloat16)


def draw_block_mask(key, part):
    devices = NTILES // TILES_DEV
    level = jax.random.randint(jax.random.fold_in(key, 11), (devices,), 1, 9)
    tile_level = jnp.repeat(level, TILES_DEV)
    picks = jax.random.randint(jax.random.fold_in(key, 12), (NTILES, NOBLK), 0, 8)
    forced = jnp.arange(NTILES)[:, None] % NOBLK == jnp.arange(NOBLK)[None, :]
    return ((picks < tile_level[:, None]) | forced).astype(jnp.int32)


def draw_obs_valid(key, part):
    counts = jax.random.randint(jax.random.fold_in(key, 21), (NOBLK,), 2, OBS_BLOCK + 1)
    full = jax.random.randint(jax.random.fold_in(key, 22), (), 0, NOBLK)
    return jnp.where(jnp.arange(NOBLK) == full, OBS_BLOCK, counts).astype(jnp.int32)


def block_scale(stream_key, extent, shards, smallest, top_value):
    loudness, own = 1.0, jax.random.fold_in(stream_key, 6)
    for position, blocks in shards:
        draws = jnp.exp(jax.random.uniform(jax.random.fold_in(own, position), (blocks,), jnp.float32, smallest / len(shards), top_value / len(shards)))
        loudness = loudness * jnp.repeat(draws, extent[position] // blocks).reshape([-1 if axis == position else 1 for axis in range(len(extent))])
    return loudness


def scatter_about(own_key, dims, scale, reach, split=(), kind=jnp.bfloat16):
    entries = scale * jax.random.normal(own_key, dims, jnp.float32)
    if split:
        entries = entries * block_scale(own_key, dims, split, -0.22, 0.18)
    return jnp.clip(entries, -reach, reach).astype(kind)


def setup_inputs(seed: int = 0) -> dict:
    streams_of = jax.random.split(jax.random.key(seed), 9)
    grid_feat = draw_grid_feat(jax.random.fold_in(streams_of[8], 71), 0)
    queries = draw_queries(jax.random.fold_in(streams_of[8], 71), 0)
    obs_keys = draw_obs_keys(jax.random.fold_in(streams_of[8], 71), 0)
    obs_values = scatter_about(streams_of[3], (OBS, D), 1.0, 6.0, ((0, 32),))
    block_mask = draw_block_mask(jax.random.fold_in(streams_of[8], 71), 0)
    obs_valid = draw_obs_valid(jax.random.fold_in(streams_of[8], 71), 0)
    out_weight = scatter_about(streams_of[6], (D, D), D ** -0.5, 0.25)
    conv_weight = scatter_about(streams_of[7], (3, 3, D, D), (9 * D) ** -0.5, 0.09375)
    return dict(grid_feat=grid_feat, queries=queries, obs_keys=obs_keys, obs_values=obs_values, block_mask=block_mask, obs_valid=obs_valid, out_weight=out_weight, conv_weight=conv_weight)


def reference(grid_feat, queries, obs_keys, obs_values, block_mask, obs_valid, out_weight, conv_weight):
    rows = jnp.arange(OBS, dtype=jnp.int32)
    key_block = rows // OBS_BLOCK
    onehot = (key_block[:, None] == jnp.arange(NOBLK, dtype=jnp.int32)[None, :]).astype(jnp.float32)
    limits = lax.optimization_barrier(jnp.sum(jnp.where(onehot > 0.5, obs_valid[None, :], 0), axis=1))
    key_ok = rows % OBS_BLOCK < limits
    keys = obs_keys.astype(jnp.float32).reshape(OBS, HEADS, HEAD)
    values = obs_values.astype(jnp.float32).reshape(OBS, HEADS, HEAD)
    scale = HEAD ** (-0.5)
    blocks = NTILES // TILES_DEV
    query_blocks = queries.reshape(blocks, TILES_DEV, LON, HEADS, HEAD)
    mask_blocks = block_mask.reshape(blocks, TILES_DEV, NOBLK)

    def one_block(pair):
        query_rows, mask_rows = pair
        wanted = jnp.dot(mask_rows.astype(jnp.float32), onehot.T, precision=lax.Precision.HIGHEST) > 0.5
        allowed = wanted & key_ok[None, :]
        scores = jnp.einsum('tqhd,khd->htqk', query_rows.astype(jnp.float32), keys) * scale
        scores = jnp.where(allowed[None, :, None, :], scores, -jnp.inf)
        top = lax.optimization_barrier(jnp.max(scores, axis=-1, keepdims=True))
        weights = jnp.exp(scores - top)
        total = lax.optimization_barrier(jnp.sum(weights, axis=-1))
        rounded = lax.optimization_barrier(weights.astype(jnp.bfloat16)).astype(jnp.float32)
        mixed = jnp.einsum('htqk,khd->htqd', rounded, values) / total[..., None]
        return jnp.transpose(mixed, (1, 2, 0, 3)).reshape(TILES_DEV * LON, D).astype(jnp.bfloat16)
    mixed = lax.map(one_block, (query_blocks, mask_blocks)).reshape(NQ, D)
    projected = jnp.dot(mixed, out_weight, preferred_element_type=jnp.float32)
    hidden = lax.optimization_barrier((grid_feat.astype(jnp.float32) + projected).astype(jnp.bfloat16))
    wide = hidden.astype(jnp.float32)
    normed = (wide * lax.rsqrt(lax.optimization_barrier(jnp.mean(wide * wide, axis=-1, keepdims=True)) + 1e-06)).astype(jnp.bfloat16)
    field = normed.reshape(NTILES, LON, D)
    padded = jnp.pad(field, ((1, 1), (0, 0), (0, 0)))
    summed = jnp.zeros((NQ, D), jnp.float32)
    for lat_off in range(3):
        for lon_off in range(3):
            moved = jnp.roll(padded[lat_off:lat_off + NTILES], 1 - lon_off, axis=1)
            summed = summed + jnp.dot(moved.reshape(NQ, D), conv_weight[lat_off, lon_off], preferred_element_type=jnp.float32)
    return (wide + summed).astype(jnp.bfloat16)
```

```python
import functools
import math

import jax
import jax.numpy as jnp
from jax import lax
from jax.experimental import pallas as pl
from jax.experimental.pallas import tpu as pltpu
from jax.sharding import PartitionSpec as P

HEADS = 8
OBS_BLOCK = 128
AXES = ("blk", "tile")
PAIR = 2
MASK_ROWS = 16
NT = (((1,), (1,)), ((), ()))


def layer_kernel(
    tiles, lon, width, nblocks,
    edge_ref, mask_ref, valid_ref, low_ref, high_ref, queries_ref, grid_ref, kv_ref, out_weight_ref,
    conv_hbm, out_ref, conv_ref, mixed_ref, field_ref, conv_sem,
):
    head = width // HEADS
    pair = PAIR * head
    obs = nblocks * OBS_BLOCK
    scale = head ** (-0.5) * math.log2(math.e)
    copies = [
        pltpu.make_async_copy(conv_hbm.at[lat_off], conv_ref.at[lat_off], conv_sem.at[lat_off])
        for lat_off in range(3)
    ]
    for copy in copies:
        copy.start()

    key_lane = lax.broadcasted_iota(jnp.int32, (1, OBS_BLOCK), 1)

    def limited(allowed, block):
        live = key_lane < valid_ref[block]
        return jnp.where(jnp.logical_and(allowed, live), 0.0, -jnp.inf)

    def own_bias(tile):
        parts = [limited(mask_ref[tile, block] > 0, block) for block in range(nblocks)]
        return jnp.concatenate(parts, axis=1)

    def halo_bias(ref):
        row = ref[2 * lon : 2 * lon + MASK_ROWS, :].astype(jnp.float32)[:1]
        parts = [
            limited(jnp.broadcast_to(row[:, block : block + 1], (1, OBS_BLOCK)) > 0.5, block)
            for block in range(nblocks)
        ]
        return jnp.concatenate(parts, axis=1)

    biases = [halo_bias(low_ref)] + [own_bias(t) for t in range(tiles)] + [halo_bias(high_ref)]

    lane = lax.broadcasted_iota(jnp.int32, (obs, pair), 1)
    ones = [(lane // head == h).astype(jnp.bfloat16) for h in range(PAIR)]
    for group in range(HEADS // PAIR):
        cols = slice(group * pair, (group + 1) * pair)
        keys = kv_ref[:, :, group * pair : (group + 1) * pair].reshape(obs, pair)
        values = kv_ref[:, :, width + group * pair : width + (group + 1) * pair].reshape(obs, pair)
        key_parts = [keys * one for one in ones]
        value_parts = jnp.concatenate(
            [jnp.concatenate([values * one, one], axis=1) for one in ones], axis=0
        )
        rows = [low_ref[:lon, cols]]
        rows += [queries_ref[t * lon : (t + 1) * lon, cols] for t in range(tiles)]
        rows += [high_ref[:lon, cols]]
        query = jnp.concatenate(rows, axis=0)
        weights = []
        for part in key_parts:
            scores = lax.dot_general(query, part, NT, preferred_element_type=jnp.float32)
            pieces = []
            for t, bias in enumerate(biases):
                piece = scores[t * lon : (t + 1) * lon] * scale + bias
                top = jnp.max(piece, axis=1, keepdims=True)
                pieces.append(jnp.exp2(piece - top).astype(jnp.bfloat16))
            weights.append(jnp.concatenate(pieces, axis=0))
        both = jnp.dot(
            jnp.concatenate(weights, axis=1), value_parts, preferred_element_type=jnp.float32
        )
        mixed_ref[:, cols] = (both[:, :pair] / both[:, pair:]).astype(jnp.bfloat16)

    projected = jnp.dot(mixed_ref[...], out_weight_ref[...], preferred_element_type=jnp.float32)
    grid = jnp.concatenate(
        [low_ref[lon : 2 * lon, :], grid_ref[...], high_ref[lon : 2 * lon, :]], axis=0
    )
    hidden = (grid.astype(jnp.float32) + projected).astype(jnp.bfloat16)
    wide = hidden.astype(jnp.float32)
    normed = wide * lax.rsqrt(jnp.mean(wide * wide, axis=-1, keepdims=True) + 1e-06)
    last = (tiles + 1) * lon
    field_ref[lon:last] = normed[lon:last].astype(jnp.bfloat16)
    field_ref[:lon] = jnp.where(edge_ref[0] > 0, normed[:lon], 0.0).astype(jnp.bfloat16)
    field_ref[last:] = jnp.where(edge_ref[1] > 0, normed[last:], 0.0).astype(jnp.bfloat16)

    sums = [None, None, None]
    for lat_off in range(3):
        copies[lat_off].wait()
        moved = field_ref[lat_off * lon : (lat_off + tiles) * lon, :]
        for lon_off in range(3):
            term = jnp.dot(moved, conv_ref[lat_off, lon_off], preferred_element_type=jnp.float32)
            sums[lon_off] = term if sums[lon_off] is None else sums[lon_off] + term
    for t in range(tiles):
        here = slice(t * lon, (t + 1) * lon)
        out_ref[here, :] = (
            wide[(t + 1) * lon : (t + 2) * lon]
            + pltpu.roll(sums[0][here], 1, 0)
            + sums[1][here]
            + pltpu.roll(sums[2][here], lon - 1, 0)
        ).astype(jnp.bfloat16)


def on_device(
    grid_feat, queries, obs_keys, obs_values, block_mask, obs_valid, out_weight, conv_weight
):
    q_dev, width = queries.shape
    tiles, nblocks = block_mask.shape
    lon = q_dev // tiles
    devices = lax.axis_size(AXES)
    me = lax.axis_index(AXES)
    edge = jnp.stack([me > 0, me < devices - 1]).astype(jnp.int32)

    mask_tile = jnp.pad(block_mask.astype(jnp.bfloat16), ((0, 0), (0, width - nblocks)))

    def packed(tile):
        rows = slice(tile * lon, (tile + 1) * lon)
        mask = jnp.broadcast_to(mask_tile[tile : tile + 1], (MASK_ROWS, width))
        return jnp.concatenate([queries[rows], grid_feat[rows], mask], axis=0)

    forward = [(i, i + 1) for i in range(devices - 1)]
    backward = [(i + 1, i) for i in range(devices - 1)]
    low = lax.ppermute(packed(tiles - 1), AXES, forward)
    high = lax.ppermute(packed(0), AXES, backward)

    kv_local = jnp.concatenate([obs_keys, obs_values], axis=1)
    kv = lax.all_to_all(
        jnp.broadcast_to(kv_local[None], (devices,) + kv_local.shape), AXES, 0, 0
    )

    vmem = pl.BlockSpec(memory_space=pltpu.VMEM)
    smem = pl.BlockSpec(memory_space=pltpu.SMEM)
    flops = 2 * q_dev * width * (9 * width + 2 * width + 4 * nblocks * OBS_BLOCK)
    return pl.pallas_call(
        functools.partial(layer_kernel, tiles, lon, width, nblocks),
        out_shape=jax.ShapeDtypeStruct((q_dev, width), jnp.bfloat16),
        in_specs=[smem] * 3 + [vmem] * 6 + [pl.BlockSpec(memory_space=pl.ANY)],
        out_specs=vmem,
        scratch_shapes=[
            pltpu.VMEM(conv_weight.shape, jnp.bfloat16),
            pltpu.VMEM(((tiles + 2) * lon, width), jnp.bfloat16),
            pltpu.VMEM(((tiles + 2) * lon, width), jnp.bfloat16),
            pltpu.SemaphoreType.DMA((3,)),
        ],
        compiler_params=pltpu.CompilerParams(vmem_limit_bytes=48 * 2**20),
        cost_estimate=pl.CostEstimate(
            flops=flops, bytes_accessed=2 * conv_weight.size, transcendentals=0
        ),
        name="layer",
    )(edge, block_mask, obs_valid, low, high, queries, grid_feat, kv, out_weight, conv_weight)


def solution(mesh):
    in_specs = (
        P(AXES, None),
        P(AXES, None),
        P(AXES, None),
        P(AXES, None),
        P(AXES, None),
        P(),
        P(),
        P(),
    )
    return jax.shard_map(
        on_device, mesh=mesh, in_specs=in_specs, out_specs=P(AXES, None), check_vma=False
    )
```

```python
import functools
import math

import jax
import jax.numpy as jnp
from jax import lax
from jax.experimental import pallas as pl
from jax.experimental.pallas import tpu as pltpu
from jax.sharding import PartitionSpec as P

HEADS = 8
OBS_BLOCK = 128
AXES = ("blk", "tile")
PAIR = 2
MASK_ROWS = 16
NT = (((1,), (1,)), ((), ()))


def layer_kernel(
    tiles, lon, width, nblocks,
    meta_ref, low_ref, high_ref, kv_hbm, queries_hbm, grid_hbm, out_weight_hbm, conv_hbm,
    out_ref, kv_ref, queries_ref, grid_ref, out_weight_ref, conv_ref, mixed_ref, field_ref, sems,
):
    head = width // HEADS
    pair = PAIR * head
    obs = nblocks * OBS_BLOCK
    scale = head ** (-0.5) * math.log2(math.e)
    moves = [(kv_hbm, kv_ref), (queries_hbm, queries_ref)]
    moves += [(out_weight_hbm, out_weight_ref), (grid_hbm, grid_ref)]
    moves += [(conv_hbm.at[lat_off], conv_ref.at[lat_off]) for lat_off in range(3)]
    copies = [
        pltpu.make_async_copy(source, target, sems.at[i]) for i, (source, target) in enumerate(moves)
    ]
    for copy in copies:
        copy.start()

    key_lane = lax.broadcasted_iota(jnp.int32, (1, OBS_BLOCK), 1)

    def limited(allowed, block):
        live = key_lane < meta_ref[2 + block]
        return jnp.where(jnp.logical_and(allowed, live), 0.0, -jnp.inf)

    def own_bias(tile):
        parts = [limited(meta_ref[2 + (1 + tile) * nblocks + block] > 0, block) for block in range(nblocks)]
        return jnp.concatenate(parts, axis=1)

    def halo_bias(ref):
        row = ref[2 * lon : 2 * lon + MASK_ROWS, :].astype(jnp.float32)[:1]
        parts = [
            limited(jnp.broadcast_to(row[:, block : block + 1], (1, OBS_BLOCK)) > 0.5, block)
            for block in range(nblocks)
        ]
        return jnp.concatenate(parts, axis=1)

    biases = [halo_bias(low_ref)] + [own_bias(t) for t in range(tiles)] + [halo_bias(high_ref)]

    copies[0].wait()
    copies[1].wait()
    lane = lax.broadcasted_iota(jnp.int32, (obs, pair), 1)
    ones = [(lane // head == h).astype(jnp.bfloat16) for h in range(PAIR)]
    for group in range(HEADS // PAIR):
        cols = slice(group * pair, (group + 1) * pair)
        keys = kv_ref[:, :, group * pair : (group + 1) * pair].reshape(obs, pair)
        values = kv_ref[:, :, width + group * pair : width + (group + 1) * pair].reshape(obs, pair)
        key_parts = [keys * one for one in ones]
        value_parts = jnp.concatenate(
            [jnp.concatenate([values * one, one], axis=1) for one in ones], axis=0
        )
        rows = [low_ref[:lon, cols]]
        rows += [queries_ref[t * lon : (t + 1) * lon, cols] for t in range(tiles)]
        rows += [high_ref[:lon, cols]]
        query = jnp.concatenate(rows, axis=0)
        weights = []
        for part in key_parts:
            scores = lax.dot_general(query, part, NT, preferred_element_type=jnp.float32)
            pieces = []
            for t, bias in enumerate(biases):
                piece = scores[t * lon : (t + 1) * lon] * scale + bias
                top = jnp.max(piece, axis=1, keepdims=True)
                pieces.append(jnp.exp2(piece - top).astype(jnp.bfloat16))
            weights.append(jnp.concatenate(pieces, axis=0))
        both = jnp.dot(
            jnp.concatenate(weights, axis=1), value_parts, preferred_element_type=jnp.float32
        )
        mixed_ref[:, cols] = (both[:, :pair] / both[:, pair:]).astype(jnp.bfloat16)

    copies[2].wait()
    copies[3].wait()
    projected = jnp.dot(mixed_ref[...], out_weight_ref[...], preferred_element_type=jnp.float32)
    grid = jnp.concatenate(
        [low_ref[lon : 2 * lon, :], grid_ref[...], high_ref[lon : 2 * lon, :]], axis=0
    )
    hidden = (grid.astype(jnp.float32) + projected).astype(jnp.bfloat16)
    wide = hidden.astype(jnp.float32)
    normed = wide * lax.rsqrt(jnp.mean(wide * wide, axis=-1, keepdims=True) + 1e-06)
    last = (tiles + 1) * lon
    field_ref[lon:last] = normed[lon:last].astype(jnp.bfloat16)
    field_ref[:lon] = jnp.where(meta_ref[0] > 0, normed[:lon], 0.0).astype(jnp.bfloat16)
    field_ref[last:] = jnp.where(meta_ref[1] > 0, normed[last:], 0.0).astype(jnp.bfloat16)

    sums = [None, None, None]
    for lat_off in range(3):
        copies[4 + lat_off].wait()
        moved = field_ref[lat_off * lon : (lat_off + tiles) * lon, :]
        for lon_off in range(3):
            term = jnp.dot(moved, conv_ref[lat_off, lon_off], preferred_element_type=jnp.float32)
            sums[lon_off] = term if sums[lon_off] is None else sums[lon_off] + term
    for t in range(tiles):
        here = slice(t * lon, (t + 1) * lon)
        out_ref[here, :] = (
            wide[(t + 1) * lon : (t + 2) * lon]
            + pltpu.roll(sums[0][here], 1, 0)
            + sums[1][here]
            + pltpu.roll(sums[2][here], lon - 1, 0)
        ).astype(jnp.bfloat16)


def on_device(
    grid_feat, queries, obs_keys, obs_values, block_mask, obs_valid, out_weight, conv_weight
):
    q_dev, width = queries.shape
    tiles, nblocks = block_mask.shape
    lon = q_dev // tiles
    devices = lax.axis_size(AXES)
    me = lax.axis_index(AXES)
    edge = jnp.stack([me > 0, me < devices - 1]).astype(jnp.int32)
    meta = jnp.concatenate([edge, obs_valid, block_mask.reshape(-1)])

    mask_tile = jnp.pad(block_mask.astype(jnp.bfloat16), ((0, 0), (0, width - nblocks)))

    def packed(tile):
        rows = slice(tile * lon, (tile + 1) * lon)
        mask = jnp.broadcast_to(mask_tile[tile : tile + 1], (MASK_ROWS, width))
        return jnp.concatenate([queries[rows], grid_feat[rows], mask], axis=0)

    forward = [(i, i + 1) for i in range(devices - 1)]
    backward = [(i + 1, i) for i in range(devices - 1)]
    low = lax.ppermute(packed(tiles - 1), AXES, forward)
    high = lax.ppermute(packed(0), AXES, backward)

    kv_local = jnp.concatenate([obs_keys, obs_values], axis=1)
    kv = lax.all_gather(kv_local, AXES, axis=0)

    vmem = pl.BlockSpec(memory_space=pltpu.VMEM)
    smem = pl.BlockSpec(memory_space=pltpu.SMEM)
    flops = 2 * q_dev * width * (9 * width + 2 * width + 4 * nblocks * OBS_BLOCK)
    return pl.pallas_call(
        functools.partial(layer_kernel, tiles, lon, width, nblocks),
        out_shape=jax.ShapeDtypeStruct((q_dev, width), jnp.bfloat16),
        in_specs=[smem] + [vmem] * 2 + [pl.BlockSpec(memory_space=pl.ANY)] * 5,
        out_specs=vmem,
        scratch_shapes=[
            pltpu.VMEM(kv.shape, jnp.bfloat16),
            pltpu.VMEM(queries.shape, jnp.bfloat16),
            pltpu.VMEM(grid_feat.shape, jnp.bfloat16),
            pltpu.VMEM(out_weight.shape, jnp.bfloat16),
            pltpu.VMEM(conv_weight.shape, jnp.bfloat16),
            pltpu.VMEM(((tiles + 2) * lon, width), jnp.bfloat16),
            pltpu.VMEM(((tiles + 2) * lon, width), jnp.bfloat16),
            pltpu.SemaphoreType.DMA((7,)),
        ],
        compiler_params=pltpu.CompilerParams(vmem_limit_bytes=48 * 2**20),
        cost_estimate=pl.CostEstimate(
            flops=flops, bytes_accessed=2 * conv_weight.size, transcendentals=0
        ),
        name="layer",
    )(meta, low, high, kv, queries, grid_feat, out_weight, conv_weight)


def solution(mesh):
    in_specs = (
        P(AXES, None),
        P(AXES, None),
        P(AXES, None),
        P(AXES, None),
        P(AXES, None),
        P(),
        P(),
        P(),
    )
    return jax.shard_map(
        on_device, mesh=mesh, in_specs=in_specs, out_specs=P(AXES, None), check_vma=False
    )
```

```python
import functools
import math

import jax
import jax.numpy as jnp
from jax import lax
from jax.experimental import pallas as pl
from jax.experimental.pallas import tpu as pltpu
from jax.sharding import PartitionSpec as P

HEADS = 8
OBS_BLOCK = 128
AXES = ("blk", "tile")
PAIR = 2
PARITIES = 2
MASK_ROWS = 16
NT = (((1,), (1,)), ((), ()))


def layer_kernel(
    tiles, lon, width, nblocks, rows,
    meta_ref, low_ref, high_ref, same_ref, other_ref, queries_hbm, grid_hbm, out_weight_hbm, conv_hbm,
    out_ref, queries_ref, grid_ref, out_weight_ref, conv_ref, mixed_ref, field_ref, sems,
):
    head = width // HEADS
    pair = PAIR * head
    obs = nblocks * OBS_BLOCK
    scale = head ** (-0.5) * math.log2(math.e)
    moves = [(queries_hbm, queries_ref), (out_weight_hbm, out_weight_ref), (grid_hbm, grid_ref)]
    moves += [(conv_hbm.at[lat_off], conv_ref.at[lat_off]) for lat_off in range(3)]
    copies = [
        pltpu.make_async_copy(source, target, sems.at[i]) for i, (source, target) in enumerate(moves)
    ]
    for copy in copies:
        copy.start()

    half = OBS_BLOCK // PARITIES
    key_lane = lax.broadcasted_iota(jnp.int32, (1, OBS_BLOCK), 1)
    spread = (key_lane % half) // rows * (PARITIES * rows) + key_lane % rows
    first = key_lane < half

    def row_bias(limit_of):
        parts = []
        for parity in (meta_ref[2], 1 - meta_ref[2]):
            place = spread + parity * rows
            for block in range(0, nblocks, PARITIES):
                limit = jnp.where(first, limit_of(block), limit_of(block + 1))
                parts.append(jnp.where(place < limit, 0.0, -jnp.inf))
        return jnp.concatenate(parts, axis=1)

    def own_limit(tile, block):
        allowed = meta_ref[3 + (1 + tile) * nblocks + block] > 0
        return jnp.where(allowed, meta_ref[3 + block], 0)

    def halo_limit(row, block):
        allowed = jnp.broadcast_to(row[:, block : block + 1], (1, OBS_BLOCK)) > 0.5
        return jnp.where(allowed, meta_ref[3 + block], 0)

    mask_rows = [
        ref[2 * lon : 2 * lon + MASK_ROWS, :].astype(jnp.float32)[:1] for ref in (low_ref, high_ref)
    ]
    biases = [row_bias(functools.partial(halo_limit, mask_rows[0]))]
    biases += [row_bias(functools.partial(own_limit, t)) for t in range(tiles)]
    biases += [row_bias(functools.partial(halo_limit, mask_rows[1]))]

    copies[0].wait()
    lane = lax.broadcasted_iota(jnp.int32, (obs, pair), 1)
    ones = [(lane // head == h).astype(jnp.bfloat16) for h in range(PAIR)]

    def both_parities(cols):
        parts = [ref[:, :, cols].reshape(obs // PARITIES, pair) for ref in (same_ref, other_ref)]
        return jnp.concatenate(parts, axis=0)

    for group in range(HEADS // PAIR):
        cols = slice(group * pair, (group + 1) * pair)
        keys = both_parities(cols)
        values = both_parities(slice(width + group * pair, width + (group + 1) * pair))
        key_parts = [keys * one for one in ones]
        value_parts = jnp.concatenate(
            [jnp.concatenate([values * one, one], axis=1) for one in ones], axis=0
        )
        query = jnp.concatenate(
            [low_ref[:lon, cols], queries_ref[:, cols], high_ref[:lon, cols]], axis=0
        )
        weights = []
        for part in key_parts:
            scores = lax.dot_general(query, part, NT, preferred_element_type=jnp.float32)
            pieces = []
            for t, bias in enumerate(biases):
                piece = scores[t * lon : (t + 1) * lon] * scale + bias
                top = jnp.max(piece, axis=1, keepdims=True)
                pieces.append(jnp.exp2(piece - top).astype(jnp.bfloat16))
            weights.append(jnp.concatenate(pieces, axis=0))
        both = jnp.dot(
            jnp.concatenate(weights, axis=1), value_parts, preferred_element_type=jnp.float32
        )
        mixed_ref[:, cols] = (both[:, :pair] / both[:, pair:]).astype(jnp.bfloat16)

    copies[1].wait()
    copies[2].wait()
    projected = jnp.dot(mixed_ref[...], out_weight_ref[...], preferred_element_type=jnp.float32)
    grid = jnp.concatenate(
        [low_ref[lon : 2 * lon, :], grid_ref[...], high_ref[lon : 2 * lon, :]], axis=0
    )
    hidden = (grid.astype(jnp.float32) + projected).astype(jnp.bfloat16)
    wide = hidden.astype(jnp.float32)
    normed = wide * lax.rsqrt(jnp.mean(wide * wide, axis=-1, keepdims=True) + 1e-06)
    last = (tiles + 1) * lon
    field_ref[lon:last] = normed[lon:last].astype(jnp.bfloat16)
    field_ref[:lon] = jnp.where(meta_ref[0] > 0, normed[:lon], 0.0).astype(jnp.bfloat16)
    field_ref[last:] = jnp.where(meta_ref[1] > 0, normed[last:], 0.0).astype(jnp.bfloat16)

    sums = [None, None, None]
    for lat_off in range(3):
        copies[3 + lat_off].wait()
        moved = field_ref[lat_off * lon : (lat_off + tiles) * lon, :]
        for lon_off in range(3):
            term = jnp.dot(moved, conv_ref[lat_off, lon_off], preferred_element_type=jnp.float32)
            sums[lon_off] = term if sums[lon_off] is None else sums[lon_off] + term
    for t in range(tiles):
        here = slice(t * lon, (t + 1) * lon)
        out_ref[here, :] = (
            wide[(t + 1) * lon : (t + 2) * lon]
            + pltpu.roll(sums[0][here], 1, 0)
            + sums[1][here]
            + pltpu.roll(sums[2][here], lon - 1, 0)
        ).astype(jnp.bfloat16)


def on_device(
    grid_feat, queries, obs_keys, obs_values, block_mask, obs_valid, out_weight, conv_weight
):
    q_dev, width = queries.shape
    tiles, nblocks = block_mask.shape
    lon = q_dev // tiles
    devices = lax.axis_size(AXES)
    me = lax.axis_index(AXES)
    edge = jnp.stack([me > 0, me < devices - 1]).astype(jnp.int32)
    meta = jnp.concatenate([edge, (me % PARITIES)[None], obs_valid, block_mask.reshape(-1)])

    mask_tile = jnp.pad(block_mask.astype(jnp.bfloat16), ((0, 0), (0, width - nblocks)))

    def packed(tile):
        rows = slice(tile * lon, (tile + 1) * lon)
        mask = jnp.broadcast_to(mask_tile[tile : tile + 1], (MASK_ROWS, width))
        return jnp.concatenate([queries[rows], grid_feat[rows], mask], axis=0)

    forward = [(i, i + 1) for i in range(devices - 1)]
    backward = [(i + 1, i) for i in range(devices - 1)]
    low = lax.ppermute(packed(tiles - 1), AXES, forward)
    high = lax.ppermute(packed(0), AXES, backward)

    kv_local = jnp.concatenate([obs_keys, obs_values], axis=1)
    groups = [list(range(parity, devices, PARITIES)) for parity in range(PARITIES)]
    blocks = jnp.broadcast_to(kv_local[None], (devices // PARITIES,) + kv_local.shape)
    same = lax.all_to_all(blocks, AXES, 0, 0, axis_index_groups=groups)
    other = lax.ppermute(same, AXES, [(i, i ^ 1) for i in range(devices)])

    vmem = pl.BlockSpec(memory_space=pltpu.VMEM)
    smem = pl.BlockSpec(memory_space=pltpu.SMEM)
    flops = 2 * q_dev * width * (9 * width + 2 * width + 4 * nblocks * OBS_BLOCK)
    return pl.pallas_call(
        functools.partial(layer_kernel, tiles, lon, width, nblocks, obs_keys.shape[0]),
        out_shape=jax.ShapeDtypeStruct((q_dev, width), jnp.bfloat16),
        in_specs=[smem] + [vmem] * 4 + [pl.BlockSpec(memory_space=pltpu.HBM)] * 4,
        out_specs=vmem,
        scratch_shapes=[
            pltpu.VMEM(queries.shape, jnp.bfloat16),
            pltpu.VMEM(grid_feat.shape, jnp.bfloat16),
            pltpu.VMEM(out_weight.shape, jnp.bfloat16),
            pltpu.VMEM(conv_weight.shape, jnp.bfloat16),
            pltpu.VMEM(((tiles + 2) * lon, width), jnp.bfloat16),
            pltpu.VMEM(((tiles + 2) * lon, width), jnp.bfloat16),
            pltpu.SemaphoreType.DMA((6,)),
        ],
        compiler_params=pltpu.CompilerParams(vmem_limit_bytes=48 * 2**20),
        cost_estimate=pl.CostEstimate(
            flops=flops, bytes_accessed=2 * conv_weight.size, transcendentals=0
        ),
        name="layer",
    )(meta, low, high, same, other, queries, grid_feat, out_weight, conv_weight)


def solution(mesh):
    in_specs = (
        P(AXES, None),
        P(AXES, None),
        P(AXES, None),
        P(AXES, None),
        P(AXES, None),
        P(),
        P(),
        P(),
    )
    return jax.shard_map(
        on_device, mesh=mesh, in_specs=in_specs, out_specs=P(AXES, None), check_vma=False
    )
```

```python
import functools
import math

import jax
import jax.numpy as jnp
from jax import lax
from jax.experimental import pallas as pl
from jax.experimental.pallas import tpu as pltpu
from jax.sharding import PartitionSpec as P

HEADS = 8
OBS_BLOCK = 128
AXES = ("blk", "tile")
PAIR = 2
CORES = 2
MASK_LANES = 128
NT = (((1,), (1,)), ((), ()))


def layer_kernel(
    tiles, lon, width, nblocks, rows,
    meta_ref, near_ref, far_ref, same_ref, other_ref, *refs,
):
    queries_refs, grid_refs = refs[:tiles], refs[tiles : 2 * tiles]
    out_weight_refs = refs[2 * tiles : 2 * tiles + 2]
    conv_hbm, out_ref, conv_ref, mixed_ref, field_ref, sems = refs[2 * tiles + 2 :]
    head = width // HEADS
    pair = PAIR * head
    obs = nblocks * OBS_BLOCK
    scale = head ** (-0.5) * math.log2(math.e)
    moves = [(conv_hbm.at[lat_off], conv_ref.at[lat_off]) for lat_off in range(3)]
    copies = [
        pltpu.make_async_copy(source, target, sems.at[i]) for i, (source, target) in enumerate(moves)
    ]
    for copy in copies:
        copy.start()

    core, near_pair, far_pair, far_exists = (meta_ref[i] for i in range(4))
    half = OBS_BLOCK // CORES
    key_lane = lax.broadcasted_iota(jnp.int32, (1, OBS_BLOCK), 1)
    spread = (key_lane % half) // rows * (CORES * rows) + key_lane % rows
    first = key_lane < half

    def row_bias(limit_of):
        parts = []
        for parity in (core, 1 - core):
            place = spread + parity * rows
            for block in range(0, nblocks, CORES):
                limit = jnp.where(first, limit_of(block), limit_of(block + 1))
                parts.append(jnp.where(place < limit, 0.0, -jnp.inf))
        return jnp.concatenate(parts, axis=1)

    def own_limit(tile, block):
        allowed = meta_ref[4 + (1 + tile) * nblocks + block] > 0
        return jnp.where(allowed, meta_ref[4 + block], 0)

    def halo_limit(row, block):
        allowed = jnp.broadcast_to(row[:, block : block + 1], (1, OBS_BLOCK)) > 0.5
        return jnp.where(allowed, meta_ref[4 + block], 0)

    def mask_row(index, take_first):
        block = other_ref[index][:, 2 * width :].astype(jnp.float32)
        return jnp.where(take_first, block[:1], block[tiles - 1 : tiles])

    biases = [row_bias(functools.partial(halo_limit, mask_row(near_pair, core == 0)))]
    biases += [row_bias(functools.partial(own_limit, t)) for t in range(tiles)]
    biases += [row_bias(functools.partial(halo_limit, mask_row(far_pair, core == 1)))]

    lane = lax.broadcasted_iota(jnp.int32, (obs, pair), 1)
    ones = [(lane // head == h).astype(jnp.bfloat16) for h in range(PAIR)]

    def both_cores(cols):
        parts = [ref[:, :, cols].reshape(obs // CORES, pair) for ref in (same_ref, other_ref)]
        return jnp.concatenate(parts, axis=0)

    for group in range(HEADS // PAIR):
        cols = slice(group * pair, (group + 1) * pair)
        keys = both_cores(cols)
        values = both_cores(slice(width + group * pair, width + (group + 1) * pair))
        key_parts = [keys * one for one in ones]
        value_parts = jnp.concatenate(
            [jnp.concatenate([values * one, one], axis=1) for one in ones], axis=0
        )
        query = jnp.concatenate(
            [near_ref[:lon, cols]] + [ref[:, cols] for ref in queries_refs] + [far_ref[:lon, cols]],
            axis=0,
        )
        weights = []
        for part in key_parts:
            scores = lax.dot_general(query, part, NT, preferred_element_type=jnp.float32)
            pieces = []
            for t, bias in enumerate(biases):
                piece = scores[t * lon : (t + 1) * lon] * scale + bias
                top = jnp.max(piece, axis=1, keepdims=True)
                pieces.append(jnp.exp2(piece - top).astype(jnp.bfloat16))
            weights.append(jnp.concatenate(pieces, axis=0))
        both = jnp.dot(
            jnp.concatenate(weights, axis=1), value_parts, preferred_element_type=jnp.float32
        )
        mixed_ref[:, cols] = (both[:, :pair] / both[:, pair:]).astype(jnp.bfloat16)

    out_weight = jnp.concatenate([ref[...] for ref in out_weight_refs], axis=0)
    projected = jnp.dot(mixed_ref[...], out_weight, preferred_element_type=jnp.float32)
    grid = jnp.concatenate(
        [near_ref[lon:, :]] + [ref[...] for ref in grid_refs] + [far_ref[lon:, :]], axis=0
    )
    hidden = (grid.astype(jnp.float32) + projected).astype(jnp.bfloat16)
    wide = hidden.astype(jnp.float32)
    normed = wide * lax.rsqrt(jnp.mean(wide * wide, axis=-1, keepdims=True) + 1e-06)
    last = (tiles + 1) * lon
    near_place = pl.multiple_of((1 - core) * last, lon)
    far_place = pl.multiple_of(core * last, lon)
    field_ref[lon:last] = normed[lon:last].astype(jnp.bfloat16)
    field_ref[pl.ds(near_place, lon)] = normed[:lon].astype(jnp.bfloat16)
    field_ref[pl.ds(far_place, lon)] = jnp.where(far_exists > 0, normed[last:], 0.0).astype(
        jnp.bfloat16
    )

    sums = [None, None, None]
    for lat_off in range(3):
        copies[lat_off].wait()
        moved = field_ref[lat_off * lon : (lat_off + tiles) * lon, :]
        for lon_off in range(3):
            term = jnp.dot(moved, conv_ref[lat_off, lon_off], preferred_element_type=jnp.float32)
            sums[lon_off] = term if sums[lon_off] is None else sums[lon_off] + term
    for t in range(tiles):
        here = slice(t * lon, (t + 1) * lon)
        out_ref[here, :] = (
            wide[(t + 1) * lon : (t + 2) * lon]
            + pltpu.roll(sums[0][here], 1, 0)
            + sums[1][here]
            + pltpu.roll(sums[2][here], lon - 1, 0)
        ).astype(jnp.bfloat16)


def on_device(
    grid_feat, queries, obs_keys, obs_values, block_mask, obs_valid, out_weight, conv_weight
):
    q_dev, width = queries.shape
    tiles, nblocks = block_mask.shape
    rows = obs_keys.shape[0]
    lon = q_dev // tiles
    blks, chain = lax.axis_size("blk"), lax.axis_size("tile")
    devices = blks * chain
    pairs = devices // CORES
    me = lax.axis_index(AXES)
    core = me % CORES

    mask_block = jnp.pad(
        block_mask.astype(jnp.bfloat16), ((0, rows - tiles), (0, MASK_LANES - nblocks))
    )
    block = jnp.concatenate([obs_keys, obs_values, mask_block], axis=1)
    members = chain // CORES
    groups = [
        [b * chain + i * CORES + c for i in range(members)] for b in range(blks) for c in range(CORES)
    ]
    column = lax.all_to_all(
        jnp.broadcast_to(block[None], (members,) + block.shape), AXES, 0, 0, axis_index_groups=groups
    )

    def pieces(array, count):
        return jnp.split(array, count, axis=0)

    query_rows, grid_rows, weight_rows = lax.optimization_barrier(
        (pieces(queries, tiles), pieces(grid_feat, tiles), pieces(out_weight, 2))
    )
    first = jnp.concatenate([query_rows[0], grid_rows[0]], axis=0)
    last = jnp.concatenate([query_rows[-1], grid_rows[-1]], axis=0)
    across = [(i, i + 1) for i in range(1, devices - 1, CORES)]
    across += [(target, source) for source, target in across]
    swap = [(i, i ^ 1) for i in range(devices)]
    far = lax.ppermute(jnp.where(core == 0, first, last), AXES, across)
    near = lax.ppermute(jnp.where(core == 0, last, first), AXES, swap)

    same = lax.all_to_all(
        jnp.broadcast_to(column[None], (blks,) + column.shape), "blk", 0, 0
    ).reshape((pairs,) + block.shape)
    other = lax.ppermute(same, AXES, swap)

    near_pair = me // CORES
    far_pair = near_pair + 2 * core - 1
    far_exists = (far_pair >= 0) & (far_pair < pairs)
    scalars = [core, near_pair, jnp.clip(far_pair, 0, pairs - 1), far_exists]
    meta = jnp.concatenate(
        [jnp.stack([s.astype(jnp.int32) for s in scalars]), obs_valid, block_mask.reshape(-1)]
    )

    vmem = pl.BlockSpec(memory_space=pltpu.VMEM)
    smem = pl.BlockSpec(memory_space=pltpu.SMEM)
    hbm = pl.BlockSpec(memory_space=pltpu.HBM)
    flops = 2 * q_dev * width * (9 * width + 2 * width + 4 * nblocks * OBS_BLOCK)
    return pl.pallas_call(
        functools.partial(layer_kernel, tiles, lon, width, nblocks, rows),
        out_shape=jax.ShapeDtypeStruct((q_dev, width), jnp.bfloat16),
        in_specs=[smem] + [vmem] * (6 + 2 * tiles) + [hbm],
        out_specs=vmem,
        scratch_shapes=[
            pltpu.VMEM(conv_weight.shape, jnp.bfloat16),
            pltpu.VMEM(((tiles + 2) * lon, width), jnp.bfloat16),
            pltpu.VMEM(((tiles + 2) * lon, width), jnp.bfloat16),
            pltpu.SemaphoreType.DMA((3,)),
        ],
        compiler_params=pltpu.CompilerParams(vmem_limit_bytes=48 * 2**20),
        cost_estimate=pl.CostEstimate(
            flops=flops, bytes_accessed=2 * conv_weight.size, transcendentals=0
        ),
        name="layer",
    )(meta, near, far, same, other, *query_rows, *grid_rows, *weight_rows, conv_weight)


def solution(mesh):
    in_specs = (
        P(AXES, None),
        P(AXES, None),
        P(AXES, None),
        P(AXES, None),
        P(AXES, None),
        P(),
        P(),
        P(),
    )
    return jax.shard_map(
        on_device, mesh=mesh, in_specs=in_specs, out_specs=P(AXES, None), check_vma=False
    )
```

```python
import functools
import math

import jax
import jax.numpy as jnp
from jax import lax
from jax.experimental import pallas as pl
from jax.experimental.pallas import tpu as pltpu
from jax.sharding import PartitionSpec as P

HEADS = 8
OBS_BLOCK = 128
AXES = ("blk", "tile")
PAIR = 2
CORES = 2
MASK_LANES = 128
NT = (((1,), (1,)), ((), ()))


def layer_kernel(
    tiles, lon, width, nblocks, rows,
    meta_ref, near_ref, far_ref, same_ref, other_ref, *refs,
):
    queries_refs, grid_refs = refs[:tiles], refs[tiles : 2 * tiles]
    out_weight_refs = refs[2 * tiles : 2 * tiles + 2]
    conv_hbm, out_ref, conv_ref, mixed_ref, field_ref, sems = refs[2 * tiles + 2 :]
    head = width // HEADS
    pair = PAIR * head
    obs = nblocks * OBS_BLOCK
    scale = head ** (-0.5) * math.log2(math.e)
    moves = [(conv_hbm.at[lat_off], conv_ref.at[lat_off]) for lat_off in range(3)]
    copies = [
        pltpu.make_async_copy(source, target, sems.at[i]) for i, (source, target) in enumerate(moves)
    ]
    for copy in copies:
        copy.start()

    core, near_pair, far_pair, far_exists = (meta_ref[i] for i in range(4))
    half = OBS_BLOCK // CORES
    key_lane = lax.broadcasted_iota(jnp.int32, (1, OBS_BLOCK), 1)
    spread = (key_lane % half) // rows * (CORES * rows) + key_lane % rows
    first = key_lane < half

    def row_bias(limit_of):
        parts = []
        for parity in (core, 1 - core):
            place = spread + parity * rows
            for block in range(0, nblocks, CORES):
                limit = jnp.where(first, limit_of(block), limit_of(block + 1))
                parts.append(jnp.where(place < limit, 0.0, -jnp.inf))
        return jnp.concatenate(parts, axis=1)

    def own_limit(tile, block):
        allowed = meta_ref[4 + (1 + tile) * nblocks + block] > 0
        return jnp.where(allowed, meta_ref[4 + block], 0)

    def halo_limit(row, block):
        allowed = jnp.broadcast_to(row[:, block : block + 1], (1, OBS_BLOCK)) > 0.5
        return jnp.where(allowed, meta_ref[4 + block], 0)

    def mask_row(index, take_first):
        block = other_ref[index][:, 2 * width :].astype(jnp.float32)
        return jnp.where(take_first, block[:1], block[tiles - 1 : tiles])

    biases = [row_bias(functools.partial(halo_limit, mask_row(near_pair, core == 0)))]
    biases += [row_bias(functools.partial(own_limit, t)) for t in range(tiles)]
    biases += [row_bias(functools.partial(halo_limit, mask_row(far_pair, core == 1)))]

    lane = lax.broadcasted_iota(jnp.int32, (obs, pair), 1)
    ones = [(lane // head == h).astype(jnp.bfloat16) for h in range(PAIR)]

    def both_cores(cols):
        parts = [ref[:, :, cols].reshape(obs // CORES, pair) for ref in (same_ref, other_ref)]
        return jnp.concatenate(parts, axis=0)

    for group in range(HEADS // PAIR):
        cols = slice(group * pair, (group + 1) * pair)
        keys = both_cores(cols)
        values = both_cores(slice(width + group * pair, width + (group + 1) * pair))
        key_parts = [keys * one for one in ones]
        value_parts = jnp.concatenate(
            [jnp.concatenate([values * one, one], axis=1) for one in ones], axis=0
        )
        query = jnp.concatenate(
            [near_ref[:lon, cols]] + [ref[:, cols] for ref in queries_refs] + [far_ref[:lon, cols]],
            axis=0,
        )
        weights = []
        for part in key_parts:
            scores = lax.dot_general(query, part, NT, preferred_element_type=jnp.float32)
            pieces = []
            for t, bias in enumerate(biases):
                piece = scores[t * lon : (t + 1) * lon] * scale + bias
                top = jnp.max(piece, axis=1, keepdims=True)
                pieces.append(jnp.exp2(piece - top).astype(jnp.bfloat16))
            weights.append(jnp.concatenate(pieces, axis=0))
        both = jnp.dot(
            jnp.concatenate(weights, axis=1), value_parts, preferred_element_type=jnp.float32
        )
        mixed_ref[:, cols] = (both[:, :pair] / both[:, pair:]).astype(jnp.bfloat16)

    depth = width // len(out_weight_refs)
    projected = sum(
        jnp.dot(
            mixed_ref[:, i * depth : (i + 1) * depth], ref[...], preferred_element_type=jnp.float32
        )
        for i, ref in enumerate(out_weight_refs)
    )
    grid = jnp.concatenate(
        [near_ref[lon:, :]] + [ref[...] for ref in grid_refs] + [far_ref[lon:, :]], axis=0
    )
    hidden = (grid.astype(jnp.float32) + projected).astype(jnp.bfloat16)
    wide = hidden.astype(jnp.float32)
    normed = wide * lax.rsqrt(jnp.mean(wide * wide, axis=-1, keepdims=True) + 1e-06)
    last = (tiles + 1) * lon
    near_place = pl.multiple_of((1 - core) * last, lon)
    far_place = pl.multiple_of(core * last, lon)
    field_ref[lon:last] = normed[lon:last].astype(jnp.bfloat16)
    field_ref[pl.ds(near_place, lon)] = normed[:lon].astype(jnp.bfloat16)
    field_ref[pl.ds(far_place, lon)] = jnp.where(far_exists > 0, normed[last:], 0.0).astype(
        jnp.bfloat16
    )

    sums = [None, None, None]
    for lat_off in range(3):
        copies[lat_off].wait()
        moved = field_ref[lat_off * lon : (lat_off + tiles) * lon, :]
        for lon_off in range(3):
            term = jnp.dot(moved, conv_ref[lat_off, lon_off], preferred_element_type=jnp.float32)
            sums[lon_off] = term if sums[lon_off] is None else sums[lon_off] + term
    for t in range(tiles):
        here = slice(t * lon, (t + 1) * lon)
        out_ref[here, :] = (
            wide[(t + 1) * lon : (t + 2) * lon]
            + pltpu.roll(sums[0][here], 1, 0)
            + sums[1][here]
            + pltpu.roll(sums[2][here], lon - 1, 0)
        ).astype(jnp.bfloat16)


def on_device(
    grid_feat, queries, obs_keys, obs_values, block_mask, obs_valid, out_weight, conv_weight
):
    q_dev, width = queries.shape
    tiles, nblocks = block_mask.shape
    rows = obs_keys.shape[0]
    lon = q_dev // tiles
    devices = lax.axis_size(AXES)
    pairs = devices // CORES
    me = lax.axis_index(AXES)
    core = me % CORES

    mask_block = jnp.pad(
        block_mask.astype(jnp.bfloat16), ((0, rows - tiles), (0, MASK_LANES - nblocks))
    )
    block = jnp.concatenate([obs_keys, obs_values, mask_block], axis=1)
    groups = [list(range(c, devices, CORES)) for c in range(CORES)]
    same = lax.all_to_all(
        jnp.broadcast_to(block[None], (pairs,) + block.shape), AXES, 0, 0, axis_index_groups=groups
    )

    def pieces(array, count):
        return jnp.split(array, count, axis=0)

    query_rows, grid_rows, weight_rows = lax.optimization_barrier(
        (pieces(queries, tiles), pieces(grid_feat, tiles), pieces(out_weight, 2))
    )
    first = jnp.concatenate([query_rows[0], grid_rows[0]], axis=0)
    last = jnp.concatenate([query_rows[-1], grid_rows[-1]], axis=0)
    across = [(i, i + 1) for i in range(1, devices - 1, CORES)]
    across += [(target, source) for source, target in across]
    swap = [(i, i ^ 1) for i in range(devices)]
    far = lax.ppermute(jnp.where(core == 0, first, last), AXES, across)
    near = lax.ppermute(jnp.where(core == 0, last, first), AXES, swap)

    other = lax.ppermute(same, AXES, swap)

    near_pair = me // CORES
    far_pair = near_pair + 2 * core - 1
    far_exists = (far_pair >= 0) & (far_pair < pairs)
    scalars = [core, near_pair, jnp.clip(far_pair, 0, pairs - 1), far_exists]
    meta = jnp.concatenate(
        [jnp.stack([s.astype(jnp.int32) for s in scalars]), obs_valid, block_mask.reshape(-1)]
    )

    vmem = pl.BlockSpec(memory_space=pltpu.VMEM)
    smem = pl.BlockSpec(memory_space=pltpu.SMEM)
    hbm = pl.BlockSpec(memory_space=pltpu.HBM)
    flops = 2 * q_dev * width * (9 * width + 2 * width + 4 * nblocks * OBS_BLOCK)
    return pl.pallas_call(
        functools.partial(layer_kernel, tiles, lon, width, nblocks, rows),
        out_shape=jax.ShapeDtypeStruct((q_dev, width), jnp.bfloat16),
        in_specs=[smem] + [vmem] * (6 + 2 * tiles) + [hbm],
        out_specs=vmem,
        scratch_shapes=[
            pltpu.VMEM(conv_weight.shape, jnp.bfloat16),
            pltpu.VMEM(((tiles + 2) * lon, width), jnp.bfloat16),
            pltpu.VMEM(((tiles + 2) * lon, width), jnp.bfloat16),
            pltpu.SemaphoreType.DMA((3,)),
        ],
        compiler_params=pltpu.CompilerParams(vmem_limit_bytes=48 * 2**20),
        cost_estimate=pl.CostEstimate(
            flops=flops, bytes_accessed=2 * conv_weight.size, transcendentals=0
        ),
        name="layer",
    )(meta, near, far, same, other, *query_rows, *grid_rows, *weight_rows, conv_weight)


def solution(mesh):
    in_specs = (
        P(AXES, None),
        P(AXES, None),
        P(AXES, None),
        P(AXES, None),
        P(AXES, None),
        P(),
        P(),
        P(),
    )
    return jax.shard_map(
        on_device, mesh=mesh, in_specs=in_specs, out_specs=P(AXES, None), check_vma=False
    )
```

```python
import functools
import math

import jax
import jax.numpy as jnp
from jax import lax
from jax.experimental import pallas as pl
from jax.experimental.pallas import tpu as pltpu
from jax.sharding import PartitionSpec as P

HEADS = 8
OBS_BLOCK = 128
AXES = ("blk", "tile")
PAIR = 2
CORES = 2
NT = (((1,), (1,)), ((), ()))


def attend_kernel(
    tiles, lon, width, nblocks, rows,
    meta_ref, same_ref, other_ref, *refs,
):
    queries_refs, grid_refs = refs[:tiles], refs[tiles : 2 * tiles]
    out_weight_refs = refs[2 * tiles : 2 * tiles + 2]
    hidden_ref, near_ref, far_ref, mixed_ref = refs[2 * tiles + 2 :]
    head = width // HEADS
    pair = PAIR * head
    obs = nblocks * OBS_BLOCK
    scale = head ** (-0.5) * math.log2(math.e)

    core = meta_ref[0]
    half = OBS_BLOCK // CORES
    key_lane = lax.broadcasted_iota(jnp.int32, (1, OBS_BLOCK), 1)
    spread = (key_lane % half) // rows * (CORES * rows) + key_lane % rows
    first = key_lane < half

    def limit(tile, block):
        allowed = meta_ref[1 + (1 + tile) * nblocks + block] > 0
        return jnp.where(allowed, meta_ref[1 + block], 0)

    def row_bias(tile):
        parts = []
        for parity in (core, 1 - core):
            place = spread + parity * rows
            for block in range(0, nblocks, CORES):
                end = jnp.where(first, limit(tile, block), limit(tile, block + 1))
                parts.append(jnp.where(place < end, 0.0, -jnp.inf))
        return jnp.concatenate(parts, axis=1)

    biases = [row_bias(t) for t in range(tiles)]

    lane = lax.broadcasted_iota(jnp.int32, (obs, pair), 1)
    ones = [(lane // head == h).astype(jnp.bfloat16) for h in range(PAIR)]

    def both_cores(cols):
        parts = [ref[:, :, cols].reshape(obs // CORES, pair) for ref in (same_ref, other_ref)]
        return jnp.concatenate(parts, axis=0)

    for group in range(HEADS // PAIR):
        cols = slice(group * pair, (group + 1) * pair)
        keys = both_cores(cols)
        values = both_cores(slice(width + group * pair, width + (group + 1) * pair))
        key_parts = [keys * one for one in ones]
        value_parts = jnp.concatenate(
            [jnp.concatenate([values * one, one], axis=1) for one in ones], axis=0
        )
        query = jnp.concatenate([ref[:, cols] for ref in queries_refs], axis=0)
        weights = []
        for part in key_parts:
            scores = lax.dot_general(query, part, NT, preferred_element_type=jnp.float32)
            pieces = []
            for t, bias in enumerate(biases):
                piece = scores[t * lon : (t + 1) * lon] * scale + bias
                top = jnp.max(piece, axis=1, keepdims=True)
                pieces.append(jnp.exp2(piece - top).astype(jnp.bfloat16))
            weights.append(jnp.concatenate(pieces, axis=0))
        both = jnp.dot(
            jnp.concatenate(weights, axis=1), value_parts, preferred_element_type=jnp.float32
        )
        mixed_ref[:, cols] = (both[:, :pair] / both[:, pair:]).astype(jnp.bfloat16)

    depth = width // len(out_weight_refs)
    projected = sum(
        jnp.dot(
            mixed_ref[:, i * depth : (i + 1) * depth], ref[...], preferred_element_type=jnp.float32
        )
        for i, ref in enumerate(out_weight_refs)
    )
    normed = []
    for t, ref in enumerate(grid_refs):
        here = slice(t * lon, (t + 1) * lon)
        hidden = (ref[...].astype(jnp.float32) + projected[here]).astype(jnp.bfloat16)
        hidden_ref[here, :] = hidden
        wide = hidden.astype(jnp.float32)
        normed.append(wide * lax.rsqrt(jnp.mean(wide * wide, axis=-1, keepdims=True) + 1e-06))
    near_ref[...] = jnp.where(core == 0, normed[-1], normed[0]).astype(jnp.bfloat16)
    far_ref[...] = jnp.where(core == 0, normed[0], normed[-1]).astype(jnp.bfloat16)


def convolve_kernel(
    tiles, lon,
    meta_ref, near_ref, far_ref, near_sent_ref, far_sent_ref, hidden_ref, *refs,
):
    conv_refs = refs[:3]
    out_ref, field_ref = refs[3:]
    core = meta_ref[0]
    for k, ref in enumerate((near_ref, near_sent_ref, far_sent_ref, far_ref)):
        place = jnp.where(core == 0, tiles + 1 - k, k) * lon
        field_ref[pl.ds(pl.multiple_of(place, lon), lon), :] = ref[...]
    sums = [None, None, None]
    for lat_off in range(3):
        moved = field_ref[lat_off * lon : (lat_off + tiles) * lon, :]
        for lon_off in range(3):
            term = jnp.dot(
                moved, conv_refs[lat_off][lon_off], preferred_element_type=jnp.float32
            )
            sums[lon_off] = term if sums[lon_off] is None else sums[lon_off] + term
    for t in range(tiles):
        here = slice(t * lon, (t + 1) * lon)
        out_ref[here, :] = (
            hidden_ref[here, :].astype(jnp.float32)
            + pltpu.roll(sums[0][here], 1, 0)
            + sums[1][here]
            + pltpu.roll(sums[2][here], lon - 1, 0)
        ).astype(jnp.bfloat16)


def on_device(
    grid_feat, queries, obs_keys, obs_values, block_mask, obs_valid, out_weight, conv_weight
):
    q_dev, width = queries.shape
    tiles, nblocks = block_mask.shape
    rows = obs_keys.shape[0]
    lon = q_dev // tiles
    obs = nblocks * OBS_BLOCK
    devices = lax.axis_size(AXES)
    pairs = devices // CORES
    core = lax.axis_index(AXES) % CORES

    block = jnp.concatenate([obs_keys, obs_values], axis=1)
    groups = [list(range(c, devices, CORES)) for c in range(CORES)]
    same = lax.all_to_all(
        jnp.broadcast_to(block[None], (pairs,) + block.shape), AXES, 0, 0, axis_index_groups=groups
    )
    swap = [(i, i ^ 1) for i in range(devices)]
    across = [(i, i + 1) for i in range(1, devices - 1, CORES)]
    across += [(target, source) for source, target in across]
    other = lax.ppermute(same, AXES, swap)

    def pieces(array, count):
        return jnp.split(array, count, axis=0)

    query_rows, grid_rows, weight_rows, conv_rows = lax.optimization_barrier(
        (
            pieces(queries, tiles),
            pieces(grid_feat, tiles),
            pieces(out_weight, 2),
            [conv_weight[i] for i in range(3)],
        )
    )
    meta = jnp.concatenate([core.astype(jnp.int32)[None], obs_valid, block_mask.reshape(-1)])

    vmem = pl.BlockSpec(memory_space=pltpu.VMEM)
    smem = pl.BlockSpec(memory_space=pltpu.SMEM)
    row_shape = jax.ShapeDtypeStruct((lon, width), jnp.bfloat16)
    full_shape = jax.ShapeDtypeStruct((q_dev, width), jnp.bfloat16)
    hidden, near_sent, far_sent = pl.pallas_call(
        functools.partial(attend_kernel, tiles, lon, width, nblocks, rows),
        out_shape=[full_shape, row_shape, row_shape],
        in_specs=[smem] + [vmem] * (4 + 2 * tiles),
        out_specs=[vmem] * 3,
        scratch_shapes=[pltpu.VMEM((q_dev, width), jnp.bfloat16)],
        compiler_params=pltpu.CompilerParams(vmem_limit_bytes=40 * 2**20),
        cost_estimate=pl.CostEstimate(
            flops=2 * q_dev * width * (width + 4 * obs), bytes_accessed=q_dev * width * 8, transcendentals=0
        ),
        name="attend",
    )(meta, same, other, *query_rows, *grid_rows, *weight_rows)
    far = lax.ppermute(far_sent, AXES, across)
    near = lax.ppermute(near_sent, AXES, swap)
    return pl.pallas_call(
        functools.partial(convolve_kernel, tiles, lon),
        out_shape=full_shape,
        in_specs=[smem] + [vmem] * 8,
        out_specs=vmem,
        scratch_shapes=[pltpu.VMEM(((tiles + 2) * lon, width), jnp.bfloat16)],
        compiler_params=pltpu.CompilerParams(vmem_limit_bytes=40 * 2**20),
        cost_estimate=pl.CostEstimate(
            flops=18 * q_dev * width * width, bytes_accessed=2 * conv_weight.size, transcendentals=0
        ),
        name="convolve",
    )(meta, near, far, near_sent, far_sent, hidden, *conv_rows)


def solution(mesh):
    in_specs = (
        P(AXES, None),
        P(AXES, None),
        P(AXES, None),
        P(AXES, None),
        P(AXES, None),
        P(),
        P(),
        P(),
    )
    return jax.shard_map(
        on_device, mesh=mesh, in_specs=in_specs, out_specs=P(AXES, None), check_vma=False
    )
```

```python
import functools
import math

import jax
import jax.numpy as jnp
from jax import lax
from jax.experimental import pallas as pl
from jax.experimental.pallas import tpu as pltpu
from jax.sharding import PartitionSpec as P

HEADS = 8
OBS_BLOCK = 128
AXES = ("blk", "tile")
PAIR = 2
CORES = 2
MASK_ROWS = 16
NT = (((1,), (1,)), ((), ()))


def layer_kernel(
    tiles, lon, width, nblocks, rows,
    meta_ref, near_ref, far_ref, same_ref, other_ref, *refs,
):
    queries_refs, grid_refs = refs[:tiles], refs[tiles : 2 * tiles]
    out_weight_refs = refs[2 * tiles : 2 * tiles + 2]
    conv_hbm, out_ref, conv_ref, mixed_ref, field_ref, sems = refs[2 * tiles + 2 :]
    head = width // HEADS
    pair = PAIR * head
    obs = nblocks * OBS_BLOCK
    scale = head ** (-0.5) * math.log2(math.e)
    copies = [
        pltpu.make_async_copy(conv_hbm.at[lat_off], conv_ref.at[lat_off], sems.at[lat_off])
        for lat_off in range(3)
    ]
    for copy in copies:
        copy.start()

    core = meta_ref[2]

    def halo(side, place, cols):
        near_first = core == (1 if side == 0 else 0)
        return jnp.where(near_first, near_ref[place, cols], far_ref[place, cols])

    every = slice(0, width)
    query_place, grid_place = slice(0, lon), slice(lon, 2 * lon)
    mask_place = slice(2 * lon, 2 * lon + MASK_ROWS)
    half = OBS_BLOCK // CORES
    key_lane = lax.broadcasted_iota(jnp.int32, (1, OBS_BLOCK), 1)
    spread = (key_lane % half) // rows * (CORES * rows) + key_lane % rows
    first = key_lane < half

    def row_bias(limit_of):
        parts = []
        for parity in (core, 1 - core):
            place = spread + parity * rows
            for block in range(0, nblocks, CORES):
                limit = jnp.where(first, limit_of(block), limit_of(block + 1))
                parts.append(jnp.where(place < limit, 0.0, -jnp.inf))
        return jnp.concatenate(parts, axis=1)

    def own_limit(tile, block):
        allowed = meta_ref[3 + (1 + tile) * nblocks + block] > 0
        return jnp.where(allowed, meta_ref[3 + block], 0)

    def halo_limit(row, block):
        allowed = jnp.broadcast_to(row[:, block : block + 1], (1, OBS_BLOCK)) > 0.5
        return jnp.where(allowed, meta_ref[3 + block], 0)

    mask_rows = [halo(side, mask_place, every).astype(jnp.float32)[:1] for side in range(2)]
    biases = [row_bias(functools.partial(halo_limit, mask_rows[0]))]
    biases += [row_bias(functools.partial(own_limit, t)) for t in range(tiles)]
    biases += [row_bias(functools.partial(halo_limit, mask_rows[1]))]

    lane = lax.broadcasted_iota(jnp.int32, (obs, pair), 1)
    ones = [(lane // head == h).astype(jnp.bfloat16) for h in range(PAIR)]

    def both_parities(cols):
        parts = [ref[:, :, cols].reshape(obs // CORES, pair) for ref in (same_ref, other_ref)]
        return jnp.concatenate(parts, axis=0)

    for group in range(HEADS // PAIR):
        cols = slice(group * pair, (group + 1) * pair)
        keys = both_parities(cols)
        values = both_parities(slice(width + group * pair, width + (group + 1) * pair))
        key_parts = [keys * one for one in ones]
        value_parts = jnp.concatenate(
            [jnp.concatenate([values * one, one], axis=1) for one in ones], axis=0
        )
        query = jnp.concatenate(
            [halo(0, query_place, cols)]
            + [ref[:, cols] for ref in queries_refs]
            + [halo(1, query_place, cols)],
            axis=0,
        )
        weights = []
        for part in key_parts:
            scores = lax.dot_general(query, part, NT, preferred_element_type=jnp.float32)
            pieces = []
            for t, bias in enumerate(biases):
                piece = scores[t * lon : (t + 1) * lon] * scale + bias
                top = jnp.max(piece, axis=1, keepdims=True)
                pieces.append(jnp.exp2(piece - top).astype(jnp.bfloat16))
            weights.append(jnp.concatenate(pieces, axis=0))
        both = jnp.dot(
            jnp.concatenate(weights, axis=1), value_parts, preferred_element_type=jnp.float32
        )
        mixed_ref[:, cols] = (both[:, :pair] / both[:, pair:]).astype(jnp.bfloat16)

    depth = width // len(out_weight_refs)
    projected = sum(
        jnp.dot(
            mixed_ref[:, i * depth : (i + 1) * depth], ref[...], preferred_element_type=jnp.float32
        )
        for i, ref in enumerate(out_weight_refs)
    )
    grid = jnp.concatenate(
        [halo(0, grid_place, every)] + [ref[...] for ref in grid_refs] + [halo(1, grid_place, every)],
        axis=0,
    )
    hidden = (grid.astype(jnp.float32) + projected).astype(jnp.bfloat16)
    wide = hidden.astype(jnp.float32)
    normed = wide * lax.rsqrt(jnp.mean(wide * wide, axis=-1, keepdims=True) + 1e-06)
    last = (tiles + 1) * lon
    field_ref[lon:last] = normed[lon:last].astype(jnp.bfloat16)
    field_ref[:lon] = jnp.where(meta_ref[0] > 0, normed[:lon], 0.0).astype(jnp.bfloat16)
    field_ref[last:] = jnp.where(meta_ref[1] > 0, normed[last:], 0.0).astype(jnp.bfloat16)

    sums = [None, None, None]
    for lat_off in range(3):
        copies[lat_off].wait()
        moved = field_ref[lat_off * lon : (lat_off + tiles) * lon, :]
        for lon_off in range(3):
            term = jnp.dot(moved, conv_ref[lat_off, lon_off], preferred_element_type=jnp.float32)
            sums[lon_off] = term if sums[lon_off] is None else sums[lon_off] + term
    for t in range(tiles):
        here = slice(t * lon, (t + 1) * lon)
        out_ref[here, :] = (
            wide[(t + 1) * lon : (t + 2) * lon]
            + pltpu.roll(sums[0][here], 1, 0)
            + sums[1][here]
            + pltpu.roll(sums[2][here], lon - 1, 0)
        ).astype(jnp.bfloat16)


def on_device(
    grid_feat, queries, obs_keys, obs_values, block_mask, obs_valid, out_weight, conv_weight
):
    q_dev, width = queries.shape
    tiles, nblocks = block_mask.shape
    lon = q_dev // tiles
    devices = lax.axis_size(AXES)
    me = lax.axis_index(AXES)
    edge = jnp.stack([me > 0, me < devices - 1]).astype(jnp.int32)
    meta = jnp.concatenate([edge, (me % CORES)[None], obs_valid, block_mask.reshape(-1)])

    kv_local = jnp.concatenate([obs_keys, obs_values], axis=1)
    groups = [list(range(parity, devices, CORES)) for parity in range(CORES)]
    blocks = jnp.broadcast_to(kv_local[None], (devices // CORES,) + kv_local.shape)
    same = lax.all_to_all(blocks, AXES, 0, 0, axis_index_groups=groups)
    swap = [(i, i ^ 1) for i in range(devices)]
    across = [(i, i + 1) for i in range(1, devices - 1, CORES)]
    across += [(target, source) for source, target in across]

    def pieces(array, count):
        return jnp.split(array, count, axis=0)

    query_rows, grid_rows, weight_rows = lax.optimization_barrier(
        (pieces(queries, tiles), pieces(grid_feat, tiles), pieces(out_weight, 2))
    )
    mask_tile = jnp.pad(block_mask.astype(jnp.bfloat16), ((0, 0), (0, width - nblocks)))

    def packed(tile):
        mask = jnp.broadcast_to(mask_tile[tile][None], (MASK_ROWS, width))
        return jnp.concatenate([query_rows[tile], grid_rows[tile], mask], axis=0)

    first, last = packed(0), packed(tiles - 1)
    even = me % CORES == 0
    far = lax.ppermute(jnp.where(even, first, last), AXES, across)
    near = lax.ppermute(jnp.where(even, last, first), AXES, swap)
    other = lax.ppermute(same, AXES, swap)

    vmem = pl.BlockSpec(memory_space=pltpu.VMEM)
    smem = pl.BlockSpec(memory_space=pltpu.SMEM)
    flops = 2 * q_dev * width * (9 * width + 2 * width + 4 * nblocks * OBS_BLOCK)
    return pl.pallas_call(
        functools.partial(layer_kernel, tiles, lon, width, nblocks, obs_keys.shape[0]),
        out_shape=jax.ShapeDtypeStruct((q_dev, width), jnp.bfloat16),
        in_specs=[smem] + [vmem] * (6 + 2 * tiles) + [pl.BlockSpec(memory_space=pltpu.HBM)],
        out_specs=vmem,
        scratch_shapes=[
            pltpu.VMEM(conv_weight.shape, jnp.bfloat16),
            pltpu.VMEM(((tiles + 2) * lon, width), jnp.bfloat16),
            pltpu.VMEM(((tiles + 2) * lon, width), jnp.bfloat16),
            pltpu.SemaphoreType.DMA((3,)),
        ],
        compiler_params=pltpu.CompilerParams(vmem_limit_bytes=48 * 2**20),
        cost_estimate=pl.CostEstimate(
            flops=flops, bytes_accessed=2 * conv_weight.size, transcendentals=0
        ),
        name="layer",
    )(meta, near, far, same, other, *query_rows, *grid_rows, *weight_rows, conv_weight)


def solution(mesh):
    in_specs = (
        P(AXES, None),
        P(AXES, None),
        P(AXES, None),
        P(AXES, None),
        P(AXES, None),
        P(),
        P(),
        P(),
    )
    return jax.shard_map(
        on_device, mesh=mesh, in_specs=in_specs, out_specs=P(AXES, None), check_vma=False
    )
```

```python
import functools
import math

import jax
import jax.numpy as jnp
from jax import lax
from jax.experimental import pallas as pl
from jax.experimental.pallas import tpu as pltpu
from jax.sharding import PartitionSpec as P

HEADS = 8
OBS_BLOCK = 128
AXES = ("blk", "tile")
PAIR = 2
CORES = 2
MASK_ROWS = 16
NT = (((1,), (1,)), ((), ()))


def attend(lon, width, nblocks, rows, core, valid, row_refs, same_ref, other_ref, weight_refs, mixed_ref):
    head = width // HEADS
    pair = PAIR * head
    obs = nblocks * OBS_BLOCK
    scale = head ** (-0.5) * math.log2(math.e)
    half = OBS_BLOCK // CORES
    key_lane = lax.broadcasted_iota(jnp.int32, (1, OBS_BLOCK), 1)
    spread = (key_lane % half) // rows * (CORES * rows) + key_lane % rows
    first = key_lane < half

    def row_bias(ref):
        mask = ref[2 * lon : 2 * lon + MASK_ROWS, :].astype(jnp.float32)[:1]

        def limit(block):
            allowed = jnp.broadcast_to(mask[:, block : block + 1], (1, OBS_BLOCK)) > 0.5
            return jnp.where(allowed, valid(block), 0)

        parts = []
        for parity in (core, 1 - core):
            place = spread + parity * rows
            for block in range(0, nblocks, CORES):
                end = jnp.where(first, limit(block), limit(block + 1))
                parts.append(jnp.where(place < end, 0.0, -jnp.inf))
        return jnp.concatenate(parts, axis=1)

    biases = [row_bias(ref) for ref in row_refs]
    lane = lax.broadcasted_iota(jnp.int32, (obs, pair), 1)
    ones = [(lane // head == h).astype(jnp.bfloat16) for h in range(PAIR)]

    def both_cores(cols):
        parts = [ref[:, :, cols].reshape(obs // CORES, pair) for ref in (same_ref, other_ref)]
        return jnp.concatenate(parts, axis=0)

    for group in range(HEADS // PAIR):
        cols = slice(group * pair, (group + 1) * pair)
        keys = both_cores(cols)
        values = both_cores(slice(width + group * pair, width + (group + 1) * pair))
        key_parts = [keys * one for one in ones]
        value_parts = jnp.concatenate(
            [jnp.concatenate([values * one, one], axis=1) for one in ones], axis=0
        )
        query = jnp.concatenate([ref[:lon, cols] for ref in row_refs], axis=0)
        weights = []
        for part in key_parts:
            scores = lax.dot_general(query, part, NT, preferred_element_type=jnp.float32)
            pieces = []
            for t, bias in enumerate(biases):
                piece = scores[t * lon : (t + 1) * lon] * scale + bias
                top = jnp.max(piece, axis=1, keepdims=True)
                pieces.append(jnp.exp2(piece - top).astype(jnp.bfloat16))
            weights.append(jnp.concatenate(pieces, axis=0))
        both = jnp.dot(
            jnp.concatenate(weights, axis=1), value_parts, preferred_element_type=jnp.float32
        )
        mixed_ref[:, cols] = (both[:, :pair] / both[:, pair:]).astype(jnp.bfloat16)

    depth = width // len(weight_refs)
    projected = sum(
        jnp.dot(
            mixed_ref[:, i * depth : (i + 1) * depth], ref[...], preferred_element_type=jnp.float32
        )
        for i, ref in enumerate(weight_refs)
    )
    grid = jnp.concatenate([ref[lon : 2 * lon, :] for ref in row_refs], axis=0)
    wide = (grid.astype(jnp.float32) + projected).astype(jnp.bfloat16).astype(jnp.float32)
    normed = wide * lax.rsqrt(jnp.mean(wide * wide, axis=-1, keepdims=True) + 1e-06)
    return wide, normed


def around(parts, lon):
    return pltpu.roll(parts[0], 1, 0) + parts[1] + pltpu.roll(parts[2], lon - 1, 0)


def inner_kernel(
    lon, width, nblocks, rows,
    meta_ref, near_ref, near_sent_ref, far_sent_ref, same_ref, other_ref, upper_ref, lower_ref,
    conv_hbm, done_ref, partial_ref, conv_ref, mixed_ref, field_ref, sems,
):
    core = meta_ref[0]
    copies = [
        pltpu.make_async_copy(conv_hbm.at[source], conv_ref.at[i], sems.at[i])
        for i, source in enumerate((1, 2 - 2 * core, 2 * core))
    ]
    for copy in copies:
        copy.start()
    wide, normed = attend(
        lon, width, nblocks, rows, core, lambda block: meta_ref[2 + block],
        (near_ref, near_sent_ref, far_sent_ref), same_ref, other_ref, (upper_ref, lower_ref), mixed_ref,
    )
    field_ref[...] = normed.astype(jnp.bfloat16)
    for copy in copies:
        copy.wait()
    inputs = jnp.concatenate([field_ref[lon:, :], field_ref[: 2 * lon, :]], axis=1)
    full, open_end = [], []
    for lon_off in range(3):
        taps = conv_ref[:2, lon_off].reshape(2 * width, width)
        term = jnp.dot(inputs, taps, preferred_element_type=jnp.float32)
        full.append(
            term[:lon]
            + jnp.dot(field_ref[2 * lon :, :], conv_ref[2, lon_off], preferred_element_type=jnp.float32)
        )
        open_end.append(term[lon:])
    done_ref[...] = (wide[lon : 2 * lon] + around(full, lon)).astype(jnp.bfloat16)
    partial_ref[...] = wide[2 * lon :] + around(open_end, lon)


def outer_kernel(
    lon, width, nblocks, rows,
    meta_ref, far_ref, same_ref, other_ref, upper_ref, lower_ref, done_ref, partial_ref,
    conv_hbm, out_ref, conv_ref, mixed_ref, sem,
):
    core = meta_ref[0]
    copy = pltpu.make_async_copy(conv_hbm.at[2 * core], conv_ref, sem)
    copy.start()
    _, normed = attend(
        lon, width, nblocks, rows, core, lambda block: meta_ref[2 + block],
        (far_ref,), same_ref, other_ref, (upper_ref, lower_ref), mixed_ref,
    )
    field = jnp.where(meta_ref[1] > 0, normed, 0.0).astype(jnp.bfloat16)
    copy.wait()
    parts = [
        jnp.dot(field, conv_ref[lon_off], preferred_element_type=jnp.float32) for lon_off in range(3)
    ]
    last = (partial_ref[...] + around(parts, lon)).astype(jnp.bfloat16)
    out_ref[pl.ds(pl.multiple_of((1 - core) * lon, lon), lon), :] = done_ref[...]
    out_ref[pl.ds(pl.multiple_of(core * lon, lon), lon), :] = last


def on_device(
    grid_feat, queries, obs_keys, obs_values, block_mask, obs_valid, out_weight, conv_weight
):
    q_dev, width = queries.shape
    tiles, nblocks = block_mask.shape
    rows = obs_keys.shape[0]
    lon = q_dev // tiles
    obs = nblocks * OBS_BLOCK
    devices = lax.axis_size(AXES)
    pairs = devices // CORES
    me = lax.axis_index(AXES)
    core = me % CORES

    block = jnp.concatenate([obs_keys, obs_values], axis=1)
    groups = [list(range(c, devices, CORES)) for c in range(CORES)]
    same = lax.all_to_all(
        jnp.broadcast_to(block[None], (pairs,) + block.shape), AXES, 0, 0, axis_index_groups=groups
    )
    swap = [(i, i ^ 1) for i in range(devices)]
    across = [(i, i + 1) for i in range(1, devices - 1, CORES)]
    across += [(target, source) for source, target in across]

    query_rows, grid_rows = lax.optimization_barrier(
        (jnp.split(queries, tiles, axis=0), jnp.split(grid_feat, tiles, axis=0))
    )
    mask_tile = jnp.pad(block_mask.astype(jnp.bfloat16), ((0, 0), (0, width - nblocks)))

    def packed(tile):
        mask = jnp.broadcast_to(mask_tile[tile][None], (MASK_ROWS, width))
        return jnp.concatenate([query_rows[tile], grid_rows[tile], mask], axis=0)

    first, last = packed(0), packed(tiles - 1)
    far_sent = jnp.where(core == 0, first, last)
    near_sent = jnp.where(core == 0, last, first)
    far = lax.ppermute(far_sent, AXES, across)
    near = lax.ppermute(near_sent, AXES, swap)
    other = lax.ppermute(same, AXES, swap)
    out_weight, _ = lax.optimization_barrier((out_weight, same))
    upper, lower = lax.optimization_barrier(tuple(jnp.split(out_weight, 2, axis=0)))

    far_exists = (me > 0) & (me < devices - 1)
    meta = jnp.concatenate([jnp.stack([core, far_exists.astype(core.dtype)]).astype(jnp.int32), obs_valid])

    vmem = pl.BlockSpec(memory_space=pltpu.VMEM)
    smem = pl.BlockSpec(memory_space=pltpu.SMEM)
    hbm = pl.BlockSpec(memory_space=pltpu.HBM)
    sizes = (lon, width, nblocks, rows)
    params = pltpu.CompilerParams(vmem_limit_bytes=48 * 2**20)
    tap_flops, row_flops = 2 * lon * width * width, 2 * lon * width * (width + 4 * obs)
    done, partial = pl.pallas_call(
        functools.partial(inner_kernel, *sizes),
        out_shape=[
            jax.ShapeDtypeStruct((lon, width), jnp.bfloat16),
            jax.ShapeDtypeStruct((lon, width), jnp.float32),
        ],
        in_specs=[smem] + [vmem] * 7 + [hbm],
        out_specs=[vmem] * 2,
        scratch_shapes=[
            pltpu.VMEM(conv_weight.shape, jnp.bfloat16),
            pltpu.VMEM((3 * lon, width), jnp.bfloat16),
            pltpu.VMEM((3 * lon, width), jnp.bfloat16),
            pltpu.SemaphoreType.DMA((3,)),
        ],
        compiler_params=params,
        cost_estimate=pl.CostEstimate(
            flops=3 * row_flops + 15 * tap_flops, bytes_accessed=2 * conv_weight.size, transcendentals=0
        ),
        name="inner",
    )(meta, near, near_sent, far_sent, same, other, upper, lower, conv_weight)
    return pl.pallas_call(
        functools.partial(outer_kernel, *sizes),
        out_shape=jax.ShapeDtypeStruct((q_dev, width), jnp.bfloat16),
        in_specs=[smem] + [vmem] * 7 + [hbm],
        out_specs=vmem,
        scratch_shapes=[
            pltpu.VMEM(conv_weight.shape[1:], jnp.bfloat16),
            pltpu.VMEM((lon, width), jnp.bfloat16),
            pltpu.SemaphoreType.DMA,
        ],
        compiler_params=params,
        cost_estimate=pl.CostEstimate(
            flops=row_flops + 3 * tap_flops, bytes_accessed=conv_weight.size, transcendentals=0
        ),
        name="outer",
    )(meta, far, same, other, upper, lower, done, partial, conv_weight)


def solution(mesh):
    in_specs = (
        P(AXES, None),
        P(AXES, None),
        P(AXES, None),
        P(AXES, None),
        P(AXES, None),
        P(),
        P(),
        P(),
    )
    return jax.shard_map(
        on_device, mesh=mesh, in_specs=in_specs, out_specs=P(AXES, None), check_vma=False
    )
```

```python
import functools
import math

import jax
import jax.numpy as jnp
from jax import lax
from jax.experimental import pallas as pl
from jax.experimental.pallas import tpu as pltpu
from jax.sharding import PartitionSpec as P

HEADS = 8
OBS_BLOCK = 128
AXES = ("blk", "tile")
PAIR = 2
CORES = 2
MASK_ROWS = 16
NT = (((1,), (1,)), ((), ()))


def attend(lon, width, nblocks, rows, core, valid, row_refs, same_ref, other_ref, weight_refs, mixed_ref):
    head = width // HEADS
    pair = PAIR * head
    obs = nblocks * OBS_BLOCK
    scale = head ** (-0.5) * math.log2(math.e)
    half = OBS_BLOCK // CORES
    key_lane = lax.broadcasted_iota(jnp.int32, (1, OBS_BLOCK), 1)
    spread = (key_lane % half) // rows * (CORES * rows) + key_lane % rows
    first = key_lane < half

    def row_bias(ref):
        mask = ref[2 * lon : 2 * lon + MASK_ROWS, :].astype(jnp.float32)[:1]

        def limit(block):
            allowed = jnp.broadcast_to(mask[:, block : block + 1], (1, OBS_BLOCK)) > 0.5
            return jnp.where(allowed, valid(block), 0)

        parts = []
        for parity in (core, 1 - core):
            place = spread + parity * rows
            for block in range(0, nblocks, CORES):
                end = jnp.where(first, limit(block), limit(block + 1))
                parts.append(jnp.where(place < end, 0.0, -jnp.inf))
        return jnp.concatenate(parts, axis=1)

    biases = [row_bias(ref) for ref in row_refs]
    lane = lax.broadcasted_iota(jnp.int32, (obs, pair), 1)
    ones = [(lane // head == h).astype(jnp.bfloat16) for h in range(PAIR)]

    def both_cores(cols):
        parts = [ref[:, :, cols].reshape(obs // CORES, pair) for ref in (same_ref, other_ref)]
        return jnp.concatenate(parts, axis=0)

    def columns(group):
        return slice(group * pair, (group + 1) * pair)

    def scores_of(group):
        keys = both_cores(columns(group))
        query = jnp.concatenate([ref[:lon, columns(group)] for ref in row_refs], axis=0)
        return [
            lax.dot_general(query, keys * one, NT, preferred_element_type=jnp.float32) for one in ones
        ]

    def weights_of(scores):
        pieces = []
        for t, bias in enumerate(biases):
            piece = scores[t * lon : (t + 1) * lon] * scale + bias
            top = jnp.max(piece, axis=1, keepdims=True)
            pieces.append(jnp.exp2(piece - top).astype(jnp.bfloat16))
        return jnp.concatenate(pieces, axis=0)

    groups = HEADS // PAIR
    ahead = scores_of(0)
    for group in range(groups):
        scores, ahead = ahead, scores_of(group + 1) if group + 1 < groups else None
        values = both_cores(columns(groups + group))
        value_parts = jnp.concatenate(
            [jnp.concatenate([values * one, one], axis=1) for one in ones], axis=0
        )
        weights = jnp.concatenate([weights_of(part) for part in scores], axis=1)
        both = jnp.dot(weights, value_parts, preferred_element_type=jnp.float32)
        mixed_ref[:, columns(group)] = (both[:, :pair] / both[:, pair:]).astype(jnp.bfloat16)

    depth = width // len(weight_refs)
    projected = sum(
        jnp.dot(
            mixed_ref[:, i * depth : (i + 1) * depth], ref[...], preferred_element_type=jnp.float32
        )
        for i, ref in enumerate(weight_refs)
    )
    grid = jnp.concatenate([ref[lon : 2 * lon, :] for ref in row_refs], axis=0)
    wide = (grid.astype(jnp.float32) + projected).astype(jnp.bfloat16).astype(jnp.float32)
    normed = wide * lax.rsqrt(jnp.mean(wide * wide, axis=-1, keepdims=True) + 1e-06)
    return wide, normed


def around(parts, lon):
    return pltpu.roll(parts[0], 1, 0) + parts[1] + pltpu.roll(parts[2], lon - 1, 0)


def inner_kernel(
    lon, width, nblocks, rows,
    meta_ref, near_ref, near_sent_ref, far_sent_ref, same_ref, other_ref, upper_ref, lower_ref,
    conv_hbm, done_ref, partial_ref, conv_ref, mixed_ref, field_ref, sems,
):
    core = meta_ref[0]
    copies = [
        pltpu.make_async_copy(conv_hbm.at[source], conv_ref.at[i], sems.at[i])
        for i, source in enumerate((1, 2 - 2 * core, 2 * core))
    ]
    for copy in copies:
        copy.start()
    wide, normed = attend(
        lon, width, nblocks, rows, core, lambda block: meta_ref[2 + block],
        (near_ref, near_sent_ref, far_sent_ref), same_ref, other_ref, (upper_ref, lower_ref), mixed_ref,
    )
    field_ref[...] = normed.astype(jnp.bfloat16)
    for copy in copies:
        copy.wait()
    inputs = jnp.concatenate([field_ref[lon:, :], field_ref[: 2 * lon, :]], axis=1)
    full, open_end = [], []
    for lon_off in range(3):
        taps = conv_ref[:2, lon_off].reshape(2 * width, width)
        term = jnp.dot(inputs, taps, preferred_element_type=jnp.float32)
        full.append(
            term[:lon]
            + jnp.dot(field_ref[2 * lon :, :], conv_ref[2, lon_off], preferred_element_type=jnp.float32)
        )
        open_end.append(term[lon:])
    done_ref[...] = (wide[lon : 2 * lon] + around(full, lon)).astype(jnp.bfloat16)
    partial_ref[...] = wide[2 * lon :] + around(open_end, lon)


def outer_kernel(
    lon, width, nblocks, rows,
    meta_ref, far_ref, same_ref, other_ref, upper_ref, lower_ref, done_ref, partial_ref,
    conv_hbm, out_ref, conv_ref, mixed_ref, sem,
):
    core = meta_ref[0]
    copy = pltpu.make_async_copy(conv_hbm.at[2 * core], conv_ref, sem)
    copy.start()
    _, normed = attend(
        lon, width, nblocks, rows, core, lambda block: meta_ref[2 + block],
        (far_ref,), same_ref, other_ref, (upper_ref, lower_ref), mixed_ref,
    )
    field = jnp.where(meta_ref[1] > 0, normed, 0.0).astype(jnp.bfloat16)
    copy.wait()
    parts = [
        jnp.dot(field, conv_ref[lon_off], preferred_element_type=jnp.float32) for lon_off in range(3)
    ]
    last = (partial_ref[...] + around(parts, lon)).astype(jnp.bfloat16)
    out_ref[pl.ds(pl.multiple_of((1 - core) * lon, lon), lon), :] = done_ref[...]
    out_ref[pl.ds(pl.multiple_of(core * lon, lon), lon), :] = last


def on_device(
    grid_feat, queries, obs_keys, obs_values, block_mask, obs_valid, out_weight, conv_weight
):
    q_dev, width = queries.shape
    tiles, nblocks = block_mask.shape
    rows = obs_keys.shape[0]
    lon = q_dev // tiles
    obs = nblocks * OBS_BLOCK
    devices = lax.axis_size(AXES)
    pairs = devices // CORES
    me = lax.axis_index(AXES)
    core = me % CORES

    block = jnp.concatenate([obs_keys, obs_values], axis=1)
    groups = [list(range(c, devices, CORES)) for c in range(CORES)]
    same = lax.all_to_all(
        jnp.broadcast_to(block[None], (pairs,) + block.shape), AXES, 0, 0, axis_index_groups=groups
    )
    swap = [(i, i ^ 1) for i in range(devices)]
    across = [(i, i + 1) for i in range(1, devices - 1, CORES)]
    across += [(target, source) for source, target in across]

    query_rows, grid_rows = lax.optimization_barrier(
        (jnp.split(queries, tiles, axis=0), jnp.split(grid_feat, tiles, axis=0))
    )
    mask_tile = jnp.pad(block_mask.astype(jnp.bfloat16), ((0, 0), (0, width - nblocks)))

    def packed(tile):
        mask = jnp.broadcast_to(mask_tile[tile][None], (MASK_ROWS, width))
        return jnp.concatenate([query_rows[tile], grid_rows[tile], mask], axis=0)

    first, last = packed(0), packed(tiles - 1)
    far_sent = jnp.where(core == 0, first, last)
    near_sent = jnp.where(core == 0, last, first)
    far = lax.ppermute(far_sent, AXES, across)
    near = lax.ppermute(near_sent, AXES, swap)
    out_weight, obs_valid, near = lax.optimization_barrier((out_weight, obs_valid, near))
    far_exists = (me > 0) & (me < devices - 1)
    meta = jnp.concatenate([jnp.stack([core, far_exists.astype(core.dtype)]).astype(jnp.int32), obs_valid])
    upper, lower = jnp.split(out_weight, 2, axis=0)
    same, upper, lower, meta = lax.optimization_barrier((same, upper, lower, meta))
    other = lax.ppermute(same, AXES, swap)

    vmem = pl.BlockSpec(memory_space=pltpu.VMEM)
    smem = pl.BlockSpec(memory_space=pltpu.SMEM)
    hbm = pl.BlockSpec(memory_space=pltpu.HBM)
    sizes = (lon, width, nblocks, rows)
    params = pltpu.CompilerParams(vmem_limit_bytes=48 * 2**20)
    tap_flops, row_flops = 2 * lon * width * width, 2 * lon * width * (width + 4 * obs)
    done, partial = pl.pallas_call(
        functools.partial(inner_kernel, *sizes),
        out_shape=[
            jax.ShapeDtypeStruct((lon, width), jnp.bfloat16),
            jax.ShapeDtypeStruct((lon, width), jnp.float32),
        ],
        in_specs=[smem] + [vmem] * 7 + [hbm],
        out_specs=[vmem] * 2,
        scratch_shapes=[
            pltpu.VMEM(conv_weight.shape, jnp.bfloat16),
            pltpu.VMEM((3 * lon, width), jnp.bfloat16),
            pltpu.VMEM((3 * lon, width), jnp.bfloat16),
            pltpu.SemaphoreType.DMA((3,)),
        ],
        compiler_params=params,
        cost_estimate=pl.CostEstimate(
            flops=3 * row_flops + 15 * tap_flops, bytes_accessed=2 * conv_weight.size, transcendentals=0
        ),
        name="inner",
    )(meta, near, near_sent, far_sent, same, other, upper, lower, conv_weight)
    return pl.pallas_call(
        functools.partial(outer_kernel, *sizes),
        out_shape=jax.ShapeDtypeStruct((q_dev, width), jnp.bfloat16),
        in_specs=[smem] + [vmem] * 7 + [hbm],
        out_specs=vmem,
        scratch_shapes=[
            pltpu.VMEM(conv_weight.shape[1:], jnp.bfloat16),
            pltpu.VMEM((lon, width), jnp.bfloat16),
            pltpu.SemaphoreType.DMA,
        ],
        compiler_params=params,
        cost_estimate=pl.CostEstimate(
            flops=row_flops + 3 * tap_flops, bytes_accessed=conv_weight.size, transcendentals=0
        ),
        name="outer",
    )(meta, far, same, other, upper, lower, done, partial, conv_weight)


def solution(mesh):
    in_specs = (
        P(AXES, None),
        P(AXES, None),
        P(AXES, None),
        P(AXES, None),
        P(AXES, None),
        P(),
        P(),
        P(),
    )
    return jax.shard_map(
        on_device, mesh=mesh, in_specs=in_specs, out_specs=P(AXES, None), check_vma=False
    )
```

```python
import functools
import math

import jax
import jax.numpy as jnp
from jax import lax
from jax.experimental import pallas as pl
from jax.experimental.pallas import tpu as pltpu
from jax.sharding import PartitionSpec as P

HEADS = 8
OBS_BLOCK = 128
AXES = ("blk", "tile")
PAIR = 2
CORES = 2
LIMIT_ROWS = 16


def both_cores(same_ref, other_ref, cols):
    return jnp.concatenate(
        [ref[:, :, cols].reshape(-1, cols.stop - cols.start) for ref in (same_ref, other_ref)], axis=0
    )


def attend(lon, width, nblocks, rows, core, row_refs, keys_of, same_ref, other_ref, weight_refs, mixed_ref):
    head = width // HEADS
    pair = PAIR * head
    obs = nblocks * OBS_BLOCK
    scale = head ** (-0.5) * math.log2(math.e)
    half = OBS_BLOCK // CORES
    key_lane = lax.broadcasted_iota(jnp.int32, (1, OBS_BLOCK), 1)
    spread = (key_lane % half) // rows * (CORES * rows) + key_lane % rows
    first = key_lane < half

    def row_bias(ref):
        limit = ref[2 * lon : 2 * lon + LIMIT_ROWS, :].astype(jnp.float32)[:1].astype(jnp.int32)

        parts = []
        for parity in (core, 1 - core):
            place = spread + parity * rows
            for block in range(0, nblocks, CORES):
                ends = [
                    jnp.broadcast_to(limit[:, b : b + 1], (1, OBS_BLOCK)) for b in (block, block + 1)
                ]
                end = jnp.where(first, ends[0], ends[1])
                parts.append(jnp.where(place < end, 0.0, -jnp.inf))
        return jnp.concatenate(parts, axis=1)

    biases = [row_bias(ref) for ref in row_refs]
    lane = lax.broadcasted_iota(jnp.int32, (obs, pair), 1)
    ones = [(lane // head == h).astype(jnp.bfloat16) for h in range(PAIR)]

    empty = jnp.zeros((head, obs), jnp.bfloat16)

    def columns(group):
        return slice(group * pair, (group + 1) * pair)

    def scores_of(group):
        keys = keys_of(columns(group))
        query = jnp.concatenate([ref[:lon, columns(group)] for ref in row_refs], axis=0)
        scores = []
        for h in range(PAIR):
            part = [keys[i * head : (i + 1) * head] if i == h else empty for i in range(PAIR)]
            part = jnp.concatenate(part, axis=0)
            scores.append(jnp.dot(query, part, preferred_element_type=jnp.float32))
        return scores

    def weights_of(scores):
        pieces = []
        for t, bias in enumerate(biases):
            piece = scores[t * lon : (t + 1) * lon] * scale + bias
            top = jnp.max(piece, axis=1, keepdims=True)
            pieces.append(jnp.exp2(piece - top).astype(jnp.bfloat16))
        return jnp.concatenate(pieces, axis=0)

    groups = HEADS // PAIR
    ahead = scores_of(0)
    for group in range(groups):
        scores, ahead = ahead, scores_of(group + 1) if group + 1 < groups else None
        values = both_cores(same_ref, other_ref, columns(groups + group))
        value_parts = jnp.concatenate(
            [jnp.concatenate([values * one, one], axis=1) for one in ones], axis=0
        )
        weights = jnp.concatenate([weights_of(part) for part in scores], axis=1)
        both = jnp.dot(weights, value_parts, preferred_element_type=jnp.float32)
        mixed_ref[:, columns(group)] = (both[:, :pair] / both[:, pair:]).astype(jnp.bfloat16)

    depth = width // len(weight_refs)
    projected = sum(
        jnp.dot(
            mixed_ref[:, i * depth : (i + 1) * depth], ref[...], preferred_element_type=jnp.float32
        )
        for i, ref in enumerate(weight_refs)
    )
    grid = jnp.concatenate([ref[lon : 2 * lon, :] for ref in row_refs], axis=0)
    wide = (grid.astype(jnp.float32) + projected).astype(jnp.bfloat16).astype(jnp.float32)
    normed = wide * lax.rsqrt(jnp.mean(wide * wide, axis=-1, keepdims=True) + 1e-06)
    return wide, normed


def around(parts, lon):
    return pltpu.roll(parts[0], 1, 0) + parts[1] + pltpu.roll(parts[2], lon - 1, 0)


def inner_kernel(
    lon, width, nblocks, rows,
    meta_ref, near_ref, near_sent_ref, far_sent_ref, same_ref, other_ref, upper_ref, lower_ref,
    conv_hbm, done_ref, partial_ref, keys_ref, conv_ref, mixed_ref, field_ref, sems,
):
    core = meta_ref[0]
    copies = [
        pltpu.make_async_copy(conv_hbm.at[source], conv_ref.at[i], sems.at[i])
        for i, source in enumerate((1, 2 - 2 * core, 2 * core))
    ]
    for copy in copies:
        copy.start()

    def keys_of(cols):
        keys = both_cores(same_ref, other_ref, cols).T
        keys_ref[cols, :] = keys
        return keys

    wide, normed = attend(
        lon, width, nblocks, rows, core, (near_ref, near_sent_ref, far_sent_ref), keys_of,
        same_ref, other_ref, (upper_ref, lower_ref), mixed_ref,
    )
    field_ref[...] = normed.astype(jnp.bfloat16)
    for copy in copies:
        copy.wait()
    inputs = jnp.concatenate([field_ref[lon:, :], field_ref[: 2 * lon, :]], axis=1)
    full, open_end = [], []
    for lon_off in range(3):
        taps = conv_ref[:2, lon_off].reshape(2 * width, width)
        term = jnp.dot(inputs, taps, preferred_element_type=jnp.float32)
        full.append(
            term[:lon]
            + jnp.dot(field_ref[2 * lon :, :], conv_ref[2, lon_off], preferred_element_type=jnp.float32)
        )
        open_end.append(term[lon:])
    done_ref[...] = (wide[lon : 2 * lon] + around(full, lon)).astype(jnp.bfloat16)
    partial_ref[...] = wide[2 * lon :] + around(open_end, lon)


def outer_kernel(
    lon, width, nblocks, rows,
    meta_ref, far_ref, same_ref, other_ref, upper_ref, lower_ref, done_ref, partial_ref, keys_ref,
    conv_hbm, out_ref, conv_ref, mixed_ref, sem,
):
    core = meta_ref[0]
    copy = pltpu.make_async_copy(conv_hbm.at[2 * core], conv_ref, sem)
    copy.start()
    _, normed = attend(
        lon, width, nblocks, rows, core, (far_ref,), lambda cols: keys_ref[cols, :],
        same_ref, other_ref, (upper_ref, lower_ref), mixed_ref,
    )
    field = jnp.where(meta_ref[1] > 0, normed, 0.0).astype(jnp.bfloat16)
    copy.wait()
    parts = [
        jnp.dot(field, conv_ref[lon_off], preferred_element_type=jnp.float32) for lon_off in range(3)
    ]
    last = (partial_ref[...] + around(parts, lon)).astype(jnp.bfloat16)
    out_ref[pl.ds(pl.multiple_of((1 - core) * lon, lon), lon), :] = done_ref[...]
    out_ref[pl.ds(pl.multiple_of(core * lon, lon), lon), :] = last


def on_device(
    grid_feat, queries, obs_keys, obs_values, block_mask, obs_valid, out_weight, conv_weight
):
    q_dev, width = queries.shape
    tiles, nblocks = block_mask.shape
    rows = obs_keys.shape[0]
    lon = q_dev // tiles
    obs = nblocks * OBS_BLOCK
    devices = lax.axis_size(AXES)
    pairs = devices // CORES
    me = lax.axis_index(AXES)
    core = me % CORES

    block = jnp.concatenate([obs_keys, obs_values], axis=1)
    groups = [list(range(c, devices, CORES)) for c in range(CORES)]
    same = lax.all_to_all(
        jnp.broadcast_to(block[None], (pairs,) + block.shape), AXES, 0, 0, axis_index_groups=groups
    )
    swap = [(i, i ^ 1) for i in range(devices)]
    across = [(i, i + 1) for i in range(1, devices - 1, CORES)]
    across += [(target, source) for source, target in across]

    query_rows, grid_rows = lax.optimization_barrier(
        (jnp.split(queries, tiles, axis=0), jnp.split(grid_feat, tiles, axis=0))
    )
    limits = jnp.where(block_mask > 0, obs_valid[None], 0).astype(jnp.bfloat16)
    limits = jnp.pad(limits, ((0, 0), (0, width - nblocks)))

    def packed(tile):
        limit = jnp.broadcast_to(limits[tile][None], (LIMIT_ROWS, width))
        return jnp.concatenate([query_rows[tile], grid_rows[tile], limit], axis=0)

    first, last = packed(0), packed(tiles - 1)
    far_sent = jnp.where(core == 0, first, last)
    near_sent = jnp.where(core == 0, last, first)
    far = lax.ppermute(far_sent, AXES, across)
    near = lax.ppermute(near_sent, AXES, swap)
    other = lax.ppermute(same, AXES, swap)
    out_weight, _ = lax.optimization_barrier((out_weight, same))
    upper, lower = lax.optimization_barrier(tuple(jnp.split(out_weight, 2, axis=0)))

    far_exists = (me > 0) & (me < devices - 1)
    meta = jnp.stack([core, far_exists.astype(core.dtype)]).astype(jnp.int32)

    vmem = pl.BlockSpec(memory_space=pltpu.VMEM)
    smem = pl.BlockSpec(memory_space=pltpu.SMEM)
    hbm = pl.BlockSpec(memory_space=pltpu.HBM)
    sizes = (lon, width, nblocks, rows)
    params = pltpu.CompilerParams(vmem_limit_bytes=48 * 2**20)
    tap_flops, row_flops = 2 * lon * width * width, 2 * lon * width * (width + 4 * obs)
    done, partial, keys = pl.pallas_call(
        functools.partial(inner_kernel, *sizes),
        out_shape=[
            jax.ShapeDtypeStruct((lon, width), jnp.bfloat16),
            jax.ShapeDtypeStruct((lon, width), jnp.float32),
            jax.ShapeDtypeStruct((width, obs), jnp.bfloat16),
        ],
        in_specs=[smem] + [vmem] * 7 + [hbm],
        out_specs=[vmem] * 3,
        scratch_shapes=[
            pltpu.VMEM(conv_weight.shape, jnp.bfloat16),
            pltpu.VMEM((3 * lon, width), jnp.bfloat16),
            pltpu.VMEM((3 * lon, width), jnp.bfloat16),
            pltpu.SemaphoreType.DMA((3,)),
        ],
        compiler_params=params,
        cost_estimate=pl.CostEstimate(
            flops=3 * row_flops + 15 * tap_flops, bytes_accessed=2 * conv_weight.size, transcendentals=0
        ),
        name="inner",
    )(meta, near, near_sent, far_sent, same, other, upper, lower, conv_weight)
    return pl.pallas_call(
        functools.partial(outer_kernel, *sizes),
        out_shape=jax.ShapeDtypeStruct((q_dev, width), jnp.bfloat16),
        in_specs=[smem] + [vmem] * 8 + [hbm],
        out_specs=vmem,
        scratch_shapes=[
            pltpu.VMEM(conv_weight.shape[1:], jnp.bfloat16),
            pltpu.VMEM((lon, width), jnp.bfloat16),
            pltpu.SemaphoreType.DMA,
        ],
        compiler_params=params,
        cost_estimate=pl.CostEstimate(
            flops=row_flops + 3 * tap_flops, bytes_accessed=conv_weight.size, transcendentals=0
        ),
        name="outer",
    )(meta, far, same, other, upper, lower, done, partial, keys, conv_weight)


def solution(mesh):
    in_specs = (
        P(AXES, None),
        P(AXES, None),
        P(AXES, None),
        P(AXES, None),
        P(AXES, None),
        P(),
        P(),
        P(),
    )
    return jax.shard_map(
        on_device, mesh=mesh, in_specs=in_specs, out_specs=P(AXES, None), check_vma=False
    )
```

```python
import functools
import math

import jax
import jax.numpy as jnp
from jax import lax
from jax.experimental import pallas as pl
from jax.experimental.pallas import tpu as pltpu
from jax.sharding import PartitionSpec as P

HEADS = 8
OBS_BLOCK = 128
AXES = ("blk", "tile")
PAIR = 2
CORES = 2
LIMIT_ROWS = 16


def both_cores(same_ref, other_ref, cols):
    return jnp.concatenate(
        [ref[:, :, cols].reshape(-1, cols.stop - cols.start) for ref in (same_ref, other_ref)], axis=0
    )


def attend(lon, width, nblocks, rows, core, row_refs, keys_of, same_ref, other_ref, weight_refs, mixed_ref):
    head = width // HEADS
    pair = PAIR * head
    obs = nblocks * OBS_BLOCK
    scale = head ** (-0.5) * math.log2(math.e)
    half = OBS_BLOCK // CORES
    key_lane = lax.broadcasted_iota(jnp.int32, (1, OBS_BLOCK), 1)
    spread = (key_lane % half) // rows * (CORES * rows) + key_lane % rows
    first = key_lane < half

    def row_bias(ref):
        limit = ref[2 * lon : 2 * lon + LIMIT_ROWS, :].astype(jnp.float32)[:1].astype(jnp.int32)

        parts = []
        for parity in (core, 1 - core):
            place = spread + parity * rows
            for block in range(0, nblocks, CORES):
                ends = [
                    jnp.broadcast_to(limit[:, b : b + 1], (1, OBS_BLOCK)) for b in (block, block + 1)
                ]
                end = jnp.where(first, ends[0], ends[1])
                parts.append(jnp.where(place < end, 0.0, -jnp.inf))
        return jnp.concatenate(parts, axis=1)

    biases = [row_bias(ref) for ref in row_refs]
    lane = lax.broadcasted_iota(jnp.int32, (obs, pair), 1)
    ones = [(lane // head == h).astype(jnp.bfloat16) for h in range(PAIR)]

    empty = jnp.zeros((head, obs), jnp.bfloat16)

    def columns(group):
        return slice(group * pair, (group + 1) * pair)

    def scores_of(group):
        keys = keys_of(columns(group))
        query = jnp.concatenate([ref[:lon, columns(group)] for ref in row_refs], axis=0)
        scores = []
        for h in range(PAIR):
            part = [keys[i * head : (i + 1) * head] if i == h else empty for i in range(PAIR)]
            part = jnp.concatenate(part, axis=0)
            scores.append(jnp.dot(query, part, preferred_element_type=jnp.float32))
        return scores

    def weights_of(scores):
        pieces = []
        for t, bias in enumerate(biases):
            piece = scores[t * lon : (t + 1) * lon] * scale + bias
            top = jnp.max(piece, axis=1, keepdims=True)
            pieces.append(jnp.exp2(piece - top).astype(jnp.bfloat16))
        return jnp.concatenate(pieces, axis=0)

    groups = HEADS // PAIR
    scores = [scores_of(group) for group in range(groups)]
    weights = [
        jnp.concatenate([weights_of(part) for part in scores[group]], axis=1) for group in range(groups)
    ]
    for group in range(groups):
        values = both_cores(same_ref, other_ref, columns(groups + group))
        value_parts = jnp.concatenate(
            [jnp.concatenate([values * one, one], axis=1) for one in ones], axis=0
        )
        both = jnp.dot(weights[group], value_parts, preferred_element_type=jnp.float32)
        mixed_ref[:, columns(group)] = (both[:, :pair] / both[:, pair:]).astype(jnp.bfloat16)

    depth = width // len(weight_refs)
    projected = sum(
        jnp.dot(
            mixed_ref[:, i * depth : (i + 1) * depth], ref[...], preferred_element_type=jnp.float32
        )
        for i, ref in enumerate(weight_refs)
    )
    grid = jnp.concatenate([ref[lon : 2 * lon, :] for ref in row_refs], axis=0)
    wide = (grid.astype(jnp.float32) + projected).astype(jnp.bfloat16).astype(jnp.float32)
    normed = wide * lax.rsqrt(jnp.mean(wide * wide, axis=-1, keepdims=True) + 1e-06)
    return wide, normed


def around(parts, lon):
    return pltpu.roll(parts[0], 1, 0) + parts[1] + pltpu.roll(parts[2], lon - 1, 0)


def inner_kernel(
    lon, width, nblocks, rows,
    meta_ref, near_ref, near_sent_ref, far_sent_ref, same_ref, other_ref, upper_ref, lower_ref,
    conv_hbm, done_ref, partial_ref, keys_ref, conv_ref, mixed_ref, field_ref, sems,
):
    core = meta_ref[0]
    copies = [
        pltpu.make_async_copy(conv_hbm.at[source], conv_ref.at[i], sems.at[i])
        for i, source in enumerate((1, 2 - 2 * core, 2 * core))
    ]
    for copy in copies:
        copy.start()

    def keys_of(cols):
        keys = both_cores(same_ref, other_ref, cols).T
        keys_ref[cols, :] = keys
        return keys

    wide, normed = attend(
        lon, width, nblocks, rows, core, (near_ref, near_sent_ref, far_sent_ref), keys_of,
        same_ref, other_ref, (upper_ref, lower_ref), mixed_ref,
    )
    field_ref[...] = normed.astype(jnp.bfloat16)
    copies[0].wait()
    copies[1].wait()
    inputs = jnp.concatenate([field_ref[lon:, :], field_ref[: 2 * lon, :]], axis=1)
    terms = [
        jnp.dot(
            inputs, conv_ref[:2, lon_off].reshape(2 * width, width), preferred_element_type=jnp.float32
        )
        for lon_off in range(3)
    ]
    copies[2].wait()
    full = [
        terms[lon_off][:lon]
        + jnp.dot(field_ref[2 * lon :, :], conv_ref[2, lon_off], preferred_element_type=jnp.float32)
        for lon_off in range(3)
    ]
    open_end = [term[lon:] for term in terms]
    done_ref[...] = (wide[lon : 2 * lon] + around(full, lon)).astype(jnp.bfloat16)
    partial_ref[...] = wide[2 * lon :] + around(open_end, lon)


def outer_kernel(
    lon, width, nblocks, rows,
    meta_ref, far_ref, same_ref, other_ref, upper_ref, lower_ref, done_ref, partial_ref, keys_ref,
    conv_hbm, out_ref, conv_ref, mixed_ref, sem,
):
    core = meta_ref[0]
    copy = pltpu.make_async_copy(conv_hbm.at[2 * core], conv_ref, sem)
    copy.start()
    _, normed = attend(
        lon, width, nblocks, rows, core, (far_ref,), lambda cols: keys_ref[cols, :],
        same_ref, other_ref, (upper_ref, lower_ref), mixed_ref,
    )
    field = jnp.where(meta_ref[1] > 0, normed, 0.0).astype(jnp.bfloat16)
    copy.wait()
    parts = [
        jnp.dot(field, conv_ref[lon_off], preferred_element_type=jnp.float32) for lon_off in range(3)
    ]
    last = (partial_ref[...] + around(parts, lon)).astype(jnp.bfloat16)
    out_ref[pl.ds(pl.multiple_of((1 - core) * lon, lon), lon), :] = done_ref[...]
    out_ref[pl.ds(pl.multiple_of(core * lon, lon), lon), :] = last


def on_device(
    grid_feat, queries, obs_keys, obs_values, block_mask, obs_valid, out_weight, conv_weight
):
    q_dev, width = queries.shape
    tiles, nblocks = block_mask.shape
    rows = obs_keys.shape[0]
    lon = q_dev // tiles
    obs = nblocks * OBS_BLOCK
    devices = lax.axis_size(AXES)
    pairs = devices // CORES
    me = lax.axis_index(AXES)
    core = me % CORES

    block = jnp.concatenate([obs_keys, obs_values], axis=1)
    groups = [list(range(c, devices, CORES)) for c in range(CORES)]
    same = lax.all_to_all(
        jnp.broadcast_to(block[None], (pairs,) + block.shape), AXES, 0, 0, axis_index_groups=groups
    )
    swap = [(i, i ^ 1) for i in range(devices)]
    across = [(i, i + 1) for i in range(1, devices - 1, CORES)]
    across += [(target, source) for source, target in across]

    query_rows, grid_rows = lax.optimization_barrier(
        (jnp.split(queries, tiles, axis=0), jnp.split(grid_feat, tiles, axis=0))
    )
    limits = jnp.where(block_mask > 0, obs_valid[None], 0).astype(jnp.bfloat16)
    limits = jnp.pad(limits, ((0, 0), (0, width - nblocks)))

    def packed(tile):
        limit = jnp.broadcast_to(limits[tile][None], (LIMIT_ROWS, width))
        return jnp.concatenate([query_rows[tile], grid_rows[tile], limit], axis=0)

    first, last = packed(0), packed(tiles - 1)
    far_sent = jnp.where(core == 0, first, last)
    near_sent = jnp.where(core == 0, last, first)
    far = lax.ppermute(far_sent, AXES, across)
    near = lax.ppermute(near_sent, AXES, swap)
    other = lax.ppermute(same, AXES, swap)
    out_weight, _ = lax.optimization_barrier((out_weight, same))
    upper, lower = lax.optimization_barrier(tuple(jnp.split(out_weight, 2, axis=0)))

    far_exists = (me > 0) & (me < devices - 1)
    meta = jnp.stack([core, far_exists.astype(core.dtype)]).astype(jnp.int32)

    vmem = pl.BlockSpec(memory_space=pltpu.VMEM)
    smem = pl.BlockSpec(memory_space=pltpu.SMEM)
    hbm = pl.BlockSpec(memory_space=pltpu.HBM)
    sizes = (lon, width, nblocks, rows)
    params = pltpu.CompilerParams(vmem_limit_bytes=48 * 2**20)
    tap_flops, row_flops = 2 * lon * width * width, 2 * lon * width * (width + 4 * obs)
    done, partial, keys = pl.pallas_call(
        functools.partial(inner_kernel, *sizes),
        out_shape=[
            jax.ShapeDtypeStruct((lon, width), jnp.bfloat16),
            jax.ShapeDtypeStruct((lon, width), jnp.float32),
            jax.ShapeDtypeStruct((width, obs), jnp.bfloat16),
        ],
        in_specs=[smem] + [vmem] * 7 + [hbm],
        out_specs=[vmem] * 3,
        scratch_shapes=[
            pltpu.VMEM(conv_weight.shape, jnp.bfloat16),
            pltpu.VMEM((3 * lon, width), jnp.bfloat16),
            pltpu.VMEM((3 * lon, width), jnp.bfloat16),
            pltpu.SemaphoreType.DMA((3,)),
        ],
        compiler_params=params,
        cost_estimate=pl.CostEstimate(
            flops=3 * row_flops + 15 * tap_flops, bytes_accessed=2 * conv_weight.size, transcendentals=0
        ),
        name="inner",
    )(meta, near, near_sent, far_sent, same, other, upper, lower, conv_weight)
    return pl.pallas_call(
        functools.partial(outer_kernel, *sizes),
        out_shape=jax.ShapeDtypeStruct((q_dev, width), jnp.bfloat16),
        in_specs=[smem] + [vmem] * 8 + [hbm],
        out_specs=vmem,
        scratch_shapes=[
            pltpu.VMEM(conv_weight.shape[1:], jnp.bfloat16),
            pltpu.VMEM((lon, width), jnp.bfloat16),
            pltpu.SemaphoreType.DMA,
        ],
        compiler_params=params,
        cost_estimate=pl.CostEstimate(
            flops=row_flops + 3 * tap_flops, bytes_accessed=conv_weight.size, transcendentals=0
        ),
        name="outer",
    )(meta, far, same, other, upper, lower, done, partial, keys, conv_weight)


def solution(mesh):
    in_specs = (
        P(AXES, None),
        P(AXES, None),
        P(AXES, None),
        P(AXES, None),
        P(AXES, None),
        P(),
        P(),
        P(),
    )
    return jax.shard_map(
        on_device, mesh=mesh, in_specs=in_specs, out_specs=P(AXES, None), check_vma=False
    )
```

```python
import functools
import math

import jax
import jax.numpy as jnp
from jax import lax
from jax.experimental import pallas as pl
from jax.experimental.pallas import tpu as pltpu
from jax.sharding import PartitionSpec as P

HEADS = 8
OBS_BLOCK = 128
AXES = ("blk", "tile")
PAIR = 2
CORES = 2
LIMIT_ROWS = 16


def both_cores(same_ref, other_ref, cols):
    return jnp.concatenate(
        [ref[:, :, cols].reshape(-1, cols.stop - cols.start) for ref in (same_ref, other_ref)], axis=0
    )


def attend(lon, width, nblocks, rows, core, row_refs, keys_of, same_ref, other_ref, weight_refs, mixed_ref):
    head = width // HEADS
    pair = PAIR * head
    obs = nblocks * OBS_BLOCK
    scale = head ** (-0.5) * math.log2(math.e)
    half = OBS_BLOCK // CORES
    key_lane = lax.broadcasted_iota(jnp.int32, (1, OBS_BLOCK), 1)
    spread = (key_lane % half) // rows * (CORES * rows) + key_lane % rows
    first = key_lane < half

    def row_bias(ref):
        limit = ref[2 * lon : 2 * lon + LIMIT_ROWS, :].astype(jnp.float32)[:1].astype(jnp.int32)

        parts = []
        for parity in (core, 1 - core):
            place = spread + parity * rows
            for block in range(0, nblocks, CORES):
                ends = [
                    jnp.broadcast_to(limit[:, b : b + 1], (1, OBS_BLOCK)) for b in (block, block + 1)
                ]
                end = jnp.where(first, ends[0], ends[1])
                parts.append(jnp.where(place < end, 0.0, -jnp.inf))
        return jnp.concatenate(parts, axis=1)

    biases = [row_bias(ref) for ref in row_refs]
    lane = lax.broadcasted_iota(jnp.int32, (obs, pair), 1)
    ones = [(lane // head == h).astype(jnp.bfloat16) for h in range(PAIR)]

    empty = jnp.zeros((head, obs), jnp.bfloat16)

    def columns(group):
        return slice(group * pair, (group + 1) * pair)

    def scores_of(group):
        keys = keys_of(columns(group))
        query = jnp.concatenate([ref[:lon, columns(group)] for ref in row_refs], axis=0)
        scores = []
        for h in range(PAIR):
            part = [keys[i * head : (i + 1) * head] if i == h else empty for i in range(PAIR)]
            part = jnp.concatenate(part, axis=0)
            scores.append(jnp.dot(query, part, preferred_element_type=jnp.float32))
        return scores

    def weights_of(scores):
        pieces = []
        for t, bias in enumerate(biases):
            piece = scores[t * lon : (t + 1) * lon] * scale + bias
            top = jnp.max(piece.astype(jnp.bfloat16), axis=1, keepdims=True).astype(jnp.float32)
            pieces.append(jnp.exp2(piece - top).astype(jnp.bfloat16))
        return jnp.concatenate(pieces, axis=0)

    groups = HEADS // PAIR
    scores = [scores_of(group) for group in range(groups)]
    weights = [
        jnp.concatenate([weights_of(part) for part in scores[group]], axis=1) for group in range(groups)
    ]
    for group in range(groups):
        values = both_cores(same_ref, other_ref, columns(groups + group))
        value_parts = jnp.concatenate(
            [jnp.concatenate([values * one, one], axis=1) for one in ones], axis=0
        )
        both = jnp.dot(weights[group], value_parts, preferred_element_type=jnp.float32)
        mixed_ref[:, columns(group)] = (both[:, :pair] / both[:, pair:]).astype(jnp.bfloat16)

    depth = width // len(weight_refs)
    projected = sum(
        jnp.dot(
            mixed_ref[:, i * depth : (i + 1) * depth], ref[...], preferred_element_type=jnp.float32
        )
        for i, ref in enumerate(weight_refs)
    )
    grid = jnp.concatenate([ref[lon : 2 * lon, :] for ref in row_refs], axis=0)
    wide = (grid.astype(jnp.float32) + projected).astype(jnp.bfloat16).astype(jnp.float32)
    normed = wide * lax.rsqrt(jnp.mean(wide * wide, axis=-1, keepdims=True) + 1e-06)
    return wide, normed


def around(parts, lon):
    return pltpu.roll(parts[0], 1, 0) + parts[1] + pltpu.roll(parts[2], lon - 1, 0)


def inner_kernel(
    lon, width, nblocks, rows,
    meta_ref, near_ref, near_sent_ref, far_sent_ref, same_ref, other_ref, upper_ref, lower_ref,
    conv_hbm, done_ref, partial_ref, keys_ref, conv_ref, mixed_ref, field_ref, sems,
):
    core = meta_ref[0]
    copies = [
        pltpu.make_async_copy(
            conv_hbm.at[source, lon_off], conv_ref.at[i, lon_off], sems.at[3 * lon_off + i]
        )
        for lon_off in range(3)
        for i, source in enumerate((1, 2 - 2 * core, 2 * core))
    ]
    for copy in copies:
        copy.start()

    def keys_of(cols):
        keys = both_cores(same_ref, other_ref, cols).T
        keys_ref[cols, :] = keys
        return keys

    wide, normed = attend(
        lon, width, nblocks, rows, core, (near_ref, near_sent_ref, far_sent_ref), keys_of,
        same_ref, other_ref, (upper_ref, lower_ref), mixed_ref,
    )
    field_ref[...] = normed.astype(jnp.bfloat16)
    inputs = jnp.concatenate([field_ref[lon:, :], field_ref[: 2 * lon, :]], axis=1)
    full, open_end = [], []
    for lon_off in range(3):
        for copy in copies[3 * lon_off : 3 * lon_off + 3]:
            copy.wait()
        taps = conv_ref[:2, lon_off].reshape(2 * width, width)
        term = jnp.dot(inputs, taps, preferred_element_type=jnp.float32)
        full.append(
            term[:lon]
            + jnp.dot(field_ref[2 * lon :, :], conv_ref[2, lon_off], preferred_element_type=jnp.float32)
        )
        open_end.append(term[lon:])
    done_ref[...] = (wide[lon : 2 * lon] + around(full, lon)).astype(jnp.bfloat16)
    partial_ref[...] = wide[2 * lon :] + around(open_end, lon)


def outer_kernel(
    lon, width, nblocks, rows,
    meta_ref, far_ref, same_ref, other_ref, upper_ref, lower_ref, done_ref, partial_ref, keys_ref,
    conv_hbm, out_ref, conv_ref, mixed_ref, sem,
):
    core = meta_ref[0]
    copy = pltpu.make_async_copy(conv_hbm.at[2 * core], conv_ref, sem)
    copy.start()
    _, normed = attend(
        lon, width, nblocks, rows, core, (far_ref,), lambda cols: keys_ref[cols, :],
        same_ref, other_ref, (upper_ref, lower_ref), mixed_ref,
    )
    field = jnp.where(meta_ref[1] > 0, normed, 0.0).astype(jnp.bfloat16)
    copy.wait()
    parts = [
        jnp.dot(field, conv_ref[lon_off], preferred_element_type=jnp.float32) for lon_off in range(3)
    ]
    last = (partial_ref[...] + around(parts, lon)).astype(jnp.bfloat16)
    out_ref[pl.ds(pl.multiple_of((1 - core) * lon, lon), lon), :] = done_ref[...]
    out_ref[pl.ds(pl.multiple_of(core * lon, lon), lon), :] = last


def on_device(
    grid_feat, queries, obs_keys, obs_values, block_mask, obs_valid, out_weight, conv_weight
):
    q_dev, width = queries.shape
    tiles, nblocks = block_mask.shape
    rows = obs_keys.shape[0]
    lon = q_dev // tiles
    obs = nblocks * OBS_BLOCK
    devices = lax.axis_size(AXES)
    pairs = devices // CORES
    me = lax.axis_index(AXES)
    core = me % CORES

    block = jnp.concatenate([obs_keys, obs_values], axis=1)
    groups = [list(range(c, devices, CORES)) for c in range(CORES)]
    same = lax.all_to_all(
        jnp.broadcast_to(block[None], (pairs,) + block.shape), AXES, 0, 0, axis_index_groups=groups
    )
    swap = [(i, i ^ 1) for i in range(devices)]
    across = [(i, i + 1) for i in range(1, devices - 1, CORES)]
    across += [(target, source) for source, target in across]

    query_rows, grid_rows = lax.optimization_barrier(
        (jnp.split(queries, tiles, axis=0), jnp.split(grid_feat, tiles, axis=0))
    )
    limits = jnp.where(block_mask > 0, obs_valid[None], 0).astype(jnp.bfloat16)
    limits = jnp.pad(limits, ((0, 0), (0, width - nblocks)))

    def packed(tile):
        limit = jnp.broadcast_to(limits[tile][None], (LIMIT_ROWS, width))
        return jnp.concatenate([query_rows[tile], grid_rows[tile], limit], axis=0)

    first, last = packed(0), packed(tiles - 1)
    far_sent = jnp.where(core == 0, first, last)
    near_sent = jnp.where(core == 0, last, first)
    far = lax.ppermute(far_sent, AXES, across)
    near = lax.ppermute(near_sent, AXES, swap)
    other = lax.ppermute(same, AXES, swap)
    out_weight, _ = lax.optimization_barrier((out_weight, same))
    upper, lower = lax.optimization_barrier(tuple(jnp.split(out_weight, 2, axis=0)))

    far_exists = (me > 0) & (me < devices - 1)
    meta = jnp.stack([core, far_exists.astype(core.dtype)]).astype(jnp.int32)

    vmem = pl.BlockSpec(memory_space=pltpu.VMEM)
    smem = pl.BlockSpec(memory_space=pltpu.SMEM)
    hbm = pl.BlockSpec(memory_space=pltpu.HBM)
    sizes = (lon, width, nblocks, rows)
    params = pltpu.CompilerParams(vmem_limit_bytes=48 * 2**20)
    tap_flops, row_flops = 2 * lon * width * width, 2 * lon * width * (width + 4 * obs)
    done, partial, keys = pl.pallas_call(
        functools.partial(inner_kernel, *sizes),
        out_shape=[
            jax.ShapeDtypeStruct((lon, width), jnp.bfloat16),
            jax.ShapeDtypeStruct((lon, width), jnp.float32),
            jax.ShapeDtypeStruct((width, obs), jnp.bfloat16),
        ],
        in_specs=[smem] + [vmem] * 7 + [hbm],
        out_specs=[vmem] * 3,
        scratch_shapes=[
            pltpu.VMEM(conv_weight.shape, jnp.bfloat16),
            pltpu.VMEM((3 * lon, width), jnp.bfloat16),
            pltpu.VMEM((3 * lon, width), jnp.bfloat16),
            pltpu.SemaphoreType.DMA((9,)),
        ],
        compiler_params=params,
        cost_estimate=pl.CostEstimate(
            flops=3 * row_flops + 15 * tap_flops, bytes_accessed=2 * conv_weight.size, transcendentals=0
        ),
        name="inner",
    )(meta, near, near_sent, far_sent, same, other, upper, lower, conv_weight)
    return pl.pallas_call(
        functools.partial(outer_kernel, *sizes),
        out_shape=jax.ShapeDtypeStruct((q_dev, width), jnp.bfloat16),
        in_specs=[smem] + [vmem] * 8 + [hbm],
        out_specs=vmem,
        scratch_shapes=[
            pltpu.VMEM(conv_weight.shape[1:], jnp.bfloat16),
            pltpu.VMEM((lon, width), jnp.bfloat16),
            pltpu.SemaphoreType.DMA,
        ],
        compiler_params=params,
        cost_estimate=pl.CostEstimate(
            flops=row_flops + 3 * tap_flops, bytes_accessed=conv_weight.size, transcendentals=0
        ),
        name="outer",
    )(meta, far, same, other, upper, lower, done, partial, keys, conv_weight)


def solution(mesh):
    in_specs = (
        P(AXES, None),
        P(AXES, None),
        P(AXES, None),
        P(AXES, None),
        P(AXES, None),
        P(),
        P(),
        P(),
    )
    return jax.shard_map(
        on_device, mesh=mesh, in_specs=in_specs, out_specs=P(AXES, None), check_vma=False
    )
```

```python
import functools
import math

import jax
import jax.numpy as jnp
from jax import lax
from jax.experimental import pallas as pl
from jax.experimental.pallas import tpu as pltpu
from jax.sharding import PartitionSpec as P

HEADS = 8
OBS_BLOCK = 128
AXES = ("blk", "tile")
PAIR = 2
CORES = 2
LIMIT_ROWS = 16


def both_cores(same_ref, other_ref, cols):
    return jnp.concatenate(
        [ref[:, :, cols].reshape(-1, cols.stop - cols.start) for ref in (same_ref, other_ref)], axis=0
    )


def attend(lon, width, nblocks, rows, core, row_refs, keys_of, same_ref, other_ref, weight_refs, mixed_ref):
    head = width // HEADS
    pair = PAIR * head
    obs = nblocks * OBS_BLOCK
    scale = head ** (-0.5) * math.log2(math.e)
    half = OBS_BLOCK // CORES
    key_lane = lax.broadcasted_iota(jnp.int32, (1, OBS_BLOCK), 1)
    spread = (key_lane % half) // rows * (CORES * rows) + key_lane % rows
    first = key_lane < half

    def row_bias(ref):
        limit = ref[2 * lon : 2 * lon + LIMIT_ROWS, :].astype(jnp.float32)[:1].astype(jnp.int32)

        parts = []
        for parity in (core, 1 - core):
            place = spread + parity * rows
            for block in range(0, nblocks, CORES):
                ends = [
                    jnp.broadcast_to(limit[:, b : b + 1], (1, OBS_BLOCK)) for b in (block, block + 1)
                ]
                end = jnp.where(first, ends[0], ends[1])
                parts.append(jnp.where(place < end, 0.0, -jnp.inf))
        return jnp.concatenate(parts, axis=1)

    biases = [row_bias(ref) for ref in row_refs]
    lane = lax.broadcasted_iota(jnp.int32, (obs, pair), 1)
    ones = [(lane // head == h).astype(jnp.bfloat16) for h in range(PAIR)]

    empty = jnp.zeros((head, obs), jnp.bfloat16)

    def columns(group):
        return slice(group * pair, (group + 1) * pair)

    def scores_of(group):
        keys = keys_of(columns(group))
        query = jnp.concatenate([ref[:lon, columns(group)] for ref in row_refs], axis=0)
        scores = []
        for h in range(PAIR):
            part = [keys[i * head : (i + 1) * head] if i == h else empty for i in range(PAIR)]
            part = jnp.concatenate(part, axis=0)
            scores.append(jnp.dot(query, part, preferred_element_type=jnp.float32))
        return scores

    def weights_of(scores):
        pieces = []
        for t, bias in enumerate(biases):
            piece = scores[t * lon : (t + 1) * lon] * scale + bias
            top = jnp.max(piece, axis=1, keepdims=True)
            pieces.append(jnp.exp2(piece - top).astype(jnp.bfloat16))
        return jnp.concatenate(pieces, axis=0)

    groups = HEADS // PAIR
    scores = [scores_of(group) for group in range(groups)]
    weights = [
        jnp.concatenate([weights_of(part) for part in scores[group]], axis=1) for group in range(groups)
    ]
    for group in range(groups):
        values = both_cores(same_ref, other_ref, columns(groups + group))
        value_parts = jnp.concatenate(
            [jnp.concatenate([values * one, one], axis=1) for one in ones], axis=0
        )
        both = jnp.dot(weights[group], value_parts, preferred_element_type=jnp.float32)
        mixed_ref[:, columns(group)] = (both[:, :pair] / both[:, pair:]).astype(jnp.bfloat16)

    depth = width // len(weight_refs)
    projected = sum(
        jnp.dot(
            mixed_ref[:, i * depth : (i + 1) * depth], ref[...], preferred_element_type=jnp.float32
        )
        for i, ref in enumerate(weight_refs)
    )
    grid = jnp.concatenate([ref[lon : 2 * lon, :] for ref in row_refs], axis=0)
    wide = (grid.astype(jnp.float32) + projected).astype(jnp.bfloat16).astype(jnp.float32)
    normed = wide * lax.rsqrt(jnp.mean(wide * wide, axis=-1, keepdims=True) + 1e-06)
    return wide, normed


def around(parts, lon):
    return pltpu.roll(parts[0], 1, 0) + parts[1] + pltpu.roll(parts[2], lon - 1, 0)


def inner_kernel(
    lon, width, nblocks, rows,
    meta_ref, near_ref, near_sent_ref, far_sent_ref, same_ref, other_ref, upper_ref, lower_ref,
    conv_hbm, edge_ref, partial_ref, keys_ref, conv_ref, mixed_ref, field_ref, sems,
):
    core = meta_ref[0]
    copies = [
        pltpu.make_async_copy(
            conv_hbm.at[source, lon_off], conv_ref.at[i, lon_off], sems.at[2 * lon_off + i]
        )
        for lon_off in range(3)
        for i, source in enumerate((1, 2 - 2 * core))
    ]
    for copy in copies:
        copy.start()

    def keys_of(cols):
        keys = both_cores(same_ref, other_ref, cols).T
        keys_ref[cols, :] = keys
        return keys

    wide, normed = attend(
        lon, width, nblocks, rows, core, (near_ref, near_sent_ref, far_sent_ref), keys_of,
        same_ref, other_ref, (upper_ref, lower_ref), mixed_ref,
    )
    field_ref[...] = normed.astype(jnp.bfloat16)
    edge_ref[...] = field_ref[2 * lon :, :]
    inputs = jnp.concatenate([field_ref[lon:, :], field_ref[: 2 * lon, :]], axis=1)
    terms = []
    for lon_off in range(3):
        for copy in copies[2 * lon_off : 2 * lon_off + 2]:
            copy.wait()
        taps = conv_ref[:, lon_off].reshape(2 * width, width)
        terms.append(jnp.dot(inputs, taps, preferred_element_type=jnp.float32))
    for start in (0, lon):
        here = slice(start, start + lon)
        shifted = around([term[here] for term in terms], lon)
        partial_ref[here, :] = wide[start + lon : start + 2 * lon] + shifted


def outer_kernel(
    lon, width, nblocks, rows,
    meta_ref, far_ref, same_ref, other_ref, upper_ref, lower_ref, edge_ref, partial_ref, keys_ref,
    conv_hbm, out_ref, conv_ref, mixed_ref, sem,
):
    core = meta_ref[0]
    copy = pltpu.make_async_copy(conv_hbm.at[2 * core], conv_ref, sem)
    copy.start()
    _, normed = attend(
        lon, width, nblocks, rows, core, (far_ref,), lambda cols: keys_ref[cols, :],
        same_ref, other_ref, (upper_ref, lower_ref), mixed_ref,
    )
    far = jnp.where(meta_ref[1] > 0, normed, 0.0).astype(jnp.bfloat16)
    field = jnp.concatenate([edge_ref[...], far], axis=0)
    copy.wait()
    terms = [
        jnp.dot(field, conv_ref[lon_off], preferred_element_type=jnp.float32) for lon_off in range(3)
    ]
    for start, tile in ((0, 1 - core), (lon, core)):
        here = slice(start, start + lon)
        total = partial_ref[here, :] + around([term[here] for term in terms], lon)
        out_ref[pl.ds(pl.multiple_of(tile * lon, lon), lon), :] = total.astype(jnp.bfloat16)


def on_device(
    grid_feat, queries, obs_keys, obs_values, block_mask, obs_valid, out_weight, conv_weight
):
    q_dev, width = queries.shape
    tiles, nblocks = block_mask.shape
    rows = obs_keys.shape[0]
    lon = q_dev // tiles
    obs = nblocks * OBS_BLOCK
    devices = lax.axis_size(AXES)
    pairs = devices // CORES
    me = lax.axis_index(AXES)
    core = me % CORES

    block = jnp.concatenate([obs_keys, obs_values], axis=1)
    groups = [list(range(c, devices, CORES)) for c in range(CORES)]
    same = lax.all_to_all(
        jnp.broadcast_to(block[None], (pairs,) + block.shape), AXES, 0, 0, axis_index_groups=groups
    )
    swap = [(i, i ^ 1) for i in range(devices)]
    across = [(i, i + 1) for i in range(1, devices - 1, CORES)]
    across += [(target, source) for source, target in across]

    query_rows, grid_rows = lax.optimization_barrier(
        (jnp.split(queries, tiles, axis=0), jnp.split(grid_feat, tiles, axis=0))
    )
    limits = jnp.where(block_mask > 0, obs_valid[None], 0).astype(jnp.bfloat16)
    limits = jnp.pad(limits, ((0, 0), (0, width - nblocks)))

    def packed(tile):
        limit = jnp.broadcast_to(limits[tile][None], (LIMIT_ROWS, width))
        return jnp.concatenate([query_rows[tile], grid_rows[tile], limit], axis=0)

    first, last = packed(0), packed(tiles - 1)
    far_sent = jnp.where(core == 0, first, last)
    near_sent = jnp.where(core == 0, last, first)
    far = lax.ppermute(far_sent, AXES, across)
    near = lax.ppermute(near_sent, AXES, swap)
    other = lax.ppermute(same, AXES, swap)
    out_weight, _ = lax.optimization_barrier((out_weight, same))
    upper, lower = lax.optimization_barrier(tuple(jnp.split(out_weight, 2, axis=0)))

    far_exists = (me > 0) & (me < devices - 1)
    meta = jnp.stack([core, far_exists.astype(core.dtype)]).astype(jnp.int32)

    vmem = pl.BlockSpec(memory_space=pltpu.VMEM)
    smem = pl.BlockSpec(memory_space=pltpu.SMEM)
    hbm = pl.BlockSpec(memory_space=pltpu.HBM)
    sizes = (lon, width, nblocks, rows)
    params = pltpu.CompilerParams(vmem_limit_bytes=48 * 2**20)
    tap_flops, row_flops = 2 * lon * width * width, 2 * lon * width * (width + 4 * obs)
    edge, partial, keys = pl.pallas_call(
        functools.partial(inner_kernel, *sizes),
        out_shape=[
            jax.ShapeDtypeStruct((lon, width), jnp.bfloat16),
            jax.ShapeDtypeStruct((q_dev, width), jnp.float32),
            jax.ShapeDtypeStruct((width, obs), jnp.bfloat16),
        ],
        in_specs=[smem] + [vmem] * 7 + [hbm],
        out_specs=[vmem] * 3,
        scratch_shapes=[
            pltpu.VMEM((2,) + conv_weight.shape[1:], jnp.bfloat16),
            pltpu.VMEM((3 * lon, width), jnp.bfloat16),
            pltpu.VMEM((3 * lon, width), jnp.bfloat16),
            pltpu.SemaphoreType.DMA((6,)),
        ],
        compiler_params=params,
        cost_estimate=pl.CostEstimate(
            flops=3 * row_flops + 12 * tap_flops, bytes_accessed=2 * conv_weight.size, transcendentals=0
        ),
        name="inner",
    )(meta, near, near_sent, far_sent, same, other, upper, lower, conv_weight)
    return pl.pallas_call(
        functools.partial(outer_kernel, *sizes),
        out_shape=jax.ShapeDtypeStruct((q_dev, width), jnp.bfloat16),
        in_specs=[smem] + [vmem] * 8 + [hbm],
        out_specs=vmem,
        scratch_shapes=[
            pltpu.VMEM(conv_weight.shape[1:], jnp.bfloat16),
            pltpu.VMEM((lon, width), jnp.bfloat16),
            pltpu.SemaphoreType.DMA,
        ],
        compiler_params=params,
        cost_estimate=pl.CostEstimate(
            flops=row_flops + 6 * tap_flops, bytes_accessed=conv_weight.size, transcendentals=0
        ),
        name="outer",
    )(meta, far, same, other, upper, lower, edge, partial, keys, conv_weight)


def solution(mesh):
    in_specs = (
        P(AXES, None),
        P(AXES, None),
        P(AXES, None),
        P(AXES, None),
        P(AXES, None),
        P(),
        P(),
        P(),
    )
    return jax.shard_map(
        on_device, mesh=mesh, in_specs=in_specs, out_specs=P(AXES, None), check_vma=False
    )
```

```python
import functools
import math

import jax
import jax.numpy as jnp
from jax import lax
from jax.experimental import pallas as pl
from jax.experimental.pallas import tpu as pltpu
from jax.sharding import PartitionSpec as P

HEADS = 8
OBS_BLOCK = 128
AXES = ("blk", "tile")
PAIR = 2
CORES = 2
LIMIT_ROWS = 16


def both_cores(same_ref, other_ref, kind, cols):
    return jnp.concatenate(
        [ref[:, kind, :, cols].reshape(-1, cols.stop - cols.start) for ref in (same_ref, other_ref)],
        axis=0,
    )


def attend(lon, width, nblocks, rows, core, row_refs, keys_of, same_ref, other_ref, weight_refs, mixed_ref):
    head = width // HEADS
    pair = PAIR * head
    obs = nblocks * OBS_BLOCK
    scale = head ** (-0.5) * math.log2(math.e)
    half = OBS_BLOCK // CORES
    key_lane = lax.broadcasted_iota(jnp.int32, (1, OBS_BLOCK), 1)
    spread = (key_lane % half) // rows * (CORES * rows) + key_lane % rows
    first = key_lane < half

    def row_bias(ref):
        limit = ref[2 * lon : 2 * lon + LIMIT_ROWS, :].astype(jnp.float32)[:1].astype(jnp.int32)

        parts = []
        for parity in (core, 1 - core):
            place = spread + parity * rows
            for block in range(0, nblocks, CORES):
                ends = [
                    jnp.broadcast_to(limit[:, b : b + 1], (1, OBS_BLOCK)) for b in (block, block + 1)
                ]
                end = jnp.where(first, ends[0], ends[1])
                parts.append(jnp.where(place < end, 0.0, -jnp.inf))
        return jnp.concatenate(parts, axis=1)

    biases = [row_bias(ref) for ref in row_refs]
    lane = lax.broadcasted_iota(jnp.int32, (obs, pair), 1)
    ones = [(lane // head == h).astype(jnp.bfloat16) for h in range(PAIR)]

    empty = jnp.zeros((head, obs), jnp.bfloat16)

    def columns(group):
        return slice(group * pair, (group + 1) * pair)

    def scores_of(group):
        keys = keys_of(columns(group))
        query = jnp.concatenate([ref[:lon, columns(group)] for ref in row_refs], axis=0)
        scores = []
        for h in range(PAIR):
            part = [keys[i * head : (i + 1) * head] if i == h else empty for i in range(PAIR)]
            part = jnp.concatenate(part, axis=0)
            scores.append(jnp.dot(query, part, preferred_element_type=jnp.float32))
        return scores

    def weights_of(scores):
        pieces = []
        for t, bias in enumerate(biases):
            piece = scores[t * lon : (t + 1) * lon] * scale + bias
            top = jnp.max(piece, axis=1, keepdims=True)
            pieces.append(jnp.exp2(piece - top).astype(jnp.bfloat16))
        return jnp.concatenate(pieces, axis=0)

    groups = HEADS // PAIR
    scores = [scores_of(group) for group in range(groups)]
    weights = [
        jnp.concatenate([weights_of(part) for part in scores[group]], axis=1) for group in range(groups)
    ]
    for group in range(groups):
        values = both_cores(same_ref, other_ref, 1, columns(group))
        value_parts = jnp.concatenate(
            [jnp.concatenate([values * one, one], axis=1) for one in ones], axis=0
        )
        both = jnp.dot(weights[group], value_parts, preferred_element_type=jnp.float32)
        mixed_ref[:, columns(group)] = (both[:, :pair] / both[:, pair:]).astype(jnp.bfloat16)

    depth = width // len(weight_refs)
    projected = sum(
        jnp.dot(
            mixed_ref[:, i * depth : (i + 1) * depth], ref[...], preferred_element_type=jnp.float32
        )
        for i, ref in enumerate(weight_refs)
    )
    grid = jnp.concatenate([ref[lon : 2 * lon, :] for ref in row_refs], axis=0)
    wide = (grid.astype(jnp.float32) + projected).astype(jnp.bfloat16).astype(jnp.float32)
    normed = wide * lax.rsqrt(jnp.mean(wide * wide, axis=-1, keepdims=True) + 1e-06)
    return wide, normed


def around(parts, lon):
    return pltpu.roll(parts[0], 1, 0) + parts[1] + pltpu.roll(parts[2], lon - 1, 0)


def inner_kernel(
    lon, width, nblocks, rows,
    meta_ref, near_ref, near_sent_ref, far_sent_ref, same_ref, other_ref, upper_ref, lower_ref,
    conv_hbm, edge_ref, partial_ref, keys_ref, last_ref, conv_ref, mixed_ref, field_ref, sems,
):
    core = meta_ref[0]
    copies = [
        pltpu.make_async_copy(
            conv_hbm.at[source, lon_off], conv_ref.at[i, lon_off], sems.at[2 * lon_off + i]
        )
        for lon_off in range(3)
        for i, source in enumerate((1, 2 - 2 * core))
    ]
    copies.append(pltpu.make_async_copy(conv_hbm.at[2 * core], last_ref, sems.at[6]))
    for copy in copies:
        copy.start()

    def keys_of(cols):
        keys = both_cores(same_ref, other_ref, 0, cols).T
        keys_ref[cols, :] = keys
        return keys

    wide, normed = attend(
        lon, width, nblocks, rows, core, (near_ref, near_sent_ref, far_sent_ref), keys_of,
        same_ref, other_ref, (upper_ref, lower_ref), mixed_ref,
    )
    field_ref[...] = normed.astype(jnp.bfloat16)
    edge_ref[...] = field_ref[2 * lon :, :]
    inputs = jnp.concatenate([field_ref[lon:, :], field_ref[: 2 * lon, :]], axis=1)
    terms = []
    for lon_off in range(3):
        for copy in copies[2 * lon_off : 2 * lon_off + 2]:
            copy.wait()
        taps = conv_ref[:, lon_off].reshape(2 * width, width)
        terms.append(jnp.dot(inputs, taps, preferred_element_type=jnp.float32))
    for start in (0, lon):
        here = slice(start, start + lon)
        shifted = around([term[here] for term in terms], lon)
        partial_ref[here, :] = wide[start + lon : start + 2 * lon] + shifted
    copies[6].wait()


def outer_kernel(
    lon, width, nblocks, rows,
    meta_ref, far_ref, same_ref, other_ref, upper_ref, lower_ref, edge_ref, partial_ref, keys_ref,
    conv_ref, out_ref, mixed_ref,
):
    core = meta_ref[0]
    _, normed = attend(
        lon, width, nblocks, rows, core, (far_ref,), lambda cols: keys_ref[cols, :],
        same_ref, other_ref, (upper_ref, lower_ref), mixed_ref,
    )
    far = jnp.where(meta_ref[1] > 0, normed, 0.0).astype(jnp.bfloat16)
    field = jnp.concatenate([edge_ref[...], far], axis=0)
    terms = [
        jnp.dot(field, conv_ref[lon_off], preferred_element_type=jnp.float32) for lon_off in range(3)
    ]
    for start, tile in ((0, 1 - core), (lon, core)):
        here = slice(start, start + lon)
        total = partial_ref[here, :] + around([term[here] for term in terms], lon)
        out_ref[pl.ds(pl.multiple_of(tile * lon, lon), lon), :] = total.astype(jnp.bfloat16)


def on_device(
    grid_feat, queries, obs_keys, obs_values, block_mask, obs_valid, out_weight, conv_weight
):
    q_dev, width = queries.shape
    tiles, nblocks = block_mask.shape
    rows = obs_keys.shape[0]
    lon = q_dev // tiles
    obs = nblocks * OBS_BLOCK
    devices = lax.axis_size(AXES)
    pairs = devices // CORES
    me = lax.axis_index(AXES)
    core = me % CORES

    groups = [list(range(c, devices, CORES)) for c in range(CORES)]
    shape = (pairs, 2) + obs_keys.shape
    is_key = lax.broadcasted_iota(jnp.int32, shape, 1) == 0
    blocks = jnp.where(is_key, obs_keys[None, None], obs_values[None, None])
    same = lax.all_to_all(blocks, AXES, 0, 0, axis_index_groups=groups)
    swap = [(i, i ^ 1) for i in range(devices)]
    across = [(i, i + 1) for i in range(1, devices - 1, CORES)]
    across += [(target, source) for source, target in across]

    query_rows, grid_rows = lax.optimization_barrier(
        (jnp.split(queries, tiles, axis=0), jnp.split(grid_feat, tiles, axis=0))
    )
    limits = jnp.where(block_mask > 0, obs_valid[None], 0).astype(jnp.bfloat16)
    limits = jnp.pad(limits, ((0, 0), (0, width - nblocks)))

    def packed(tile):
        limit = jnp.broadcast_to(limits[tile][None], (LIMIT_ROWS, width))
        return jnp.concatenate([query_rows[tile], grid_rows[tile], limit], axis=0)

    first, last = packed(0), packed(tiles - 1)
    far_sent = jnp.where(core == 0, first, last)
    near_sent = jnp.where(core == 0, last, first)
    far = lax.ppermute(far_sent, AXES, across)
    near = lax.ppermute(near_sent, AXES, swap)
    other = lax.ppermute(same, AXES, swap)
    out_weight, _ = lax.optimization_barrier((out_weight, same))
    upper, lower = lax.optimization_barrier(tuple(jnp.split(out_weight, 2, axis=0)))

    far_exists = (me > 0) & (me < devices - 1)
    meta = jnp.stack([core, far_exists.astype(core.dtype)]).astype(jnp.int32)

    vmem = pl.BlockSpec(memory_space=pltpu.VMEM)
    smem = pl.BlockSpec(memory_space=pltpu.SMEM)
    hbm = pl.BlockSpec(memory_space=pltpu.HBM)
    sizes = (lon, width, nblocks, rows)
    params = pltpu.CompilerParams(vmem_limit_bytes=48 * 2**20)
    tap_flops, row_flops = 2 * lon * width * width, 2 * lon * width * (width + 4 * obs)
    edge, partial, keys, taps = pl.pallas_call(
        functools.partial(inner_kernel, *sizes),
        out_shape=[
            jax.ShapeDtypeStruct((lon, width), jnp.bfloat16),
            jax.ShapeDtypeStruct((q_dev, width), jnp.float32),
            jax.ShapeDtypeStruct((width, obs), jnp.bfloat16),
            jax.ShapeDtypeStruct(conv_weight.shape[1:], jnp.bfloat16),
        ],
        in_specs=[smem] + [vmem] * 7 + [hbm],
        out_specs=[vmem] * 4,
        scratch_shapes=[
            pltpu.VMEM((2,) + conv_weight.shape[1:], jnp.bfloat16),
            pltpu.VMEM((3 * lon, width), jnp.bfloat16),
            pltpu.VMEM((3 * lon, width), jnp.bfloat16),
            pltpu.SemaphoreType.DMA((7,)),
        ],
        compiler_params=params,
        cost_estimate=pl.CostEstimate(
            flops=3 * row_flops + 12 * tap_flops, bytes_accessed=2 * conv_weight.size, transcendentals=0
        ),
        name="inner",
    )(meta, near, near_sent, far_sent, same, other, upper, lower, conv_weight)
    return pl.pallas_call(
        functools.partial(outer_kernel, *sizes),
        out_shape=jax.ShapeDtypeStruct((q_dev, width), jnp.bfloat16),
        in_specs=[smem] + [vmem] * 9,
        out_specs=vmem,
        scratch_shapes=[
            pltpu.VMEM((lon, width), jnp.bfloat16),
        ],
        compiler_params=params,
        cost_estimate=pl.CostEstimate(
            flops=row_flops + 6 * tap_flops, bytes_accessed=conv_weight.size, transcendentals=0
        ),
        name="outer",
    )(meta, far, same, other, upper, lower, edge, partial, keys, taps)


def solution(mesh):
    in_specs = (
        P(AXES, None),
        P(AXES, None),
        P(AXES, None),
        P(AXES, None),
        P(AXES, None),
        P(),
        P(),
        P(),
    )
    return jax.shard_map(
        on_device, mesh=mesh, in_specs=in_specs, out_specs=P(AXES, None), check_vma=False
    )
```

```python
import functools
import math

import jax
import jax.numpy as jnp
from jax import lax
from jax.experimental import pallas as pl
from jax.experimental.pallas import tpu as pltpu
from jax.sharding import PartitionSpec as P

HEADS = 8
OBS_BLOCK = 128
AXES = ("blk", "tile")
PAIR = 2
CORES = 2
LIMIT_ROWS = 16


def both_cores(same_ref, other_ref, kind, cols):
    return jnp.concatenate(
        [ref[:, kind, :, cols].reshape(-1, cols.stop - cols.start) for ref in (same_ref, other_ref)],
        axis=0,
    )


def attend(lon, width, nblocks, rows, core, row_refs, keys_of, same_ref, other_ref, weight_refs, mixed_ref):
    head = width // HEADS
    pair = PAIR * head
    obs = nblocks * OBS_BLOCK
    scale = head ** (-0.5) * math.log2(math.e)
    half = OBS_BLOCK // CORES
    key_lane = lax.broadcasted_iota(jnp.int32, (1, OBS_BLOCK), 1)
    spread = (key_lane % half) // rows * (CORES * rows) + key_lane % rows
    first = key_lane < half

    def row_bias(ref):
        limit = ref[2 * lon : 2 * lon + LIMIT_ROWS, :].astype(jnp.float32)[:1].astype(jnp.int32)

        parts = []
        for parity in (core, 1 - core):
            place = spread + parity * rows
            for block in range(0, nblocks, CORES):
                ends = [
                    jnp.broadcast_to(limit[:, b : b + 1], (1, OBS_BLOCK)) for b in (block, block + 1)
                ]
                end = jnp.where(first, ends[0], ends[1])
                parts.append(jnp.where(place < end, 0.0, -jnp.inf))
        return jnp.concatenate(parts, axis=1)

    biases = [row_bias(ref) for ref in row_refs]
    lane = lax.broadcasted_iota(jnp.int32, (obs, pair), 1)
    ones = [(lane // head == h).astype(jnp.bfloat16) for h in range(PAIR)]

    empty = jnp.zeros((head, obs), jnp.bfloat16)

    def columns(group):
        return slice(group * pair, (group + 1) * pair)

    def scores_of(group):
        keys = keys_of(columns(group))
        query = jnp.concatenate([ref[:lon, columns(group)] for ref in row_refs], axis=0)
        scores = []
        for h in range(PAIR):
            part = [keys[i * head : (i + 1) * head] if i == h else empty for i in range(PAIR)]
            part = jnp.concatenate(part, axis=0)
            scores.append(jnp.dot(query, part, preferred_element_type=jnp.float32))
        return scores

    def weights_of(scores):
        pieces = []
        for t, bias in enumerate(biases):
            piece = scores[t * lon : (t + 1) * lon] * scale + bias
            top = jnp.max(piece, axis=1, keepdims=True)
            pieces.append(jnp.exp2(piece - top).astype(jnp.bfloat16))
        return jnp.concatenate(pieces, axis=0)

    groups = HEADS // PAIR
    scores = [scores_of(group) for group in range(groups)]
    weights = [
        jnp.concatenate([weights_of(part) for part in scores[group]], axis=1) for group in range(groups)
    ]
    for group in range(groups):
        values = both_cores(same_ref, other_ref, 1, columns(group))
        value_parts = jnp.concatenate(
            [jnp.concatenate([values * one, one], axis=1) for one in ones], axis=0
        )
        both = jnp.dot(weights[group], value_parts, preferred_element_type=jnp.float32)
        mixed_ref[:, columns(group)] = (both[:, :pair] / both[:, pair:]).astype(jnp.bfloat16)

    depth = width // len(weight_refs)
    projected = sum(
        jnp.dot(
            mixed_ref[:, i * depth : (i + 1) * depth], ref[...], preferred_element_type=jnp.float32
        )
        for i, ref in enumerate(weight_refs)
    )
    grid = jnp.concatenate([ref[lon : 2 * lon, :] for ref in row_refs], axis=0)
    wide = (grid.astype(jnp.float32) + projected).astype(jnp.bfloat16).astype(jnp.float32)
    normed = wide * lax.rsqrt(jnp.mean(wide * wide, axis=-1, keepdims=True) + 1e-06)
    return wide, normed


def around(parts, lon):
    return pltpu.roll(parts[0], 1, 0) + parts[1] + pltpu.roll(parts[2], lon - 1, 0)


def inner_kernel(
    lon, width, nblocks, rows,
    meta_ref, near_ref, near_sent_ref, far_sent_ref, same_ref, other_ref, upper_ref, lower_ref,
    conv_hbm, edge_ref, partial_ref, keys_ref, last_ref, conv_ref, mixed_ref, field_ref, sems,
):
    core = meta_ref[0]
    copies = [
        pltpu.make_async_copy(
            conv_hbm.at[source, lon_off], conv_ref.at[i, lon_off], sems.at[2 * lon_off + i]
        )
        for lon_off in range(3)
        for i, source in enumerate((1, 2 - 2 * core))
    ]
    copies.append(pltpu.make_async_copy(conv_hbm.at[2 * core, :2], last_ref, sems.at[6]))
    for copy in copies:
        copy.start()

    def keys_of(cols):
        keys = both_cores(same_ref, other_ref, 0, cols).T
        keys_ref[cols, :] = keys
        return keys

    wide, normed = attend(
        lon, width, nblocks, rows, core, (near_ref, near_sent_ref, far_sent_ref), keys_of,
        same_ref, other_ref, (upper_ref, lower_ref), mixed_ref,
    )
    field_ref[...] = normed.astype(jnp.bfloat16)
    edge_ref[...] = field_ref[2 * lon :, :]
    inputs = jnp.concatenate([field_ref[lon:, :], field_ref[: 2 * lon, :]], axis=1)
    terms = []
    for lon_off in range(3):
        for copy in copies[2 * lon_off : 2 * lon_off + 2]:
            copy.wait()
        taps = conv_ref[:, lon_off].reshape(2 * width, width)
        terms.append(jnp.dot(inputs, taps, preferred_element_type=jnp.float32))
    for start in (0, lon):
        here = slice(start, start + lon)
        shifted = around([term[here] for term in terms], lon)
        partial_ref[here, :] = wide[start + lon : start + 2 * lon] + shifted
    copies[6].wait()


def outer_kernel(
    lon, width, nblocks, rows,
    meta_ref, far_ref, same_ref, other_ref, upper_ref, lower_ref, edge_ref, partial_ref, keys_ref,
    taps_ref, conv_hbm, out_ref, conv_ref, mixed_ref, sem,
):
    core = meta_ref[0]
    copy = pltpu.make_async_copy(conv_hbm.at[2 * core, 2], conv_ref, sem)
    copy.start()
    _, normed = attend(
        lon, width, nblocks, rows, core, (far_ref,), lambda cols: keys_ref[cols, :],
        same_ref, other_ref, (upper_ref, lower_ref), mixed_ref,
    )
    far = jnp.where(meta_ref[1] > 0, normed, 0.0).astype(jnp.bfloat16)
    field = jnp.concatenate([edge_ref[...], far], axis=0)
    terms = [
        jnp.dot(field, taps_ref[lon_off], preferred_element_type=jnp.float32) for lon_off in range(2)
    ]
    copy.wait()
    terms.append(jnp.dot(field, conv_ref[...], preferred_element_type=jnp.float32))
    for start, tile in ((0, 1 - core), (lon, core)):
        here = slice(start, start + lon)
        total = partial_ref[here, :] + around([term[here] for term in terms], lon)
        out_ref[pl.ds(pl.multiple_of(tile * lon, lon), lon), :] = total.astype(jnp.bfloat16)


def on_device(
    grid_feat, queries, obs_keys, obs_values, block_mask, obs_valid, out_weight, conv_weight
):
    q_dev, width = queries.shape
    tiles, nblocks = block_mask.shape
    rows = obs_keys.shape[0]
    lon = q_dev // tiles
    obs = nblocks * OBS_BLOCK
    devices = lax.axis_size(AXES)
    pairs = devices // CORES
    me = lax.axis_index(AXES)
    core = me % CORES

    block = jnp.stack([obs_keys, obs_values])
    groups = [list(range(c, devices, CORES)) for c in range(CORES)]
    same = lax.all_to_all(
        jnp.broadcast_to(block[None], (pairs,) + block.shape), AXES, 0, 0, axis_index_groups=groups
    )
    swap = [(i, i ^ 1) for i in range(devices)]
    across = [(i, i + 1) for i in range(1, devices - 1, CORES)]
    across += [(target, source) for source, target in across]

    query_rows, grid_rows = lax.optimization_barrier(
        (jnp.split(queries, tiles, axis=0), jnp.split(grid_feat, tiles, axis=0))
    )
    limits = jnp.where(block_mask > 0, obs_valid[None], 0).astype(jnp.bfloat16)
    limits = jnp.pad(limits, ((0, 0), (0, width - nblocks)))

    def packed(tile):
        limit = jnp.broadcast_to(limits[tile][None], (LIMIT_ROWS, width))
        return jnp.concatenate([query_rows[tile], grid_rows[tile], limit], axis=0)

    first, last = packed(0), packed(tiles - 1)
    far_sent = jnp.where(core == 0, first, last)
    near_sent = jnp.where(core == 0, last, first)
    near = lax.ppermute(near_sent, AXES, swap)
    far = lax.ppermute(far_sent, AXES, across)
    other = lax.ppermute(same, AXES, swap)
    out_weight, _ = lax.optimization_barrier((out_weight, same))
    upper, lower = lax.optimization_barrier(tuple(jnp.split(out_weight, 2, axis=0)))

    far_exists = (me > 0) & (me < devices - 1)
    meta = jnp.stack([core, far_exists.astype(core.dtype)]).astype(jnp.int32)

    vmem = pl.BlockSpec(memory_space=pltpu.VMEM)
    smem = pl.BlockSpec(memory_space=pltpu.SMEM)
    hbm = pl.BlockSpec(memory_space=pltpu.HBM)
    sizes = (lon, width, nblocks, rows)
    params = pltpu.CompilerParams(vmem_limit_bytes=48 * 2**20)
    tap_flops, row_flops = 2 * lon * width * width, 2 * lon * width * (width + 4 * obs)
    edge, partial, keys, taps = pl.pallas_call(
        functools.partial(inner_kernel, *sizes),
        out_shape=[
            jax.ShapeDtypeStruct((lon, width), jnp.bfloat16),
            jax.ShapeDtypeStruct((q_dev, width), jnp.float32),
            jax.ShapeDtypeStruct((width, obs), jnp.bfloat16),
            jax.ShapeDtypeStruct((2, width, width), jnp.bfloat16),
        ],
        in_specs=[smem] + [vmem] * 7 + [hbm],
        out_specs=[vmem] * 4,
        scratch_shapes=[
            pltpu.VMEM((2,) + conv_weight.shape[1:], jnp.bfloat16),
            pltpu.VMEM((3 * lon, width), jnp.bfloat16),
            pltpu.VMEM((3 * lon, width), jnp.bfloat16),
            pltpu.SemaphoreType.DMA((7,)),
        ],
        compiler_params=params,
        cost_estimate=pl.CostEstimate(
            flops=3 * row_flops + 12 * tap_flops, bytes_accessed=2 * conv_weight.size, transcendentals=0
        ),
        name="inner",
    )(meta, near, near_sent, far_sent, same, other, upper, lower, conv_weight)
    return pl.pallas_call(
        functools.partial(outer_kernel, *sizes),
        out_shape=jax.ShapeDtypeStruct((q_dev, width), jnp.bfloat16),
        in_specs=[smem] + [vmem] * 9 + [hbm],
        out_specs=vmem,
        scratch_shapes=[
            pltpu.VMEM((width, width), jnp.bfloat16),
            pltpu.VMEM((lon, width), jnp.bfloat16),
            pltpu.SemaphoreType.DMA,
        ],
        compiler_params=params,
        cost_estimate=pl.CostEstimate(
            flops=row_flops + 6 * tap_flops, bytes_accessed=conv_weight.size, transcendentals=0
        ),
        name="outer",
    )(meta, far, same, other, upper, lower, edge, partial, keys, taps, conv_weight)


def solution(mesh):
    in_specs = (
        P(AXES, None),
        P(AXES, None),
        P(AXES, None),
        P(AXES, None),
        P(AXES, None),
        P(),
        P(),
        P(),
    )
    return jax.shard_map(
        on_device, mesh=mesh, in_specs=in_specs, out_specs=P(AXES, None), check_vma=False
    )
```

```python
import functools
import math

import jax
import jax.numpy as jnp
from jax import lax
from jax.experimental import pallas as pl
from jax.experimental.pallas import tpu as pltpu
from jax.sharding import PartitionSpec as P

HEADS = 8
OBS_BLOCK = 128
AXES = ("blk", "tile")
PAIR = 2
CORES = 2
LIMIT_ROWS = 16


def both_cores(same_ref, other_ref, kind, cols):
    return jnp.concatenate(
        [ref[:, kind, :, cols].reshape(-1, cols.stop - cols.start) for ref in (same_ref, other_ref)],
        axis=0,
    )


def attend(lon, width, nblocks, rows, core, row_refs, keys_of, same_ref, other_ref, weight_refs, mixed_ref):
    head = width // HEADS
    pair = PAIR * head
    obs = nblocks * OBS_BLOCK
    scale = head ** (-0.5) * math.log2(math.e)
    half = OBS_BLOCK // CORES
    key_lane = lax.broadcasted_iota(jnp.int32, (1, OBS_BLOCK), 1)
    spread = (key_lane % half) // rows * (CORES * rows) + key_lane % rows
    first = key_lane < half

    def row_bias(ref):
        limit = ref[2 * lon : 2 * lon + LIMIT_ROWS, :].astype(jnp.float32)[:1].astype(jnp.int32)

        parts = []
        for parity in (core, 1 - core):
            place = spread + parity * rows
            for block in range(0, nblocks, CORES):
                ends = [
                    jnp.broadcast_to(limit[:, b : b + 1], (1, OBS_BLOCK)) for b in (block, block + 1)
                ]
                end = jnp.where(first, ends[0], ends[1])
                parts.append(jnp.where(place < end, 0.0, -jnp.inf))
        return jnp.concatenate(parts, axis=1)

    biases = [row_bias(ref) for ref in row_refs]
    lane = lax.broadcasted_iota(jnp.int32, (obs, pair), 1)
    ones = [(lane // head == h).astype(jnp.bfloat16) for h in range(PAIR)]

    empty = jnp.zeros((head, obs), jnp.bfloat16)

    def columns(group):
        return slice(group * pair, (group + 1) * pair)

    def scores_of(group):
        keys = keys_of(columns(group))
        query = jnp.concatenate([ref[:lon, columns(group)] for ref in row_refs], axis=0)
        scores = []
        for h in range(PAIR):
            part = [keys[i * head : (i + 1) * head] if i == h else empty for i in range(PAIR)]
            part = jnp.concatenate(part, axis=0)
            scores.append(jnp.dot(query, part, preferred_element_type=jnp.float32))
        return scores

    def weights_of(scores):
        pieces = []
        for t, bias in enumerate(biases):
            piece = scores[t * lon : (t + 1) * lon] * scale + bias
            top = jnp.max(piece, axis=1, keepdims=True)
            pieces.append(jnp.exp2(piece - top).astype(jnp.bfloat16))
        return jnp.concatenate(pieces, axis=0)

    groups = HEADS // PAIR
    scores = [scores_of(group) for group in range(groups)]
    weights = [
        jnp.concatenate([weights_of(part) for part in scores[group]], axis=1) for group in range(groups)
    ]
    for group in range(groups):
        values = both_cores(same_ref, other_ref, 1, columns(group))
        value_parts = jnp.concatenate(
            [jnp.concatenate([values * one, one], axis=1) for one in ones], axis=0
        )
        both = jnp.dot(weights[group], value_parts, preferred_element_type=jnp.float32)
        mixed_ref[:, columns(group)] = (both[:, :pair] / both[:, pair:]).astype(jnp.bfloat16)

    depth = width // len(weight_refs)
    projected = sum(
        jnp.dot(
            mixed_ref[:, i * depth : (i + 1) * depth], ref[...], preferred_element_type=jnp.float32
        )
        for i, ref in enumerate(weight_refs)
    )
    grid = jnp.concatenate([ref[lon : 2 * lon, :] for ref in row_refs], axis=0)
    wide = (grid.astype(jnp.float32) + projected).astype(jnp.bfloat16).astype(jnp.float32)
    normed = wide * lax.rsqrt(jnp.mean(wide * wide, axis=-1, keepdims=True) + 1e-06)
    return wide, normed


def around(parts, lon):
    return pltpu.roll(parts[0], 1, 0) + parts[1] + pltpu.roll(parts[2], lon - 1, 0)


def inner_kernel(
    lon, width, nblocks, rows,
    meta_ref, near_ref, near_sent_ref, far_sent_ref, same_ref, other_ref, upper_ref, lower_ref,
    conv_ref, edge_ref, partial_ref, keys_ref, mixed_ref, field_ref,
):
    core = meta_ref[0]

    def keys_of(cols):
        keys = both_cores(same_ref, other_ref, 0, cols).T
        keys_ref[cols, :] = keys
        return keys

    wide, normed = attend(
        lon, width, nblocks, rows, core, (near_ref, near_sent_ref, far_sent_ref), keys_of,
        same_ref, other_ref, (upper_ref, lower_ref), mixed_ref,
    )
    field_ref[...] = normed.astype(jnp.bfloat16)
    edge_ref[...] = field_ref[2 * lon :, :]
    inputs = jnp.concatenate([field_ref[lon:, :], field_ref[: 2 * lon, :]], axis=1)
    terms = []
    for lon_off in range(3):
        taps = jnp.concatenate([conv_ref[1, lon_off], conv_ref[2 - 2 * core, lon_off]], axis=0)
        terms.append(jnp.dot(inputs, taps, preferred_element_type=jnp.float32))
    for start in (0, lon):
        here = slice(start, start + lon)
        shifted = around([term[here] for term in terms], lon)
        partial_ref[here, :] = wide[start + lon : start + 2 * lon] + shifted


def outer_kernel(
    lon, width, nblocks, rows,
    meta_ref, far_ref, same_ref, other_ref, upper_ref, lower_ref, edge_ref, partial_ref, keys_ref,
    conv_ref, out_ref, mixed_ref,
):
    core = meta_ref[0]
    _, normed = attend(
        lon, width, nblocks, rows, core, (far_ref,), lambda cols: keys_ref[cols, :],
        same_ref, other_ref, (upper_ref, lower_ref), mixed_ref,
    )
    far = jnp.where(meta_ref[1] > 0, normed, 0.0).astype(jnp.bfloat16)
    field = jnp.concatenate([edge_ref[...], far], axis=0)
    terms = [
        jnp.dot(field, conv_ref[2 * core, lon_off], preferred_element_type=jnp.float32)
        for lon_off in range(3)
    ]
    for start, tile in ((0, 1 - core), (lon, core)):
        here = slice(start, start + lon)
        total = partial_ref[here, :] + around([term[here] for term in terms], lon)
        out_ref[pl.ds(pl.multiple_of(tile * lon, lon), lon), :] = total.astype(jnp.bfloat16)


def pack_kernel(lon, *refs):
    queries_refs, grid_refs, limit_refs = refs[:2], refs[2:4], refs[4:6]
    near_ref, far_ref = refs[6:]
    even = lax.axis_index("tile") % CORES == 0
    for place, pair_refs in (
        (slice(0, lon), queries_refs),
        (slice(lon, 2 * lon), grid_refs),
        (slice(2 * lon, 2 * lon + LIMIT_ROWS), limit_refs),
    ):
        first, last = pair_refs[0][...], pair_refs[1][...]
        far_ref[place, :] = jnp.where(even, first, last)
        near_ref[place, :] = jnp.where(even, last, first)


def on_device(
    grid_feat, queries, obs_keys, obs_values, block_mask, obs_valid, out_weight, conv_weight
):
    q_dev, width = queries.shape
    tiles, nblocks = block_mask.shape
    rows = obs_keys.shape[0]
    lon = q_dev // tiles
    obs = nblocks * OBS_BLOCK
    devices = lax.axis_size(AXES)
    pairs = devices // CORES
    me = lax.axis_index(AXES)
    core = me % CORES

    block = jnp.stack([obs_keys, obs_values])
    groups = [list(range(c, devices, CORES)) for c in range(CORES)]
    same = lax.all_to_all(
        jnp.broadcast_to(block[None], (pairs,) + block.shape), AXES, 0, 0, axis_index_groups=groups
    )
    swap = [(i, i ^ 1) for i in range(devices)]
    across = [(i, i + 1) for i in range(1, devices - 1, CORES)]
    across += [(target, source) for source, target in across]

    query_rows, grid_rows = lax.optimization_barrier(
        (jnp.split(queries, tiles, axis=0), jnp.split(grid_feat, tiles, axis=0))
    )
    limits = jnp.where(block_mask > 0, obs_valid[None], 0).astype(jnp.bfloat16)
    limits = jnp.pad(limits, ((0, 0), (0, width - nblocks)))

    limit_rows = [
        jnp.broadcast_to(limits[tile][None], (LIMIT_ROWS, width)) for tile in range(tiles)
    ]
    vmem = pl.BlockSpec(memory_space=pltpu.VMEM)
    payload = jax.ShapeDtypeStruct((2 * lon + LIMIT_ROWS, width), jnp.bfloat16)
    near_sent, far_sent = pl.pallas_call(
        functools.partial(pack_kernel, lon),
        out_shape=[payload] * 2,
        in_specs=[vmem] * 6,
        out_specs=[vmem] * 2,
        cost_estimate=pl.CostEstimate(flops=10**10, bytes_accessed=4 * payload.size * 2, transcendentals=0),
        name="pack",
    )(*query_rows, *grid_rows, *limit_rows)
    far = lax.ppermute(far_sent, AXES, across)
    near = lax.ppermute(near_sent, AXES, swap)
    other = lax.ppermute(same, AXES, swap)
    out_weight, _ = lax.optimization_barrier((out_weight, same))
    upper, lower = lax.optimization_barrier(tuple(jnp.split(out_weight, 2, axis=0)))

    far_exists = (me > 0) & (me < devices - 1)
    meta = jnp.stack([core, far_exists.astype(core.dtype)]).astype(jnp.int32)

    smem = pl.BlockSpec(memory_space=pltpu.SMEM)
    sizes = (lon, width, nblocks, rows)
    params = pltpu.CompilerParams(vmem_limit_bytes=40 * 2**20)
    tap_flops, row_flops = 2 * lon * width * width, 2 * lon * width * (width + 4 * obs)
    edge, partial, keys = pl.pallas_call(
        functools.partial(inner_kernel, *sizes),
        out_shape=[
            jax.ShapeDtypeStruct((lon, width), jnp.bfloat16),
            jax.ShapeDtypeStruct((q_dev, width), jnp.float32),
            jax.ShapeDtypeStruct((width, obs), jnp.bfloat16),
        ],
        in_specs=[smem] + [vmem] * 8,
        out_specs=[vmem] * 3,
        scratch_shapes=[
            pltpu.VMEM((3 * lon, width), jnp.bfloat16),
            pltpu.VMEM((3 * lon, width), jnp.bfloat16),
        ],
        compiler_params=params,
        cost_estimate=pl.CostEstimate(
            flops=3 * row_flops + 12 * tap_flops, bytes_accessed=2 * conv_weight.size, transcendentals=0
        ),
        name="inner",
    )(meta, near, near_sent, far_sent, same, other, upper, lower, conv_weight)
    return pl.pallas_call(
        functools.partial(outer_kernel, *sizes),
        out_shape=jax.ShapeDtypeStruct((q_dev, width), jnp.bfloat16),
        in_specs=[smem] + [vmem] * 9,
        out_specs=vmem,
        scratch_shapes=[
            pltpu.VMEM((lon, width), jnp.bfloat16),
        ],
        compiler_params=params,
        cost_estimate=pl.CostEstimate(
            flops=row_flops + 6 * tap_flops, bytes_accessed=conv_weight.size, transcendentals=0
        ),
        name="outer",
    )(meta, far, same, other, upper, lower, edge, partial, keys, conv_weight)


def solution(mesh):
    in_specs = (
        P(AXES, None),
        P(AXES, None),
        P(AXES, None),
        P(AXES, None),
        P(AXES, None),
        P(),
        P(),
        P(),
    )
    return jax.shard_map(
        on_device, mesh=mesh, in_specs=in_specs, out_specs=P(AXES, None), check_vma=False
    )
```

```python
import functools
import math

import jax
import jax.numpy as jnp
from jax import lax
from jax.experimental import pallas as pl
from jax.experimental.pallas import tpu as pltpu
from jax.sharding import PartitionSpec as P

HEADS = 8
OBS_BLOCK = 128
AXES = ("blk", "tile")
PAIR = 2
CORES = 2
LIMIT_ROWS = 16


def both_cores(same_ref, other_ref, kind, cols):
    return jnp.concatenate(
        [ref[:, kind, :, cols].reshape(-1, cols.stop - cols.start) for ref in (same_ref, other_ref)],
        axis=0,
    )


def attend(lon, width, nblocks, rows, core, row_refs, keys_of, same_ref, other_ref, weight_refs, mixed_ref):
    head = width // HEADS
    pair = PAIR * head
    obs = nblocks * OBS_BLOCK
    scale = head ** (-0.5) * math.log2(math.e)
    half = OBS_BLOCK // CORES
    key_lane = lax.broadcasted_iota(jnp.int32, (1, OBS_BLOCK), 1)
    spread = (key_lane % half) // rows * (CORES * rows) + key_lane % rows
    first = key_lane < half

    def row_bias(ref):
        limit = ref[2 * lon : 2 * lon + LIMIT_ROWS, :].astype(jnp.float32)[:1].astype(jnp.int32)

        parts = []
        for parity in (core, 1 - core):
            place = spread + parity * rows
            for block in range(0, nblocks, CORES):
                ends = [
                    jnp.broadcast_to(limit[:, b : b + 1], (1, OBS_BLOCK)) for b in (block, block + 1)
                ]
                end = jnp.where(first, ends[0], ends[1])
                parts.append(jnp.where(place < end, 0.0, -jnp.inf))
        return jnp.concatenate(parts, axis=1)

    biases = [row_bias(ref) for ref in row_refs]
    lane = lax.broadcasted_iota(jnp.int32, (obs, pair), 1)
    ones = [(lane // head == h).astype(jnp.bfloat16) for h in range(PAIR)]

    empty = jnp.zeros((head, obs), jnp.bfloat16)

    def columns(group):
        return slice(group * pair, (group + 1) * pair)

    def scores_of(group):
        keys = keys_of(columns(group))
        query = jnp.concatenate([ref[:lon, columns(group)] for ref in row_refs], axis=0)
        scores = []
        for h in range(PAIR):
            part = [keys[i * head : (i + 1) * head] if i == h else empty for i in range(PAIR)]
            part = jnp.concatenate(part, axis=0)
            scores.append(jnp.dot(query, part, preferred_element_type=jnp.float32))
        return scores

    def weights_of(scores):
        pieces = []
        for t, bias in enumerate(biases):
            piece = scores[t * lon : (t + 1) * lon] * scale + bias
            top = jnp.max(piece, axis=1, keepdims=True)
            pieces.append(jnp.exp2(piece - top).astype(jnp.bfloat16))
        return jnp.concatenate(pieces, axis=0)

    groups = HEADS // PAIR
    scores = [scores_of(group) for group in range(groups)]
    weights = [
        jnp.concatenate([weights_of(part) for part in scores[group]], axis=1) for group in range(groups)
    ]
    for group in range(groups):
        values = both_cores(same_ref, other_ref, 1, columns(group))
        value_parts = jnp.concatenate(
            [jnp.concatenate([values * one, one], axis=1) for one in ones], axis=0
        )
        both = jnp.dot(weights[group], value_parts, preferred_element_type=jnp.float32)
        mixed_ref[:, columns(group)] = (both[:, :pair] / both[:, pair:]).astype(jnp.bfloat16)

    depth = width // len(weight_refs)
    projected = sum(
        jnp.dot(
            mixed_ref[:, i * depth : (i + 1) * depth], ref[...], preferred_element_type=jnp.float32
        )
        for i, ref in enumerate(weight_refs)
    )
    grid = jnp.concatenate([ref[lon : 2 * lon, :] for ref in row_refs], axis=0)
    wide = (grid.astype(jnp.float32) + projected).astype(jnp.bfloat16).astype(jnp.float32)
    normed = wide * lax.rsqrt(jnp.mean(wide * wide, axis=-1, keepdims=True) + 1e-06)
    return wide, normed


def around(parts, lon):
    return pltpu.roll(parts[0], 1, 0) + parts[1] + pltpu.roll(parts[2], lon - 1, 0)


def inner_kernel(
    lon, width, nblocks, rows,
    meta_ref, near_ref, near_sent_ref, far_sent_ref, same_ref, other_ref, upper_ref, lower_ref,
    conv_ref, edge_ref, partial_ref, keys_ref, mixed_ref, field_ref,
):
    core = meta_ref[0]

    def keys_of(cols):
        keys = both_cores(same_ref, other_ref, 0, cols).T
        keys_ref[cols, :] = keys
        return keys

    wide, normed = attend(
        lon, width, nblocks, rows, core, (near_ref, near_sent_ref, far_sent_ref), keys_of,
        same_ref, other_ref, (upper_ref, lower_ref), mixed_ref,
    )
    field_ref[...] = normed.astype(jnp.bfloat16)
    edge_ref[...] = field_ref[2 * lon :, :]
    inputs = jnp.concatenate([field_ref[lon:, :], field_ref[: 2 * lon, :]], axis=1)
    terms = []
    for lon_off in range(3):
        taps = jnp.concatenate([conv_ref[1, lon_off], conv_ref[2 - 2 * core, lon_off]], axis=0)
        terms.append(jnp.dot(inputs, taps, preferred_element_type=jnp.float32))
    for start in (0, lon):
        here = slice(start, start + lon)
        shifted = around([term[here] for term in terms], lon)
        partial_ref[here, :] = wide[start + lon : start + 2 * lon] + shifted


def outer_kernel(
    lon, width, nblocks, rows,
    meta_ref, far_ref, same_ref, other_ref, upper_ref, lower_ref, edge_ref, partial_ref, keys_ref,
    conv_ref, out_ref, mixed_ref,
):
    core = meta_ref[0]
    _, normed = attend(
        lon, width, nblocks, rows, core, (far_ref,), lambda cols: keys_ref[cols, :],
        same_ref, other_ref, (upper_ref, lower_ref), mixed_ref,
    )
    far = jnp.where(meta_ref[1] > 0, normed, 0.0).astype(jnp.bfloat16)
    field = jnp.concatenate([edge_ref[...], far], axis=0)
    terms = [
        jnp.dot(field, conv_ref[2 * core, lon_off], preferred_element_type=jnp.float32)
        for lon_off in range(3)
    ]
    for start, tile in ((0, 1 - core), (lon, core)):
        here = slice(start, start + lon)
        total = partial_ref[here, :] + around([term[here] for term in terms], lon)
        out_ref[pl.ds(pl.multiple_of(tile * lon, lon), lon), :] = total.astype(jnp.bfloat16)


def pack_kernel(lon, *refs):
    queries_refs, grid_refs, limit_refs = refs[:2], refs[2:4], refs[4:6]
    near_ref, far_ref = refs[6:]
    even = lax.axis_index("tile") % CORES == 0
    for place, pair_refs in (
        (slice(0, lon), queries_refs),
        (slice(lon, 2 * lon), grid_refs),
        (slice(2 * lon, 2 * lon + LIMIT_ROWS), limit_refs),
    ):
        first, last = pair_refs[0][...], pair_refs[1][...]
        far_ref[place, :] = jnp.where(even, first, last)
        near_ref[place, :] = jnp.where(even, last, first)


def on_device(
    grid_feat, queries, obs_keys, obs_values, block_mask, obs_valid, out_weight, conv_weight
):
    q_dev, width = queries.shape
    tiles, nblocks = block_mask.shape
    rows = obs_keys.shape[0]
    lon = q_dev // tiles
    obs = nblocks * OBS_BLOCK
    devices = lax.axis_size(AXES)
    pairs = devices // CORES
    me = lax.axis_index(AXES)
    core = me % CORES

    block = jnp.stack([obs_keys, obs_values])
    groups = [list(range(c, devices, CORES)) for c in range(CORES)]
    same = lax.all_to_all(
        jnp.broadcast_to(block[None], (pairs,) + block.shape), AXES, 0, 0, axis_index_groups=groups
    )
    swap = [(i, i ^ 1) for i in range(devices)]
    across = [(i, i + 1) for i in range(1, devices - 1, CORES)]
    across += [(target, source) for source, target in across]

    query_rows, grid_rows = lax.optimization_barrier(
        (jnp.split(queries, tiles, axis=0), jnp.split(grid_feat, tiles, axis=0))
    )
    limits = jnp.where(block_mask > 0, obs_valid[None], 0).astype(jnp.bfloat16)
    limits = jnp.pad(limits, ((0, 0), (0, width - nblocks)))

    limit_rows = [
        jnp.broadcast_to(limits[tile][None], (LIMIT_ROWS, width)) for tile in range(tiles)
    ]
    vmem = pl.BlockSpec(memory_space=pltpu.VMEM)
    payload = jax.ShapeDtypeStruct((2 * lon + LIMIT_ROWS, width), jnp.bfloat16)
    near_sent, far_sent = pl.pallas_call(
        functools.partial(pack_kernel, lon),
        out_shape=[payload] * 2,
        in_specs=[vmem] * 6,
        out_specs=[vmem] * 2,
        compiler_params=pltpu.CompilerParams(vmem_limit_bytes=4 * 2**20),
        cost_estimate=pl.CostEstimate(flops=10**10, bytes_accessed=8 * payload.size, transcendentals=0),
        name="pack",
    )(*query_rows, *grid_rows, *limit_rows)
    far = lax.ppermute(far_sent, AXES, across)
    near = lax.ppermute(near_sent, AXES, swap)
    other = lax.ppermute(same, AXES, swap)
    out_weight, _ = lax.optimization_barrier((out_weight, same))
    upper, lower = lax.optimization_barrier(tuple(jnp.split(out_weight, 2, axis=0)))

    far_exists = (me > 0) & (me < devices - 1)
    meta = jnp.stack([core, far_exists.astype(core.dtype)]).astype(jnp.int32)

    smem = pl.BlockSpec(memory_space=pltpu.SMEM)
    sizes = (lon, width, nblocks, rows)
    params = pltpu.CompilerParams(vmem_limit_bytes=40 * 2**20)
    tap_flops, row_flops = 2 * lon * width * width, 2 * lon * width * (width + 4 * obs)
    edge, partial, keys = pl.pallas_call(
        functools.partial(inner_kernel, *sizes),
        out_shape=[
            jax.ShapeDtypeStruct((lon, width), jnp.bfloat16),
            jax.ShapeDtypeStruct((q_dev, width), jnp.float32),
            jax.ShapeDtypeStruct((width, obs), jnp.bfloat16),
        ],
        in_specs=[smem] + [vmem] * 8,
        out_specs=[vmem] * 3,
        scratch_shapes=[
            pltpu.VMEM((3 * lon, width), jnp.bfloat16),
            pltpu.VMEM((3 * lon, width), jnp.bfloat16),
        ],
        compiler_params=params,
        cost_estimate=pl.CostEstimate(
            flops=3 * row_flops + 12 * tap_flops, bytes_accessed=2 * conv_weight.size, transcendentals=0
        ),
        name="inner",
    )(meta, near, near_sent, far_sent, same, other, upper, lower, conv_weight)
    return pl.pallas_call(
        functools.partial(outer_kernel, *sizes),
        out_shape=jax.ShapeDtypeStruct((q_dev, width), jnp.bfloat16),
        in_specs=[smem] + [vmem] * 9,
        out_specs=vmem,
        scratch_shapes=[
            pltpu.VMEM((lon, width), jnp.bfloat16),
        ],
        compiler_params=params,
        cost_estimate=pl.CostEstimate(
            flops=row_flops + 6 * tap_flops, bytes_accessed=conv_weight.size, transcendentals=0
        ),
        name="outer",
    )(meta, far, same, other, upper, lower, edge, partial, keys, conv_weight)


def solution(mesh):
    in_specs = (
        P(AXES, None),
        P(AXES, None),
        P(AXES, None),
        P(AXES, None),
        P(AXES, None),
        P(),
        P(),
        P(),
    )
    return jax.shard_map(
        on_device, mesh=mesh, in_specs=in_specs, out_specs=P(AXES, None), check_vma=False
    )
```

```python
import functools
import math

import jax
import jax.numpy as jnp
from jax import lax
from jax.experimental import pallas as pl
from jax.experimental.pallas import tpu as pltpu
from jax.sharding import PartitionSpec as P

HEADS = 8
OBS_BLOCK = 128
AXES = ("blk", "tile")
PAIR = 2
CORES = 2
LIMIT_ROWS = 16


def both_cores(same_ref, other_ref, kind, cols):
    return jnp.concatenate(
        [ref[:, kind, :, cols].reshape(-1, cols.stop - cols.start) for ref in (same_ref, other_ref)],
        axis=0,
    )


def attend(lon, width, nblocks, rows, core, row_refs, keys_of, same_ref, other_ref, weight_refs, mixed_ref):
    head = width // HEADS
    pair = PAIR * head
    obs = nblocks * OBS_BLOCK
    scale = head ** (-0.5) * math.log2(math.e)
    half = OBS_BLOCK // CORES
    key_lane = lax.broadcasted_iota(jnp.int32, (1, OBS_BLOCK), 1)
    spread = (key_lane % half) // rows * (CORES * rows) + key_lane % rows
    first = key_lane < half

    def row_bias(ref):
        limit = ref[2 * lon : 2 * lon + LIMIT_ROWS, :].astype(jnp.float32)[:1].astype(jnp.int32)

        parts = []
        for parity in (core, 1 - core):
            place = spread + parity * rows
            for block in range(0, nblocks, CORES):
                ends = [
                    jnp.broadcast_to(limit[:, b : b + 1], (1, OBS_BLOCK)) for b in (block, block + 1)
                ]
                end = jnp.where(first, ends[0], ends[1])
                parts.append(jnp.where(place < end, 0.0, -jnp.inf))
        return jnp.concatenate(parts, axis=1)

    biases = [row_bias(ref) for ref in row_refs]
    lane = lax.broadcasted_iota(jnp.int32, (obs, pair), 1)
    ones = [(lane // head == h).astype(jnp.bfloat16) for h in range(PAIR)]

    empty = jnp.zeros((head, obs), jnp.bfloat16)

    def columns(group):
        return slice(group * pair, (group + 1) * pair)

    def scores_of(group):
        keys = keys_of(columns(group))
        query = jnp.concatenate([ref[:lon, columns(group)] for ref in row_refs], axis=0)
        scores = []
        for h in range(PAIR):
            part = [keys[i * head : (i + 1) * head] if i == h else empty for i in range(PAIR)]
            part = jnp.concatenate(part, axis=0)
            scores.append(jnp.dot(query, part, preferred_element_type=jnp.float32))
        return scores

    def weights_of(scores):
        pieces = []
        for t, bias in enumerate(biases):
            piece = scores[t * lon : (t + 1) * lon] * scale + bias
            top = jnp.max(piece, axis=1, keepdims=True)
            pieces.append(jnp.exp2(piece - top).astype(jnp.bfloat16))
        return jnp.concatenate(pieces, axis=0)

    groups = HEADS // PAIR
    scores = [scores_of(group) for group in range(groups)]
    weights = [
        jnp.concatenate([weights_of(part) for part in scores[group]], axis=1) for group in range(groups)
    ]
    for group in range(groups):
        values = both_cores(same_ref, other_ref, 1, columns(group))
        value_parts = jnp.concatenate(
            [jnp.concatenate([values * one, one], axis=1) for one in ones], axis=0
        )
        both = jnp.dot(weights[group], value_parts, preferred_element_type=jnp.float32)
        mixed_ref[:, columns(group)] = (both[:, :pair] / both[:, pair:]).astype(jnp.bfloat16)

    depth = width // len(weight_refs)
    projected = sum(
        jnp.dot(
            mixed_ref[:, i * depth : (i + 1) * depth], ref[...], preferred_element_type=jnp.float32
        )
        for i, ref in enumerate(weight_refs)
    )
    grid = jnp.concatenate([ref[lon : 2 * lon, :] for ref in row_refs], axis=0)
    wide = (grid.astype(jnp.float32) + projected).astype(jnp.bfloat16).astype(jnp.float32)
    normed = wide * lax.rsqrt(jnp.mean(wide * wide, axis=-1, keepdims=True) + 1e-06)
    return wide, normed


def around(parts, lon):
    return pltpu.roll(parts[0], 1, 0) + parts[1] + pltpu.roll(parts[2], lon - 1, 0)


def inner_kernel(
    lon, width, nblocks, rows,
    meta_ref, near_ref, near_sent_ref, far_sent_ref, same_ref, other_ref, upper_ref, lower_ref,
    conv_ref, edge_ref, partial_ref, keys_ref, mixed_ref, field_ref,
):
    core = meta_ref[0]

    def keys_of(cols):
        keys = both_cores(same_ref, other_ref, 0, cols).T
        keys_ref[cols, :] = keys
        return keys

    wide, normed = attend(
        lon, width, nblocks, rows, core, (near_ref, near_sent_ref, far_sent_ref), keys_of,
        same_ref, other_ref, (upper_ref, lower_ref), mixed_ref,
    )
    field_ref[...] = normed.astype(jnp.bfloat16)
    edge_ref[...] = field_ref[2 * lon :, :]
    inputs = jnp.concatenate([field_ref[lon:, :], field_ref[: 2 * lon, :]], axis=1)
    terms = []
    for lon_off in range(3):
        taps = jnp.concatenate([conv_ref[1, lon_off], conv_ref[0, lon_off]], axis=0)
        terms.append(jnp.dot(inputs, taps, preferred_element_type=jnp.float32))
    for start in (0, lon):
        here = slice(start, start + lon)
        shifted = around([term[here] for term in terms], lon)
        partial_ref[here, :] = wide[start + lon : start + 2 * lon] + shifted


def outer_kernel(
    lon, width, nblocks, rows,
    meta_ref, far_ref, same_ref, other_ref, upper_ref, lower_ref, edge_ref, partial_ref, keys_ref,
    conv_ref, out_ref, mixed_ref,
):
    core = meta_ref[0]
    _, normed = attend(
        lon, width, nblocks, rows, core, (far_ref,), lambda cols: keys_ref[cols, :],
        same_ref, other_ref, (upper_ref, lower_ref), mixed_ref,
    )
    far = jnp.where(meta_ref[1] > 0, normed, 0.0).astype(jnp.bfloat16)
    field = jnp.concatenate([edge_ref[...], far], axis=0)
    terms = [
        jnp.dot(field, conv_ref[2, lon_off], preferred_element_type=jnp.float32)
        for lon_off in range(3)
    ]
    for start, tile in ((0, 1 - core), (lon, core)):
        here = slice(start, start + lon)
        total = partial_ref[here, :] + around([term[here] for term in terms], lon)
        out_ref[pl.ds(pl.multiple_of(tile * lon, lon), lon), :] = total.astype(jnp.bfloat16)


def pack_kernel(lon, *refs):
    queries_refs, grid_refs, limit_refs = refs[:2], refs[2:4], refs[4:6]
    near_ref, far_ref = refs[6:]
    even = lax.axis_index("tile") % CORES == 0
    for place, pair_refs in (
        (slice(0, lon), queries_refs),
        (slice(lon, 2 * lon), grid_refs),
        (slice(2 * lon, 2 * lon + LIMIT_ROWS), limit_refs),
    ):
        first, last = pair_refs[0][...], pair_refs[1][...]
        far_ref[place, :] = jnp.where(even, first, last)
        near_ref[place, :] = jnp.where(even, last, first)


def on_device(
    grid_feat, queries, obs_keys, obs_values, block_mask, obs_valid, out_weight, conv_weight
):
    q_dev, width = queries.shape
    tiles, nblocks = block_mask.shape
    rows = obs_keys.shape[0]
    lon = q_dev // tiles
    obs = nblocks * OBS_BLOCK
    devices = lax.axis_size(AXES)
    pairs = devices // CORES
    me = lax.axis_index(AXES)
    core = me % CORES

    block = jnp.stack([obs_keys, obs_values])
    groups = [list(range(c, devices, CORES)) for c in range(CORES)]
    same = lax.all_to_all(
        jnp.broadcast_to(block[None], (pairs,) + block.shape), AXES, 0, 0, axis_index_groups=groups
    )
    swap = [(i, i ^ 1) for i in range(devices)]
    across = [(i, i + 1) for i in range(1, devices - 1, CORES)]
    across += [(target, source) for source, target in across]

    query_rows, grid_rows = lax.optimization_barrier(
        (jnp.split(queries, tiles, axis=0), jnp.split(grid_feat, tiles, axis=0))
    )
    limits = jnp.where(block_mask > 0, obs_valid[None], 0).astype(jnp.bfloat16)
    limits = jnp.pad(limits, ((0, 0), (0, width - nblocks)))

    limit_rows = [
        jnp.broadcast_to(limits[tile][None], (LIMIT_ROWS, width)) for tile in range(tiles)
    ]
    vmem = pl.BlockSpec(memory_space=pltpu.VMEM)
    payload = jax.ShapeDtypeStruct((2 * lon + LIMIT_ROWS, width), jnp.bfloat16)
    near_sent, far_sent = pl.pallas_call(
        functools.partial(pack_kernel, lon),
        out_shape=[payload] * 2,
        in_specs=[vmem] * 6,
        out_specs=[vmem] * 2,
        compiler_params=pltpu.CompilerParams(vmem_limit_bytes=4 * 2**20),
        cost_estimate=pl.CostEstimate(flops=10**10, bytes_accessed=8 * payload.size, transcendentals=0),
        name="pack",
    )(*query_rows, *grid_rows, *limit_rows)
    far = lax.ppermute(far_sent, AXES, across)
    near = lax.ppermute(near_sent, AXES, swap)
    other = lax.ppermute(same, AXES, swap)
    out_weight, conv_weight, _ = lax.optimization_barrier((out_weight, conv_weight, same))
    conv_weight = jnp.where(core == 0, conv_weight[::-1], conv_weight)
    upper, lower = lax.optimization_barrier(tuple(jnp.split(out_weight, 2, axis=0)))

    far_exists = (me > 0) & (me < devices - 1)
    meta = jnp.stack([core, far_exists.astype(core.dtype)]).astype(jnp.int32)

    smem = pl.BlockSpec(memory_space=pltpu.SMEM)
    sizes = (lon, width, nblocks, rows)
    params = pltpu.CompilerParams(vmem_limit_bytes=40 * 2**20)
    tap_flops, row_flops = 2 * lon * width * width, 2 * lon * width * (width + 4 * obs)
    edge, partial, keys = pl.pallas_call(
        functools.partial(inner_kernel, *sizes),
        out_shape=[
            jax.ShapeDtypeStruct((lon, width), jnp.bfloat16),
            jax.ShapeDtypeStruct((q_dev, width), jnp.float32),
            jax.ShapeDtypeStruct((width, obs), jnp.bfloat16),
        ],
        in_specs=[smem] + [vmem] * 8,
        out_specs=[vmem] * 3,
        scratch_shapes=[
            pltpu.VMEM((3 * lon, width), jnp.bfloat16),
            pltpu.VMEM((3 * lon, width), jnp.bfloat16),
        ],
        compiler_params=params,
        cost_estimate=pl.CostEstimate(
            flops=3 * row_flops + 12 * tap_flops, bytes_accessed=2 * conv_weight.size, transcendentals=0
        ),
        name="inner",
    )(meta, near, near_sent, far_sent, same, other, upper, lower, conv_weight)
    return pl.pallas_call(
        functools.partial(outer_kernel, *sizes),
        out_shape=jax.ShapeDtypeStruct((q_dev, width), jnp.bfloat16),
        in_specs=[smem] + [vmem] * 9,
        out_specs=vmem,
        scratch_shapes=[
            pltpu.VMEM((lon, width), jnp.bfloat16),
        ],
        compiler_params=params,
        cost_estimate=pl.CostEstimate(
            flops=row_flops + 6 * tap_flops, bytes_accessed=conv_weight.size, transcendentals=0
        ),
        name="outer",
    )(meta, far, same, other, upper, lower, edge, partial, keys, conv_weight)


def solution(mesh):
    in_specs = (
        P(AXES, None),
        P(AXES, None),
        P(AXES, None),
        P(AXES, None),
        P(AXES, None),
        P(),
        P(),
        P(),
    )
    return jax.shard_map(
        on_device, mesh=mesh, in_specs=in_specs, out_specs=P(AXES, None), check_vma=False
    )
```

```python
import functools
import math

import jax
import jax.numpy as jnp
from jax import lax
from jax.experimental import pallas as pl
from jax.experimental.pallas import tpu as pltpu
from jax.sharding import PartitionSpec as P

HEADS = 8
OBS_BLOCK = 128
AXES = ("blk", "tile")
PAIR = 2
CORES = 2
LIMIT_ROWS = 16


def both_cores(same_ref, other_ref, kind, cols):
    return jnp.concatenate(
        [ref[:, kind, :, cols].reshape(-1, cols.stop - cols.start) for ref in (same_ref, other_ref)],
        axis=0,
    )


def attend(lon, width, nblocks, rows, core, row_refs, keys_of, same_ref, other_ref, weight_refs, mixed_ref):
    head = width // HEADS
    pair = PAIR * head
    obs = nblocks * OBS_BLOCK
    scale = head ** (-0.5) * math.log2(math.e)
    half = OBS_BLOCK // CORES
    key_lane = lax.broadcasted_iota(jnp.int32, (1, OBS_BLOCK), 1)
    spread = (key_lane % half) // rows * (CORES * rows) + key_lane % rows
    first = key_lane < half

    def row_bias(ref):
        limit = ref[2 * lon : 2 * lon + LIMIT_ROWS, :].astype(jnp.float32)[:1].astype(jnp.int32)

        parts = []
        for parity in (core, 1 - core):
            place = spread + parity * rows
            for block in range(0, nblocks, CORES):
                ends = [
                    jnp.broadcast_to(limit[:, b : b + 1], (1, OBS_BLOCK)) for b in (block, block + 1)
                ]
                end = jnp.where(first, ends[0], ends[1])
                parts.append(jnp.where(place < end, 0.0, -jnp.inf))
        return jnp.concatenate(parts, axis=1)

    biases = [row_bias(ref) for ref in row_refs]
    lane = lax.broadcasted_iota(jnp.int32, (obs, pair), 1)
    ones = [(lane // head == h).astype(jnp.bfloat16) for h in range(PAIR)]

    empty = jnp.zeros((head, obs), jnp.bfloat16)

    def columns(group):
        return slice(group * pair, (group + 1) * pair)

    def scores_of(group):
        keys = keys_of(columns(group))
        query = jnp.concatenate([ref[:lon, columns(group)] for ref in row_refs], axis=0)
        scores = []
        for h in range(PAIR):
            part = [keys[i * head : (i + 1) * head] if i == h else empty for i in range(PAIR)]
            part = jnp.concatenate(part, axis=0)
            scores.append(jnp.dot(query, part, preferred_element_type=jnp.float32))
        return scores

    def weights_of(scores):
        pieces = []
        for t, bias in enumerate(biases):
            piece = scores[t * lon : (t + 1) * lon] * scale + bias
            top = jnp.max(piece, axis=1, keepdims=True)
            pieces.append(jnp.exp2(piece - top).astype(jnp.bfloat16))
        return jnp.concatenate(pieces, axis=0)

    groups = HEADS // PAIR
    scores = [scores_of(group) for group in range(groups)]
    weights = [
        jnp.concatenate([weights_of(part) for part in scores[group]], axis=1) for group in range(groups)
    ]
    for group in range(groups):
        values = both_cores(same_ref, other_ref, 1, columns(group))
        value_parts = jnp.concatenate(
            [jnp.concatenate([values * one, one], axis=1) for one in ones], axis=0
        )
        both = jnp.dot(weights[group], value_parts, preferred_element_type=jnp.float32)
        mixed_ref[:, columns(group)] = (both[:, :pair] / both[:, pair:]).astype(jnp.bfloat16)

    depth = width // len(weight_refs)
    projected = sum(
        jnp.dot(
            mixed_ref[:, i * depth : (i + 1) * depth], ref[...], preferred_element_type=jnp.float32
        )
        for i, ref in enumerate(weight_refs)
    )
    grid = jnp.concatenate([ref[lon : 2 * lon, :] for ref in row_refs], axis=0)
    wide = (grid.astype(jnp.float32) + projected).astype(jnp.bfloat16).astype(jnp.float32)
    normed = wide * lax.rsqrt(jnp.mean(wide * wide, axis=-1, keepdims=True) + 1e-06)
    return wide, normed


def around(parts, lon):
    return pltpu.roll(parts[0], 1, 0) + parts[1] + pltpu.roll(parts[2], lon - 1, 0)


def inner_kernel(
    lon, width, nblocks, rows,
    meta_ref, near_ref, near_sent_ref, far_sent_ref, same_ref, other_ref, upper_ref, lower_ref,
    conv_ref, edge_ref, partial_ref, keys_ref, mixed_ref, field_ref,
):
    core = meta_ref[0]

    def keys_of(cols):
        keys = both_cores(same_ref, other_ref, 0, cols).T
        keys_ref[cols, :] = keys
        return keys

    wide, normed = attend(
        lon, width, nblocks, rows, core, (near_ref, near_sent_ref, far_sent_ref), keys_of,
        same_ref, other_ref, (upper_ref, lower_ref), mixed_ref,
    )
    field_ref[...] = normed.astype(jnp.bfloat16)
    edge_ref[...] = field_ref[2 * lon :, :]
    inputs = jnp.concatenate([field_ref[lon:, :], field_ref[: 2 * lon, :]], axis=1)
    terms = []
    for lon_off in range(3):
        taps = jnp.concatenate([conv_ref[1, lon_off], conv_ref[0, lon_off]], axis=0)
        terms.append(jnp.dot(inputs, taps, preferred_element_type=jnp.float32))
    for start in (0, lon):
        here = slice(start, start + lon)
        shifted = around([term[here] for term in terms], lon)
        partial_ref[here, :] = wide[start + lon : start + 2 * lon] + shifted


def outer_kernel(
    lon, width, nblocks, rows,
    meta_ref, far_ref, same_ref, other_ref, upper_ref, lower_ref, edge_ref, partial_ref, keys_ref,
    conv_ref, out_ref, mixed_ref,
):
    core = meta_ref[0]
    _, normed = attend(
        lon, width, nblocks, rows, core, (far_ref,), lambda cols: keys_ref[cols, :],
        same_ref, other_ref, (upper_ref, lower_ref), mixed_ref,
    )
    far = jnp.where(meta_ref[1] > 0, normed, 0.0).astype(jnp.bfloat16)
    field = jnp.concatenate([edge_ref[...], far], axis=0)
    terms = [
        jnp.dot(field, conv_ref[2, lon_off], preferred_element_type=jnp.float32)
        for lon_off in range(3)
    ]
    for start, tile in ((0, 1 - core), (lon, core)):
        here = slice(start, start + lon)
        total = partial_ref[here, :] + around([term[here] for term in terms], lon)
        out_ref[pl.ds(pl.multiple_of(tile * lon, lon), lon), :] = total.astype(jnp.bfloat16)


def pack_kernel(lon, *refs):
    queries_refs, grid_refs, limit_refs = refs[:2], refs[2:4], refs[4:6]
    near_ref, far_ref = refs[6:]
    even = lax.axis_index("tile") % CORES == 0
    for place, pair_refs in (
        (slice(0, lon), queries_refs),
        (slice(lon, 2 * lon), grid_refs),
        (slice(2 * lon, 2 * lon + LIMIT_ROWS), limit_refs),
    ):
        first, last = pair_refs[0][...], pair_refs[1][...]
        far_ref[place, :] = jnp.where(even, first, last)
        near_ref[place, :] = jnp.where(even, last, first)


def fetch_kernel(conv_hbm, conv_ref, sems):
    core = lax.axis_index("tile") % CORES
    copies = [
        pltpu.make_async_copy(conv_hbm.at[source], conv_ref.at[i], sems.at[i])
        for i, source in enumerate((2 - 2 * core, 1, 2 * core))
    ]
    for copy in copies:
        copy.start()
    for copy in copies:
        copy.wait()


def on_device(
    grid_feat, queries, obs_keys, obs_values, block_mask, obs_valid, out_weight, conv_weight
):
    q_dev, width = queries.shape
    tiles, nblocks = block_mask.shape
    rows = obs_keys.shape[0]
    lon = q_dev // tiles
    obs = nblocks * OBS_BLOCK
    devices = lax.axis_size(AXES)
    pairs = devices // CORES
    me = lax.axis_index(AXES)
    core = me % CORES

    block = jnp.stack([obs_keys, obs_values])
    groups = [list(range(c, devices, CORES)) for c in range(CORES)]
    same = lax.all_to_all(
        jnp.broadcast_to(block[None], (pairs,) + block.shape), AXES, 0, 0, axis_index_groups=groups
    )
    swap = [(i, i ^ 1) for i in range(devices)]
    across = [(i, i + 1) for i in range(1, devices - 1, CORES)]
    across += [(target, source) for source, target in across]

    query_rows, grid_rows = lax.optimization_barrier(
        (jnp.split(queries, tiles, axis=0), jnp.split(grid_feat, tiles, axis=0))
    )
    limits = jnp.where(block_mask > 0, obs_valid[None], 0).astype(jnp.bfloat16)
    limits = jnp.pad(limits, ((0, 0), (0, width - nblocks)))

    limit_rows = [
        jnp.broadcast_to(limits[tile][None], (LIMIT_ROWS, width)) for tile in range(tiles)
    ]
    vmem = pl.BlockSpec(memory_space=pltpu.VMEM)
    payload = jax.ShapeDtypeStruct((2 * lon + LIMIT_ROWS, width), jnp.bfloat16)
    near_sent, far_sent = pl.pallas_call(
        functools.partial(pack_kernel, lon),
        out_shape=[payload] * 2,
        in_specs=[vmem] * 6,
        out_specs=[vmem] * 2,
        compiler_params=pltpu.CompilerParams(vmem_limit_bytes=4 * 2**20),
        cost_estimate=pl.CostEstimate(flops=10**10, bytes_accessed=8 * payload.size, transcendentals=0),
        name="pack",
    )(*query_rows, *grid_rows, *limit_rows)
    far = lax.ppermute(far_sent, AXES, across)
    near = lax.ppermute(near_sent, AXES, swap)
    conv_weight, _ = lax.optimization_barrier((conv_weight, near_sent))
    taps = pl.pallas_call(
        fetch_kernel,
        out_shape=jax.ShapeDtypeStruct(conv_weight.shape, jnp.bfloat16),
        in_specs=[pl.BlockSpec(memory_space=pltpu.HBM)],
        out_specs=vmem,
        scratch_shapes=[pltpu.SemaphoreType.DMA((3,))],
        compiler_params=pltpu.CompilerParams(vmem_limit_bytes=4 * 2**20),
        cost_estimate=pl.CostEstimate(flops=0, bytes_accessed=4 * conv_weight.size, transcendentals=0),
        name="fetch",
    )(conv_weight)
    same, taps = lax.optimization_barrier((same, taps))
    other = lax.ppermute(same, AXES, swap)
    out_weight, _ = lax.optimization_barrier((out_weight, same))
    upper, lower = lax.optimization_barrier(tuple(jnp.split(out_weight, 2, axis=0)))

    far_exists = (me > 0) & (me < devices - 1)
    meta = jnp.stack([core, far_exists.astype(core.dtype)]).astype(jnp.int32)

    smem = pl.BlockSpec(memory_space=pltpu.SMEM)
    sizes = (lon, width, nblocks, rows)
    params = pltpu.CompilerParams(vmem_limit_bytes=40 * 2**20)
    tap_flops, row_flops = 2 * lon * width * width, 2 * lon * width * (width + 4 * obs)
    edge, partial, keys = pl.pallas_call(
        functools.partial(inner_kernel, *sizes),
        out_shape=[
            jax.ShapeDtypeStruct((lon, width), jnp.bfloat16),
            jax.ShapeDtypeStruct((q_dev, width), jnp.float32),
            jax.ShapeDtypeStruct((width, obs), jnp.bfloat16),
        ],
        in_specs=[smem] + [vmem] * 8,
        out_specs=[vmem] * 3,
        scratch_shapes=[
            pltpu.VMEM((3 * lon, width), jnp.bfloat16),
            pltpu.VMEM((3 * lon, width), jnp.bfloat16),
        ],
        compiler_params=params,
        cost_estimate=pl.CostEstimate(
            flops=3 * row_flops + 12 * tap_flops, bytes_accessed=2 * conv_weight.size, transcendentals=0
        ),
        name="inner",
    )(meta, near, near_sent, far_sent, same, other, upper, lower, taps)
    return pl.pallas_call(
        functools.partial(outer_kernel, *sizes),
        out_shape=jax.ShapeDtypeStruct((q_dev, width), jnp.bfloat16),
        in_specs=[smem] + [vmem] * 9,
        out_specs=vmem,
        scratch_shapes=[
            pltpu.VMEM((lon, width), jnp.bfloat16),
        ],
        compiler_params=params,
        cost_estimate=pl.CostEstimate(
            flops=row_flops + 6 * tap_flops, bytes_accessed=conv_weight.size, transcendentals=0
        ),
        name="outer",
    )(meta, far, same, other, upper, lower, edge, partial, keys, taps)


def solution(mesh):
    in_specs = (
        P(AXES, None),
        P(AXES, None),
        P(AXES, None),
        P(AXES, None),
        P(AXES, None),
        P(),
        P(),
        P(),
    )
    return jax.shard_map(
        on_device, mesh=mesh, in_specs=in_specs, out_specs=P(AXES, None), check_vma=False
    )
```

```python
import functools
import math

import jax
import jax.numpy as jnp
from jax import lax
from jax.experimental import pallas as pl
from jax.experimental.pallas import tpu as pltpu
from jax.sharding import PartitionSpec as P

HEADS = 8
OBS_BLOCK = 128
AXES = ("blk", "tile")
PAIR = 2
CORES = 2
LIMIT_ROWS = 16


def both_cores(same_ref, other_ref, kind, cols):
    return jnp.concatenate(
        [ref[:, kind, :, cols].reshape(-1, cols.stop - cols.start) for ref in (same_ref, other_ref)],
        axis=0,
    )


def attend(lon, width, nblocks, rows, core, row_refs, keys_of, same_ref, other_ref, weight_refs, mixed_ref):
    head = width // HEADS
    pair = PAIR * head
    obs = nblocks * OBS_BLOCK
    scale = head ** (-0.5) * math.log2(math.e)
    half = OBS_BLOCK // CORES
    key_lane = lax.broadcasted_iota(jnp.int32, (1, OBS_BLOCK), 1)
    spread = (key_lane % half) // rows * (CORES * rows) + key_lane % rows
    first = key_lane < half

    def row_bias(ref):
        limit = ref[2 * lon : 2 * lon + LIMIT_ROWS, :].astype(jnp.float32)[:1].astype(jnp.int32)

        parts = []
        for parity in (core, 1 - core):
            place = spread + parity * rows
            for block in range(0, nblocks, CORES):
                ends = [
                    jnp.broadcast_to(limit[:, b : b + 1], (1, OBS_BLOCK)) for b in (block, block + 1)
                ]
                end = jnp.where(first, ends[0], ends[1])
                parts.append(jnp.where(place < end, 0.0, -jnp.inf))
        return jnp.concatenate(parts, axis=1)

    biases = [row_bias(ref) for ref in row_refs]
    lane = lax.broadcasted_iota(jnp.int32, (obs, pair), 1)
    ones = [(lane // head == h).astype(jnp.bfloat16) for h in range(PAIR)]

    empty = jnp.zeros((head, obs), jnp.bfloat16)

    def columns(group):
        return slice(group * pair, (group + 1) * pair)

    def scores_of(group):
        keys = keys_of(columns(group))
        query = jnp.concatenate([ref[:lon, columns(group)] for ref in row_refs], axis=0)
        scores = []
        for h in range(PAIR):
            part = [keys[i * head : (i + 1) * head] if i == h else empty for i in range(PAIR)]
            part = jnp.concatenate(part, axis=0)
            scores.append(jnp.dot(query, part, preferred_element_type=jnp.float32))
        return scores

    def weights_of(scores):
        pieces = []
        for t, bias in enumerate(biases):
            piece = scores[t * lon : (t + 1) * lon] * scale + bias
            top = jnp.max(piece, axis=1, keepdims=True)
            pieces.append(jnp.exp2(piece - top).astype(jnp.bfloat16))
        return jnp.concatenate(pieces, axis=0)

    groups = HEADS // PAIR
    scores = [scores_of(group) for group in range(groups)]
    weights = [
        jnp.concatenate([weights_of(part) for part in scores[group]], axis=1) for group in range(groups)
    ]
    for group in range(groups):
        values = both_cores(same_ref, other_ref, 1, columns(group))
        value_parts = jnp.concatenate(
            [jnp.concatenate([values * one, one], axis=1) for one in ones], axis=0
        )
        both = jnp.dot(weights[group], value_parts, preferred_element_type=jnp.float32)
        mixed_ref[:, columns(group)] = (both[:, :pair] / both[:, pair:]).astype(jnp.bfloat16)

    depth = width // len(weight_refs)
    projected = sum(
        jnp.dot(
            mixed_ref[:, i * depth : (i + 1) * depth], ref[...], preferred_element_type=jnp.float32
        )
        for i, ref in enumerate(weight_refs)
    )
    grid = jnp.concatenate([ref[lon : 2 * lon, :] for ref in row_refs], axis=0)
    wide = (grid.astype(jnp.float32) + projected).astype(jnp.bfloat16).astype(jnp.float32)
    normed = wide * lax.rsqrt(jnp.mean(wide * wide, axis=-1, keepdims=True) + 1e-06)
    return wide, normed


def around(parts, lon):
    return pltpu.roll(parts[0], 1, 0) + parts[1] + pltpu.roll(parts[2], lon - 1, 0)


def inner_kernel(
    lon, width, nblocks, rows,
    meta_ref, near_ref, near_sent_ref, far_sent_ref, same_ref, other_ref, upper_ref, lower_ref,
    conv_ref, edge_ref, partial_ref, keys_ref, mixed_ref, field_ref,
):
    core = meta_ref[0]

    def keys_of(cols):
        keys = both_cores(same_ref, other_ref, 0, cols).T
        keys_ref[cols, :] = keys
        return keys

    wide, normed = attend(
        lon, width, nblocks, rows, core, (near_ref, near_sent_ref, far_sent_ref), keys_of,
        same_ref, other_ref, (upper_ref, lower_ref), mixed_ref,
    )
    field_ref[...] = normed.astype(jnp.bfloat16)
    edge_ref[...] = field_ref[2 * lon :, :]
    inputs = jnp.concatenate([field_ref[lon:, :], field_ref[: 2 * lon, :]], axis=1)
    terms = []
    for lon_off in range(3):
        taps = jnp.concatenate([conv_ref[1, lon_off], conv_ref[0, lon_off]], axis=0)
        terms.append(jnp.dot(inputs, taps, preferred_element_type=jnp.float32))
    for start in (0, lon):
        here = slice(start, start + lon)
        shifted = around([term[here] for term in terms], lon)
        partial_ref[here, :] = wide[start + lon : start + 2 * lon] + shifted


def outer_kernel(
    lon, width, nblocks, rows,
    meta_ref, far_ref, same_ref, other_ref, upper_ref, lower_ref, edge_ref, partial_ref, keys_ref,
    conv_ref, out_ref, mixed_ref,
):
    core = meta_ref[0]
    _, normed = attend(
        lon, width, nblocks, rows, core, (far_ref,), lambda cols: keys_ref[cols, :],
        same_ref, other_ref, (upper_ref, lower_ref), mixed_ref,
    )
    far = jnp.where(meta_ref[1] > 0, normed, 0.0).astype(jnp.bfloat16)
    field = jnp.concatenate([edge_ref[...], far], axis=0)
    terms = [
        jnp.dot(field, conv_ref[2, lon_off], preferred_element_type=jnp.float32)
        for lon_off in range(3)
    ]
    for start, tile in ((0, 1 - core), (lon, core)):
        here = slice(start, start + lon)
        total = partial_ref[here, :] + around([term[here] for term in terms], lon)
        out_ref[pl.ds(pl.multiple_of(tile * lon, lon), lon), :] = total.astype(jnp.bfloat16)


def pack_kernel(lon, *refs):
    queries_refs, grid_refs, limit_refs = refs[:2], refs[2:4], refs[4:6]
    near_ref, far_ref = refs[6:]
    even = lax.axis_index("tile") % CORES == 0
    for place, pair_refs in (
        (slice(0, lon), queries_refs),
        (slice(lon, 2 * lon), grid_refs),
        (slice(2 * lon, 2 * lon + LIMIT_ROWS), limit_refs),
    ):
        first, last = pair_refs[0][...], pair_refs[1][...]
        far_ref[place, :] = jnp.where(even, first, last)
        near_ref[place, :] = jnp.where(even, last, first)


def fetch_kernel(conv_hbm, conv_ref, sems):
    core = lax.axis_index("tile") % CORES
    copies = [
        pltpu.make_async_copy(conv_hbm.at[source], conv_ref.at[i], sems.at[i])
        for i, source in enumerate((2 - 2 * core, 1, 2 * core))
    ]
    for copy in copies:
        copy.start()
    for copy in copies:
        copy.wait()


def on_device(
    grid_feat, queries, obs_keys, obs_values, block_mask, obs_valid, out_weight, conv_weight
):
    q_dev, width = queries.shape
    tiles, nblocks = block_mask.shape
    rows = obs_keys.shape[0]
    lon = q_dev // tiles
    obs = nblocks * OBS_BLOCK
    devices = lax.axis_size(AXES)
    pairs = devices // CORES
    me = lax.axis_index(AXES)
    core = me % CORES

    block = jnp.stack([obs_keys, obs_values])
    groups = [list(range(c, devices, CORES)) for c in range(CORES)]
    same = lax.all_to_all(
        jnp.broadcast_to(block[None], (pairs,) + block.shape), AXES, 0, 0, axis_index_groups=groups
    )
    swap = [(i, i ^ 1) for i in range(devices)]
    across = [(i, i + 1) for i in range(1, devices - 1, CORES)]
    across += [(target, source) for source, target in across]

    query_rows, grid_rows = lax.optimization_barrier(
        (jnp.split(queries, tiles, axis=0), jnp.split(grid_feat, tiles, axis=0))
    )
    limits = jnp.where(block_mask > 0, obs_valid[None], 0).astype(jnp.bfloat16)
    limits = jnp.pad(limits, ((0, 0), (0, width - nblocks)))

    limit_rows = [
        jnp.broadcast_to(limits[tile][None], (LIMIT_ROWS, width)) for tile in range(tiles)
    ]
    vmem = pl.BlockSpec(memory_space=pltpu.VMEM)
    payload = jax.ShapeDtypeStruct((2 * lon + LIMIT_ROWS, width), jnp.bfloat16)
    near_sent, far_sent = pl.pallas_call(
        functools.partial(pack_kernel, lon),
        out_shape=[payload] * 2,
        in_specs=[vmem] * 6,
        out_specs=[vmem] * 2,
        compiler_params=pltpu.CompilerParams(vmem_limit_bytes=4 * 2**20),
        cost_estimate=pl.CostEstimate(flops=10**10, bytes_accessed=8 * payload.size, transcendentals=0),
        name="pack",
    )(*query_rows, *grid_rows, *limit_rows)
    far = lax.ppermute(far_sent, AXES, across)
    near = lax.ppermute(near_sent, AXES, swap)
    conv_weight, _ = lax.optimization_barrier((conv_weight, near_sent))
    taps = pl.pallas_call(
        fetch_kernel,
        out_shape=jax.ShapeDtypeStruct(conv_weight.shape, jnp.bfloat16),
        in_specs=[pl.BlockSpec(memory_space=pltpu.HBM)],
        out_specs=vmem,
        scratch_shapes=[pltpu.SemaphoreType.DMA((3,))],
        compiler_params=pltpu.CompilerParams(vmem_limit_bytes=4 * 2**20),
        cost_estimate=pl.CostEstimate(flops=0, bytes_accessed=4 * conv_weight.size, transcendentals=0),
        name="fetch",
    )(conv_weight)
    same, taps = lax.optimization_barrier((same, taps))
    other = lax.ppermute(same, AXES, swap)
    out_weight, _ = lax.optimization_barrier((out_weight, same))
    upper, lower = lax.optimization_barrier(tuple(jnp.split(out_weight, 2, axis=0)))

    far_exists = (me > 0) & (me < devices - 1)
    meta = jnp.stack([core, far_exists.astype(core.dtype)]).astype(jnp.int32)

    smem = pl.BlockSpec(memory_space=pltpu.SMEM)
    sizes = (lon, width, nblocks, rows)
    params = pltpu.CompilerParams(vmem_limit_bytes=(16 + 2 * nblocks) * 2**20)
    tap_flops, row_flops = 2 * lon * width * width, 2 * lon * width * (width + 4 * obs)
    edge, partial, keys = pl.pallas_call(
        functools.partial(inner_kernel, *sizes),
        out_shape=[
            jax.ShapeDtypeStruct((lon, width), jnp.bfloat16),
            jax.ShapeDtypeStruct((q_dev, width), jnp.float32),
            jax.ShapeDtypeStruct((width, obs), jnp.bfloat16),
        ],
        in_specs=[smem] + [vmem] * 8,
        out_specs=[vmem] * 3,
        scratch_shapes=[
            pltpu.VMEM((3 * lon, width), jnp.bfloat16),
            pltpu.VMEM((3 * lon, width), jnp.bfloat16),
        ],
        compiler_params=params,
        cost_estimate=pl.CostEstimate(
            flops=3 * row_flops + 12 * tap_flops, bytes_accessed=2 * conv_weight.size, transcendentals=0
        ),
        name="inner",
    )(meta, near, near_sent, far_sent, same, other, upper, lower, taps)
    return pl.pallas_call(
        functools.partial(outer_kernel, *sizes),
        out_shape=jax.ShapeDtypeStruct((q_dev, width), jnp.bfloat16),
        in_specs=[smem] + [vmem] * 9,
        out_specs=vmem,
        scratch_shapes=[
            pltpu.VMEM((lon, width), jnp.bfloat16),
        ],
        compiler_params=params,
        cost_estimate=pl.CostEstimate(
            flops=row_flops + 6 * tap_flops, bytes_accessed=conv_weight.size, transcendentals=0
        ),
        name="outer",
    )(meta, far, same, other, upper, lower, edge, partial, keys, taps)


def solution(mesh):
    in_specs = (
        P(AXES, None),
        P(AXES, None),
        P(AXES, None),
        P(AXES, None),
        P(AXES, None),
        P(),
        P(),
        P(),
    )
    return jax.shard_map(
        on_device, mesh=mesh, in_specs=in_specs, out_specs=P(AXES, None), check_vma=False
    )
```

```python
import functools
import math

import jax
import jax.numpy as jnp
from jax import lax
from jax.experimental import pallas as pl
from jax.experimental.pallas import tpu as pltpu
from jax.sharding import PartitionSpec as P

HEADS = 8
OBS_BLOCK = 128
AXES = ("blk", "tile")
PAIR = 2
CORES = 2
LIMIT_ROWS = 16


def both_cores(same_ref, other_ref, kind, cols):
    return jnp.concatenate(
        [ref[:, kind, :, cols].reshape(-1, cols.stop - cols.start) for ref in (same_ref, other_ref)],
        axis=0,
    )


def attend(lon, width, nblocks, rows, core, row_refs, keys_of, same_ref, other_ref, weight_refs, mixed_ref):
    head = width // HEADS
    pair = PAIR * head
    obs = nblocks * OBS_BLOCK
    scale = head ** (-0.5) * math.log2(math.e)
    half = OBS_BLOCK // CORES
    key_lane = lax.broadcasted_iota(jnp.int32, (1, OBS_BLOCK), 1)
    spread = (key_lane % half) // rows * (CORES * rows) + key_lane % rows
    first = key_lane < half

    def row_bias(ref):
        limit = ref[2 * lon : 2 * lon + LIMIT_ROWS, :].astype(jnp.float32)[:1].astype(jnp.int32)

        parts = []
        for parity in (core, 1 - core):
            place = spread + parity * rows
            for block in range(0, nblocks, CORES):
                ends = [
                    jnp.broadcast_to(limit[:, b : b + 1], (1, OBS_BLOCK)) for b in (block, block + 1)
                ]
                end = jnp.where(first, ends[0], ends[1])
                parts.append(jnp.where(place < end, 0.0, -jnp.inf))
        return jnp.concatenate(parts, axis=1)

    biases = [row_bias(ref) for ref in row_refs]
    lane = lax.broadcasted_iota(jnp.int32, (obs, pair), 1)
    ones = [(lane // head == h).astype(jnp.bfloat16) for h in range(PAIR)]

    empty = jnp.zeros((head, obs), jnp.bfloat16)

    def columns(group):
        return slice(group * pair, (group + 1) * pair)

    def scores_of(group):
        keys = keys_of(columns(group))
        query = jnp.concatenate([ref[:lon, columns(group)] for ref in row_refs], axis=0)
        scores = []
        for h in range(PAIR):
            part = [keys[i * head : (i + 1) * head] if i == h else empty for i in range(PAIR)]
            part = jnp.concatenate(part, axis=0)
            scores.append(jnp.dot(query, part, preferred_element_type=jnp.float32))
        return scores

    def weights_of(scores):
        pieces = []
        for t, bias in enumerate(biases):
            piece = scores[t * lon : (t + 1) * lon] * scale + bias
            top = jnp.max(piece, axis=1, keepdims=True)
            pieces.append(jnp.exp2(piece - top).astype(jnp.bfloat16))
        return jnp.concatenate(pieces, axis=0)

    groups = HEADS // PAIR
    scores = [scores_of(group) for group in range(groups)]
    weights = [
        jnp.concatenate([weights_of(part) for part in scores[group]], axis=1) for group in range(groups)
    ]
    for group in range(groups):
        values = both_cores(same_ref, other_ref, 1, columns(group))
        value_parts = jnp.concatenate(
            [jnp.concatenate([values * one, one], axis=1) for one in ones], axis=0
        )
        both = jnp.dot(weights[group], value_parts, preferred_element_type=jnp.float32)
        mixed_ref[:, columns(group)] = (both[:, :pair] / both[:, pair:]).astype(jnp.bfloat16)

    depth = width // len(weight_refs)
    projected = sum(
        jnp.dot(
            mixed_ref[:, i * depth : (i + 1) * depth], ref[...], preferred_element_type=jnp.float32
        )
        for i, ref in enumerate(weight_refs)
    )
    grid = jnp.concatenate([ref[lon : 2 * lon, :] for ref in row_refs], axis=0)
    wide = (grid.astype(jnp.float32) + projected).astype(jnp.bfloat16).astype(jnp.float32)
    normed = wide * lax.rsqrt(jnp.mean(wide * wide, axis=-1, keepdims=True) + 1e-06)
    return wide, normed


def around(parts, lon):
    return pltpu.roll(parts[0], 1, 0) + parts[1] + pltpu.roll(parts[2], lon - 1, 0)


def inner_kernel(
    lon, width, nblocks, rows,
    meta_ref, near_ref, near_sent_ref, far_sent_ref, same_ref, other_ref, upper_ref, lower_ref,
    conv_hbm, edge_ref, partial_ref, keys_ref, last_ref, conv_ref, mixed_ref, field_ref, sems,
):
    core = meta_ref[0]
    copies = [
        pltpu.make_async_copy(conv_hbm.at[source], conv_ref.at[i], sems.at[i])
        for i, source in enumerate((1, 2 - 2 * core))
    ]
    copies.append(pltpu.make_async_copy(conv_hbm.at[2 * core], last_ref, sems.at[2]))
    for copy in copies:
        copy.start()

    def keys_of(cols):
        keys = both_cores(same_ref, other_ref, 0, cols).T
        keys_ref[cols, :] = keys
        return keys

    wide, normed = attend(
        lon, width, nblocks, rows, core, (near_ref, near_sent_ref, far_sent_ref), keys_of,
        same_ref, other_ref, (upper_ref, lower_ref), mixed_ref,
    )
    field_ref[...] = normed.astype(jnp.bfloat16)
    edge_ref[...] = field_ref[2 * lon :, :]
    inputs = jnp.concatenate([field_ref[lon:, :], field_ref[: 2 * lon, :]], axis=1)
    terms = []
    copies[0].wait()
    copies[1].wait()
    for lon_off in range(3):
        taps = conv_ref[:, lon_off].reshape(2 * width, width)
        terms.append(jnp.dot(inputs, taps, preferred_element_type=jnp.float32))
    for start in (0, lon):
        here = slice(start, start + lon)
        shifted = around([term[here] for term in terms], lon)
        partial_ref[here, :] = wide[start + lon : start + 2 * lon] + shifted
    copies[2].wait()


def outer_kernel(
    lon, width, nblocks, rows,
    meta_ref, far_ref, same_ref, other_ref, upper_ref, lower_ref, edge_ref, partial_ref, keys_ref,
    conv_ref, out_ref, mixed_ref,
):
    core = meta_ref[0]
    _, normed = attend(
        lon, width, nblocks, rows, core, (far_ref,), lambda cols: keys_ref[cols, :],
        same_ref, other_ref, (upper_ref, lower_ref), mixed_ref,
    )
    far = jnp.where(meta_ref[1] > 0, normed, 0.0).astype(jnp.bfloat16)
    field = jnp.concatenate([edge_ref[...], far], axis=0)
    terms = [
        jnp.dot(field, conv_ref[lon_off], preferred_element_type=jnp.float32) for lon_off in range(3)
    ]
    for start, tile in ((0, 1 - core), (lon, core)):
        here = slice(start, start + lon)
        total = partial_ref[here, :] + around([term[here] for term in terms], lon)
        out_ref[pl.ds(pl.multiple_of(tile * lon, lon), lon), :] = total.astype(jnp.bfloat16)


def pack_kernel(lon, *refs):
    queries_refs, grid_refs, limit_refs = refs[:2], refs[2:4], refs[4:6]
    near_ref, far_ref = refs[6:]
    even = lax.axis_index("tile") % CORES == 0
    for place, pair_refs in (
        (slice(0, lon), queries_refs),
        (slice(lon, 2 * lon), grid_refs),
        (slice(2 * lon, 2 * lon + LIMIT_ROWS), limit_refs),
    ):
        first, last = pair_refs[0][...], pair_refs[1][...]
        far_ref[place, :] = jnp.where(even, first, last)
        near_ref[place, :] = jnp.where(even, last, first)


def on_device(
    grid_feat, queries, obs_keys, obs_values, block_mask, obs_valid, out_weight, conv_weight
):
    q_dev, width = queries.shape
    tiles, nblocks = block_mask.shape
    rows = obs_keys.shape[0]
    lon = q_dev // tiles
    obs = nblocks * OBS_BLOCK
    devices = lax.axis_size(AXES)
    pairs = devices // CORES
    me = lax.axis_index(AXES)
    core = me % CORES

    block = jnp.stack([obs_keys, obs_values])
    groups = [list(range(c, devices, CORES)) for c in range(CORES)]
    same = lax.all_to_all(
        jnp.broadcast_to(block[None], (pairs,) + block.shape), AXES, 0, 0, axis_index_groups=groups
    )
    swap = [(i, i ^ 1) for i in range(devices)]
    across = [(i, i + 1) for i in range(1, devices - 1, CORES)]
    across += [(target, source) for source, target in across]

    query_rows, grid_rows = lax.optimization_barrier(
        (jnp.split(queries, tiles, axis=0), jnp.split(grid_feat, tiles, axis=0))
    )
    limits = jnp.where(block_mask > 0, obs_valid[None], 0).astype(jnp.bfloat16)
    limits = jnp.pad(limits, ((0, 0), (0, width - nblocks)))

    limit_rows = [
        jnp.broadcast_to(limits[tile][None], (LIMIT_ROWS, width)) for tile in range(tiles)
    ]
    vmem = pl.BlockSpec(memory_space=pltpu.VMEM)
    payload = jax.ShapeDtypeStruct((2 * lon + LIMIT_ROWS, width), jnp.bfloat16)
    near_sent, far_sent = pl.pallas_call(
        functools.partial(pack_kernel, lon),
        out_shape=[payload] * 2,
        in_specs=[vmem] * 6,
        out_specs=[vmem] * 2,
        compiler_params=pltpu.CompilerParams(vmem_limit_bytes=4 * 2**20),
        cost_estimate=pl.CostEstimate(flops=10**10, bytes_accessed=8 * payload.size, transcendentals=0),
        name="pack",
    )(*query_rows, *grid_rows, *limit_rows)
    far = lax.ppermute(far_sent, AXES, across)
    near = lax.ppermute(near_sent, AXES, swap)
    other = lax.ppermute(same, AXES, swap)
    out_weight, _ = lax.optimization_barrier((out_weight, same))
    upper, lower = lax.optimization_barrier(tuple(jnp.split(out_weight, 2, axis=0)))

    far_exists = (me > 0) & (me < devices - 1)
    meta = jnp.stack([core, far_exists.astype(core.dtype)]).astype(jnp.int32)

    smem = pl.BlockSpec(memory_space=pltpu.SMEM)
    hbm = pl.BlockSpec(memory_space=pltpu.HBM)
    sizes = (lon, width, nblocks, rows)
    params = pltpu.CompilerParams(vmem_limit_bytes=48 * 2**20)
    tap_flops, row_flops = 2 * lon * width * width, 2 * lon * width * (width + 4 * obs)
    edge, partial, keys, taps = pl.pallas_call(
        functools.partial(inner_kernel, *sizes),
        out_shape=[
            jax.ShapeDtypeStruct((lon, width), jnp.bfloat16),
            jax.ShapeDtypeStruct((q_dev, width), jnp.float32),
            jax.ShapeDtypeStruct((width, obs), jnp.bfloat16),
            jax.ShapeDtypeStruct(conv_weight.shape[1:], jnp.bfloat16),
        ],
        in_specs=[smem] + [vmem] * 7 + [hbm],
        out_specs=[vmem] * 4,
        scratch_shapes=[
            pltpu.VMEM((2,) + conv_weight.shape[1:], jnp.bfloat16),
            pltpu.VMEM((3 * lon, width), jnp.bfloat16),
            pltpu.VMEM((3 * lon, width), jnp.bfloat16),
            pltpu.SemaphoreType.DMA((3,)),
        ],
        compiler_params=params,
        cost_estimate=pl.CostEstimate(
            flops=3 * row_flops + 12 * tap_flops, bytes_accessed=2 * conv_weight.size, transcendentals=0
        ),
        name="inner",
    )(meta, near, near_sent, far_sent, same, other, upper, lower, conv_weight)
    return pl.pallas_call(
        functools.partial(outer_kernel, *sizes),
        out_shape=jax.ShapeDtypeStruct((q_dev, width), jnp.bfloat16),
        in_specs=[smem] + [vmem] * 9,
        out_specs=vmem,
        scratch_shapes=[
            pltpu.VMEM((lon, width), jnp.bfloat16),
        ],
        compiler_params=params,
        cost_estimate=pl.CostEstimate(
            flops=row_flops + 6 * tap_flops, bytes_accessed=conv_weight.size, transcendentals=0
        ),
        name="outer",
    )(meta, far, same, other, upper, lower, edge, partial, keys, taps)


def solution(mesh):
    in_specs = (
        P(AXES, None),
        P(AXES, None),
        P(AXES, None),
        P(AXES, None),
        P(AXES, None),
        P(),
        P(),
        P(),
    )
    return jax.shard_map(
        on_device, mesh=mesh, in_specs=in_specs, out_specs=P(AXES, None), check_vma=False
    )
```

```python
import functools
import math

import jax
import jax.numpy as jnp
from jax import lax
from jax.experimental import pallas as pl
from jax.experimental.pallas import tpu as pltpu
from jax.sharding import PartitionSpec as P

HEADS = 8
OBS_BLOCK = 128
AXES = ("blk", "tile")
PAIR = 2
CORES = 2
LIMIT_ROWS = 16


def both_cores(same_ref, other_ref, kind, cols):
    return jnp.concatenate(
        [ref[:, kind, :, cols].reshape(-1, cols.stop - cols.start) for ref in (same_ref, other_ref)],
        axis=0,
    )


def attend(lon, width, nblocks, rows, core, row_refs, keys_of, same_ref, other_ref, weight_refs, mixed_ref):
    head = width // HEADS
    pair = PAIR * head
    obs = nblocks * OBS_BLOCK
    scale = head ** (-0.5) * math.log2(math.e)
    half = OBS_BLOCK // CORES
    key_lane = lax.broadcasted_iota(jnp.int32, (1, OBS_BLOCK), 1)
    spread = (key_lane % half) // rows * (CORES * rows) + key_lane % rows
    first = key_lane < half

    def row_bias(ref):
        limit = ref[2 * lon : 2 * lon + LIMIT_ROWS, :].astype(jnp.float32)[:1].astype(jnp.int32)

        parts = []
        for parity in (core, 1 - core):
            place = spread + parity * rows
            for block in range(0, nblocks, CORES):
                ends = [
                    jnp.broadcast_to(limit[:, b : b + 1], (1, OBS_BLOCK)) for b in (block, block + 1)
                ]
                end = jnp.where(first, ends[0], ends[1])
                parts.append(jnp.where(place < end, 0.0, -jnp.inf))
        return jnp.concatenate(parts, axis=1)

    biases = [row_bias(ref) for ref in row_refs]
    lane = lax.broadcasted_iota(jnp.int32, (obs, pair), 1)
    ones = [(lane // head == h).astype(jnp.bfloat16) for h in range(PAIR)]

    empty = jnp.zeros((head, obs), jnp.bfloat16)

    def columns(group):
        return slice(group * pair, (group + 1) * pair)

    def scores_of(group):
        keys = keys_of(columns(group))
        query = jnp.concatenate([ref[:lon, columns(group)] for ref in row_refs], axis=0)
        scores = []
        for h in range(PAIR):
            part = [keys[i * head : (i + 1) * head] if i == h else empty for i in range(PAIR)]
            part = jnp.concatenate(part, axis=0)
            scores.append(jnp.dot(query, part, preferred_element_type=jnp.float32))
        return scores

    def weights_of(scores):
        pieces = []
        for t, bias in enumerate(biases):
            piece = scores[t * lon : (t + 1) * lon] * scale + bias
            top = jnp.max(piece, axis=1, keepdims=True)
            pieces.append(jnp.exp2(piece - top).astype(jnp.bfloat16))
        return jnp.concatenate(pieces, axis=0)

    groups = HEADS // PAIR
    scores = [scores_of(group) for group in range(groups)]
    weights = [
        jnp.concatenate([weights_of(part) for part in scores[group]], axis=1) for group in range(groups)
    ]
    for group in range(groups):
        values = both_cores(same_ref, other_ref, 1, columns(group))
        value_parts = jnp.concatenate(
            [jnp.concatenate([values * one, one], axis=1) for one in ones], axis=0
        )
        both = jnp.dot(weights[group], value_parts, preferred_element_type=jnp.float32)
        mixed_ref[:, columns(group)] = (both[:, :pair] / both[:, pair:]).astype(jnp.bfloat16)

    depth = width // len(weight_refs)
    projected = sum(
        jnp.dot(
            mixed_ref[:, i * depth : (i + 1) * depth], ref[...], preferred_element_type=jnp.float32
        )
        for i, ref in enumerate(weight_refs)
    )
    grid = jnp.concatenate([ref[lon : 2 * lon, :] for ref in row_refs], axis=0)
    wide = (grid.astype(jnp.float32) + projected).astype(jnp.bfloat16).astype(jnp.float32)
    normed = wide * lax.rsqrt(jnp.mean(wide * wide, axis=-1, keepdims=True) + 1e-06)
    return wide, normed


def around(parts, lon):
    return pltpu.roll(parts[0], 1, 0) + parts[1] + pltpu.roll(parts[2], lon - 1, 0)


def inner_kernel(
    lon, width, nblocks, rows,
    meta_ref, near_ref, near_sent_ref, far_sent_ref, same_ref, other_ref, upper_ref, lower_ref,
    conv_hbm, edge_ref, partial_ref, keys_ref, last_ref, conv_ref, mixed_ref, field_ref, sems,
):
    core = meta_ref[0]
    copies = [
        pltpu.make_async_copy(
            conv_hbm.at[source, lon_off], conv_ref.at[i, lon_off], sems.at[2 * lon_off + i]
        )
        for lon_off in range(3)
        for i, source in enumerate((1, 2 - 2 * core))
    ]
    copies.append(pltpu.make_async_copy(conv_hbm.at[2 * core], last_ref, sems.at[6]))
    for copy in copies:
        copy.start()

    def keys_of(cols):
        keys = both_cores(same_ref, other_ref, 0, cols).T
        keys_ref[cols, :] = keys
        return keys

    wide, normed = attend(
        lon, width, nblocks, rows, core, (near_ref, near_sent_ref, far_sent_ref), keys_of,
        same_ref, other_ref, (upper_ref, lower_ref), mixed_ref,
    )
    field_ref[...] = normed.astype(jnp.bfloat16)
    edge_ref[...] = field_ref[2 * lon :, :]
    inputs = jnp.concatenate([field_ref[lon:, :], field_ref[: 2 * lon, :]], axis=1)
    terms = []
    for lon_off in range(3):
        for copy in copies[2 * lon_off : 2 * lon_off + 2]:
            copy.wait()
        taps = conv_ref[:, lon_off].reshape(2 * width, width)
        terms.append(jnp.dot(inputs, taps, preferred_element_type=jnp.float32))
    for start in (0, lon):
        here = slice(start, start + lon)
        shifted = around([term[here] for term in terms], lon)
        partial_ref[here, :] = wide[start + lon : start + 2 * lon] + shifted
    copies[6].wait()


def outer_kernel(
    lon, width, nblocks, rows,
    meta_ref, far_ref, same_ref, other_ref, upper_ref, lower_ref, edge_ref, partial_ref, keys_ref,
    conv_ref, out_ref, mixed_ref,
):
    core = meta_ref[0]
    _, normed = attend(
        lon, width, nblocks, rows, core, (far_ref,), lambda cols: keys_ref[cols, :],
        same_ref, other_ref, (upper_ref, lower_ref), mixed_ref,
    )
    far = jnp.where(meta_ref[1] > 0, normed, 0.0).astype(jnp.bfloat16)
    field = jnp.concatenate([edge_ref[...], far], axis=0)
    terms = [
        jnp.dot(field, conv_ref[lon_off], preferred_element_type=jnp.float32) for lon_off in range(3)
    ]
    for start, tile in ((0, 1 - core), (lon, core)):
        here = slice(start, start + lon)
        total = partial_ref[here, :] + around([term[here] for term in terms], lon)
        out_ref[pl.ds(pl.multiple_of(tile * lon, lon), lon), :] = total.astype(jnp.bfloat16)


def pack_kernel(lon, *refs):
    queries_refs, grid_refs, limit_refs = refs[:2], refs[2:4], refs[4:6]
    near_ref, far_ref = refs[6:]
    even = lax.axis_index("tile") % CORES == 0
    for place, pair_refs in (
        (slice(0, lon), queries_refs),
        (slice(lon, 2 * lon), grid_refs),
        (slice(2 * lon, 2 * lon + LIMIT_ROWS), limit_refs),
    ):
        first, last = pair_refs[0][...], pair_refs[1][...]
        far_ref[place, :] = jnp.where(even, first, last)
        near_ref[place, :] = jnp.where(even, last, first)


def on_device(
    grid_feat, queries, obs_keys, obs_values, block_mask, obs_valid, out_weight, conv_weight
):
    q_dev, width = queries.shape
    tiles, nblocks = block_mask.shape
    rows = obs_keys.shape[0]
    lon = q_dev // tiles
    obs = nblocks * OBS_BLOCK
    devices = lax.axis_size(AXES)
    pairs = devices // CORES
    me = lax.axis_index(AXES)
    core = me % CORES

    block = jnp.stack([obs_keys, obs_values])
    groups = [list(range(c, devices, CORES)) for c in range(CORES)]
    same = lax.all_to_all(
        jnp.broadcast_to(block[None], (pairs,) + block.shape), AXES, 0, 0, axis_index_groups=groups
    )
    swap = [(i, i ^ 1) for i in range(devices)]
    across = [(i, i + 1) for i in range(1, devices - 1, CORES)]
    across += [(target, source) for source, target in across]

    query_rows, grid_rows = lax.optimization_barrier(
        (jnp.split(queries, tiles, axis=0), jnp.split(grid_feat, tiles, axis=0))
    )
    limits = jnp.where(block_mask > 0, obs_valid[None], 0).astype(jnp.bfloat16)
    limits = jnp.pad(limits, ((0, 0), (0, width - nblocks)))

    limit_rows = [
        jnp.broadcast_to(limits[tile][None], (LIMIT_ROWS, width)) for tile in range(tiles)
    ]
    vmem = pl.BlockSpec(memory_space=pltpu.VMEM)
    payload = jax.ShapeDtypeStruct((2 * lon + LIMIT_ROWS, width), jnp.bfloat16)
    near_sent, far_sent = pl.pallas_call(
        functools.partial(pack_kernel, lon),
        out_shape=[payload] * 2,
        in_specs=[vmem] * 6,
        out_specs=[vmem] * 2,
        compiler_params=pltpu.CompilerParams(vmem_limit_bytes=4 * 2**20),
        cost_estimate=pl.CostEstimate(flops=10**10, bytes_accessed=8 * payload.size, transcendentals=0),
        name="pack",
    )(*query_rows, *grid_rows, *limit_rows)
    far = lax.ppermute(far_sent, AXES, across)
    near = lax.ppermute(near_sent, AXES, swap)
    other = lax.ppermute(same, AXES, swap)
    out_weight, _ = lax.optimization_barrier((out_weight, same))
    upper, lower = lax.optimization_barrier(tuple(jnp.split(out_weight, 2, axis=0)))

    far_exists = (me > 0) & (me < devices - 1)
    meta = jnp.stack([core, far_exists.astype(core.dtype)]).astype(jnp.int32)

    smem = pl.BlockSpec(memory_space=pltpu.SMEM)
    hbm = pl.BlockSpec(memory_space=pltpu.HBM)
    sizes = (lon, width, nblocks, rows)
    params = pltpu.CompilerParams(vmem_limit_bytes=48 * 2**20)
    tap_flops, row_flops = 2 * lon * width * width, 2 * lon * width * (width + 4 * obs)
    edge, partial, keys, taps = pl.pallas_call(
        functools.partial(inner_kernel, *sizes),
        out_shape=[
            jax.ShapeDtypeStruct((lon, width), jnp.bfloat16),
            jax.ShapeDtypeStruct((q_dev, width), jnp.float32),
            jax.ShapeDtypeStruct((width, obs), jnp.bfloat16),
            jax.ShapeDtypeStruct(conv_weight.shape[1:], jnp.bfloat16),
        ],
        in_specs=[smem] + [vmem] * 7 + [hbm],
        out_specs=[vmem] * 4,
        scratch_shapes=[
            pltpu.VMEM((2,) + conv_weight.shape[1:], jnp.bfloat16),
            pltpu.VMEM((3 * lon, width), jnp.bfloat16),
            pltpu.VMEM((3 * lon, width), jnp.bfloat16),
            pltpu.SemaphoreType.DMA((7,)),
        ],
        compiler_params=params,
        cost_estimate=pl.CostEstimate(
            flops=3 * row_flops + 12 * tap_flops, bytes_accessed=2 * conv_weight.size, transcendentals=0
        ),
        name="inner",
    )(meta, near, near_sent, far_sent, same, other, upper, lower, conv_weight)
    return pl.pallas_call(
        functools.partial(outer_kernel, *sizes),
        out_shape=jax.ShapeDtypeStruct((q_dev, width), jnp.bfloat16),
        in_specs=[smem] + [vmem] * 9,
        out_specs=vmem,
        scratch_shapes=[
            pltpu.VMEM((lon, width), jnp.bfloat16),
        ],
        compiler_params=params,
        cost_estimate=pl.CostEstimate(
            flops=row_flops + 6 * tap_flops, bytes_accessed=conv_weight.size, transcendentals=0
        ),
        name="outer",
    )(meta, far, same, other, upper, lower, edge, partial, keys, taps)


def solution(mesh):
    in_specs = (
        P(AXES, None),
        P(AXES, None),
        P(AXES, None),
        P(AXES, None),
        P(AXES, None),
        P(),
        P(),
        P(),
    )
    return jax.shard_map(
        on_device, mesh=mesh, in_specs=in_specs, out_specs=P(AXES, None), check_vma=False
    )
```
